32 devices in a mesh: gx: 4 (over z), gy: 4 (over y, x), gz: 2 (over core).
Axes of the slice: x: 2, y: 2, z: 4, core: 2. Of those that a mesh axis runs over, the one named last changes fastest.
Arguments:
- populations0: bfloat16 [26, 16, 32, 512], P(None, 'gz', 'gx', 'gy'), may hold values from 0 to 1, as said below
- populations1: bfloat16 [26, 16, 32, 512], P(None, 'gz', 'gx', 'gy'), may hold values from 0 to 1, as said below
- cotangent: float32 [26, 16, 32, 512], P(None, 'gz', 'gx', 'gy'), may hold values from -6 to 6
Outputs:
- gradient: float32 [26, 16, 32, 512], P(None, 'gz', 'gx', 'gy')
The draws below stay inside these ranges and needn't reach their ends.
Inputs may be any that keep to these rules, and one draw needn't show every extreme that they name: `populations0`: every entry is positive; in every cell the 7 phase populations sum to between 0.1 and 1.3. `populations1`: every entry is positive; in every cell the 7 phase populations sum to between 0.1 and 1.3.
All inputs are finite; a program needn't handle non-finite values.
Results may differ from the reference program's by a relative error of at most 0.0003.
Values sent between devices are 32-bit elements; how exact they have to be, the bound alone decides.
A program may use at most 64 MiB of HBM per device.

```python
import jax
import jax.numpy as jnp
import numpy as np
from jax import lax

NZ = 16
NX = 32
NY = 512


VELOCITY = np.array([[0, 0, 0], [1, 0, 0], [-1, 0, 0], [0, 1, 0], [0, -1, 0], [0, 0, 1], [0, 0, -1], [1, 1, 0], [-1, -1, 0], [1, -1, 0], [-1, 1, 0], [1, 0, 1], [-1, 0, -1], [1, 0, -1], [-1, 0, 1], [0, 1, 1], [0, -1, -1], [0, 1, -1], [0, -1, 1]])


FLOW_WEIGHT = [1.0 / 3.0] + [1.0 / 18.0] * 6 + [1.0 / 36.0] * 12


PHASE_WEIGHT = [0.25] + [0.125] * 6


def expand_drawn(weights):
    values = [float(entry) for entry in list(weights)]
    return jnp.asarray(values, jnp.float32).reshape((-1, 1, 1, 1))


def draw_state(key):
    subkeys = jax.random.split(key, 6)
    extent = (NZ, NX, NY)
    fraction = jax.random.uniform(subkeys[0], extent, jnp.float32, 0.2, 0.8)
    velocity = jnp.clip(0.04 * jax.random.normal(subkeys[1], (3,) + extent, jnp.float32), -0.1, 0.1)
    pressure = jax.random.uniform(subkeys[2], extent, jnp.float32, 0.8, 1.2)
    density = 0.2 + 0.8 * fraction
    along_flow = expand_drawn(VELOCITY[:, 0]) * velocity[0] + expand_drawn(VELOCITY[:, 1]) * velocity[1] + expand_drawn(VELOCITY[:, 2]) * velocity[2]
    speed_square = velocity[0] * velocity[0] + velocity[1] * velocity[1] + velocity[2] * velocity[2]
    flow_noise = jax.random.uniform(subkeys[3], (19,) + extent, jnp.float32, 0.85, 1.15)
    phase_noise = jax.random.uniform(subkeys[4], (7,) + extent, jnp.float32, 0.85, 1.15)
    flow_part = expand_drawn(FLOW_WEIGHT) * (pressure + density * (3.0 * along_flow + 4.5 * along_flow * along_flow - 1.5 * speed_square)) * flow_noise
    phase_part = expand_drawn(PHASE_WEIGHT) * fraction * (1.0 + 4.0 * along_flow[:7]) * phase_noise
    return jnp.concatenate([flow_part, phase_part], 0).astype(jnp.bfloat16)


def draw_populations0(key, part):
    return draw_state(jax.random.fold_in(key, 11))


def draw_populations1(key, part):
    return draw_state(jax.random.fold_in(key, 12))


def levels(stream_key, dims, cuts, smallest, top_value):
    level = 1.0
    for dim, parts in cuts:
        heights = jax.random.uniform(jax.random.fold_in(jax.random.fold_in(stream_key, 6), dim), (parts,), jnp.float32, smallest / len(cuts), top_value / len(cuts))
        level = level * jnp.repeat(jnp.exp(heights), dims[dim] // parts).reshape((-1,) + (1,) * (len(dims) - 1 - dim))
    return level


def scatter_about(stream_key, shape, spread, limit, shards=(), held_as=jnp.bfloat16):
    result = spread * jax.random.normal(stream_key, shape, jnp.float32)
    if shards:
        result = result * levels(stream_key, shape, shards, -0.22, 0.18)
    return jnp.clip(result, -limit, limit).astype(held_as)


def setup_inputs(seed: int = 0) -> dict:
    streams_of = jax.random.split(jax.random.key(seed), 4)
    return {
        "populations0": draw_populations0(jax.random.fold_in(streams_of[3], 71), 0),
        "populations1": draw_populations1(jax.random.fold_in(streams_of[3], 71), 0),
        "cotangent": scatter_about(streams_of[2], (26, NZ, NX, NY), 1.0, 6.0, ((1, 2), (2, 4), (3, 4)), jnp.float32),
    }


VELOCITY = np.array([[0, 0, 0], [1, 0, 0], [-1, 0, 0], [0, 1, 0], [0, -1, 0], [0, 0, 1], [0, 0, -1], [1, 1, 0], [-1, -1, 0], [1, -1, 0], [-1, 1, 0], [1, 0, 1], [-1, 0, -1], [1, 0, -1], [-1, 0, 1], [0, 1, 1], [0, -1, -1], [0, 1, -1], [0, -1, 1]])
OPPOSITE = [0, 2, 1, 4, 3, 6, 5, 8, 7, 10, 9, 12, 11, 14, 13, 16, 15, 18, 17]
FLOW_WEIGHT = [1.0 / 3.0] + [1.0 / 18.0] * 6 + [1.0 / 36.0] * 12
PHASE_WEIGHT = [0.25] + [0.125] * 6
VELOCITY_ALL = np.concatenate([VELOCITY, VELOCITY[:7]], 0)
OPPOSITE_ALL = OPPOSITE + [19 + mirror for mirror in OPPOSITE[:7]]
WELL_DEPTH = 0.3
STIFFNESS = 0.6
SHARPEN = 0.3
PHASE_RATE = 1.4
UNITS = ((1, 0, 0), (0, 1, 0), (0, 0, 1))

def expand(weights, rank):
    values = [float(entry) for entry in list(weights)]
    return jnp.asarray(values, jnp.float32).reshape((-1,) + (1,) * rank)

def along(velocity_table, vector):
    rank = vector.ndim - 1
    total = expand(velocity_table[:, 0], rank) * vector[0]
    for direction in range(1, 3):
        total = total + expand(velocity_table[:, direction], rank) * vector[direction]
    return total

def collide(populations, phase_grad, potential_grad):
    rank = populations.ndim - 1
    flow_part = populations[:19]
    phase_part = populations[19:]
    fraction = lax.optimization_barrier(jnp.sum(phase_part, 0))
    density = 0.2 + 0.8 * fraction
    pressure = lax.optimization_barrier(jnp.sum(flow_part, 0))
    body_force = -fraction[None] * potential_grad
    momentum = jnp.stack([lax.optimization_barrier(jnp.sum(expand(VELOCITY[:, direction], rank) * flow_part, 0)) for direction in range(3)])
    velocity = (momentum + 0.5 * body_force) / density[None]
    along_flow = along(VELOCITY, velocity)
    speed_square = lax.optimization_barrier(jnp.sum(velocity * velocity, 0))
    relax_rate = 1.1 + 0.5 * fraction
    flow_equil = expand(FLOW_WEIGHT, rank) * (pressure + density * (3.0 * along_flow + 4.5 * along_flow * along_flow - 1.5 * speed_square))
    along_force = along(VELOCITY, body_force)
    speed_force = lax.optimization_barrier(jnp.sum(velocity * body_force, 0))
    source = expand(FLOW_WEIGHT, rank) * (3.0 * (along_force - speed_force) + 9.0 * along_flow * along_force)
    flow_post = flow_part - relax_rate * (flow_part - flow_equil) + (1.0 - 0.5 * relax_rate) * source
    magnitude = jnp.sqrt(lax.optimization_barrier(jnp.sum(phase_grad * phase_grad, 0)) + 0.0625)
    normal = phase_grad / magnitude
    along_normal = along(VELOCITY[:7], normal)
    phase_equil = expand(PHASE_WEIGHT, rank) * (fraction * (1.0 + 4.0 * along_flow[:7]) + 4.0 * SHARPEN * fraction * (1.0 - fraction) * along_normal)
    phase_post = phase_part - PHASE_RATE * (phase_part - phase_equil)
    return jnp.concatenate([flow_post, phase_post], 0)

def neighbour(values, offset):
    height = values.shape[0]
    padded = jnp.pad(values, ((1, 1), (0, 0), (0, 0)))
    shifted = padded[1 + offset[0]:1 + offset[0] + height]
    return jnp.roll(shifted, (-offset[1], -offset[2]), axis=(1, 2))

def negate(offset):
    return tuple((-entry for entry in offset))

def gradient(values):
    return jnp.stack([(neighbour(values, unit) - neighbour(values, negate(unit))) * 0.5 for unit in UNITS])

def laplace(values):
    total = -6.0 * values
    for unit in UNITS:
        total = total + neighbour(values, unit) + neighbour(values, negate(unit))
    return total

def well_term(fraction):
    return 4.0 * WELL_DEPTH * fraction * (fraction - 1.0) * (fraction - 0.5)

def phase_fields(fraction):
    potential = well_term(fraction) - STIFFNESS * laplace(fraction)
    return (gradient(fraction), gradient(potential))

def stream(post):
    height = post.shape[1]
    outputs = []
    for member in range(26):
        step_z, step_x, step_y = (int(entry) for entry in VELOCITY_ALL[member])
        values = jnp.roll(post[member], (step_x, step_y), axis=(1, 2))
        padded = jnp.pad(values, ((1, 1), (0, 0), (0, 0)))
        values = padded[1 - step_z:1 - step_z + height]
        if step_z == 1:
            values = values.at[0].set(post[OPPOSITE_ALL[member], 0])
        elif step_z == -1:
            values = values.at[height - 1].set(post[OPPOSITE_ALL[member], height - 1])
        outputs.append(values)
    return jnp.stack(outputs)

def plane_adjoint(plane_items):
    populations, phase_grad, potential_grad, arrived = plane_items
    pullback = jax.vjp(collide, populations, phase_grad, potential_grad)[1]
    return pullback(arrived)

def adjoint_step(stored, adjoint):
    populations = stored.astype(jnp.float32)
    fraction = lax.optimization_barrier(jnp.sum(populations[19:], 0))
    (phase_grad, potential_grad), phase_pullback = jax.vjp(phase_fields, fraction)
    stream_pullback = jax.vjp(stream, populations)[1]
    arrived, = stream_pullback(adjoint)
    planes = lax.map(plane_adjoint, (jnp.moveaxis(populations, 1, 0), jnp.moveaxis(phase_grad, 1, 0), jnp.moveaxis(potential_grad, 1, 0), jnp.moveaxis(arrived, 1, 0)))
    restored = [jnp.moveaxis(piece, 0, 1) for piece in planes]
    phase_adjoint, = phase_pullback((restored[1], restored[2]))
    return jnp.concatenate([restored[0][:19], restored[0][19:] + phase_adjoint[None]], 0)

def reference(populations0, populations1, cotangent):
    adjoint1 = adjoint_step(populations1, cotangent)
    return adjoint_step(populations0, adjoint1)
```

```python
import jax
import jax.numpy as jnp
import numpy as np
from jax import lax
from jax.experimental import pallas as pl
from jax.experimental.pallas import tpu as pltpu
from jax.sharding import PartitionSpec as P

VELOCITY = [
    (0, 0, 0),
    (1, 0, 0),
    (-1, 0, 0),
    (0, 1, 0),
    (0, -1, 0),
    (0, 0, 1),
    (0, 0, -1),
    (1, 1, 0),
    (-1, -1, 0),
    (1, -1, 0),
    (-1, 1, 0),
    (1, 0, 1),
    (-1, 0, -1),
    (1, 0, -1),
    (-1, 0, 1),
    (0, 1, 1),
    (0, -1, -1),
    (0, 1, -1),
    (0, -1, 1),
]
OPPOSITE = [0, 2, 1, 4, 3, 6, 5, 8, 7, 10, 9, 12, 11, 14, 13, 16, 15, 18, 17]
VELOCITY = VELOCITY + VELOCITY[:7]
OPPOSITE = OPPOSITE + [19 + mirror for mirror in OPPOSITE[:7]]
WELL = 1.2
STIFFNESS = 0.6
SHARPEN = 0.3
PHASE_RATE = 1.4
MESH = pl.DeviceIdType.MESH

RISING = [i for i in range(26) if VELOCITY[i][0] == 1]
FALLING = [i for i in range(26) if VELOCITY[i][0] == -1]
ALONG_X = {sign: [i for i in range(26) if VELOCITY[i][1] == sign] for sign in (1, -1)}
ALONG_Y = {sign: [i for i in range(26) if VELOCITY[i][2] == sign] for sign in (1, -1)}
DIAGONAL = {VELOCITY[i][1:]: i for i in range(15, 19)}
SIDES = [(-1, 0), (1, 0), (0, -1), (0, 1)]
CORNERS = [(-1, -1), (-1, 1), (1, -1), (1, 1)]
SLOT = {way: i for i, way in enumerate(SIDES)}
SLOT.update({way: i for i, way in enumerate(CORNERS)})


def kernel(
    pop0, pop1, cot, out,
    adj_a, adj_b, phase, grads, sens, phibar, slope, phi,
    z1s, z1r, face1s, face1r, diag1s, diag1r, face0r, diag0s, diag0r,
    z2s, z2r, zd2s, zd2r, face2s, face2r, diag2s, diag2r, d2s, d2r, e2s, e2r,
    z3s, z3r, y3r, x3s, x3r,
    zd4s, zd4r, d4s, d4r, e4s, e4r,
    send_sem, recv_sem,
):
    gx, gy, gz = lax.axis_index("gx"), lax.axis_index("gy"), lax.axis_index("gz")
    nx, ny = lax.axis_size("gx"), lax.axis_size("gy")
    low = gz == 0
    partner = (gx, gy, 1 - gz)

    def device(way):
        return (lax.rem(gx + way[0] + nx, nx), lax.rem(gy + way[1] + ny, ny), gz)

    barrier = pltpu.get_barrier_semaphore()
    for target in [partner] + [device(way) for way in SIDES + CORNERS]:
        pl.semaphore_signal(barrier, inc=1, device_id=target, device_id_type=MESH)

    copies = []

    def send(src, dst, target):
        index = len(copies)
        copy = pltpu.make_async_remote_copy(
            src_ref=src,
            dst_ref=dst,
            send_sem=send_sem.at[index],
            recv_sem=recv_sem.at[index],
            device_id=target,
            device_id_type=MESH,
        )
        copy.start()
        copies.append(copy)
        return copy

    def arrive(group):
        for copy in group:
            copy.wait_recv()

    row = lax.broadcasted_iota(jnp.int32, (8, 128), 0)
    lane = lax.broadcasted_iota(jnp.int32, (8, 128), 1)
    row3 = lax.broadcasted_iota(jnp.int32, (8, 8, 128), 1)
    lane3 = lax.broadcasted_iota(jnp.int32, (8, 8, 128), 2)

    def zeros(*shape):
        return jnp.zeros(shape, jnp.float32)

    def roll(values, shift, axis):
        shift = shift % values.shape[axis]
        return values if shift == 0 else pltpu.roll(values, shift, axis)

    def layers(values, before, after):
        shape = values.shape[1:]
        parts = [zeros(before, *shape)] if before else []
        parts.append(values)
        if after:
            parts.append(zeros(after, *shape))
        return jnp.concatenate(parts, 0)

    def torus(center, rows, lanes, both):
        return jnp.concatenate(
            [jnp.concatenate([center, lanes], 2), jnp.concatenate([rows, both], 2)], 1
        )

    def embed(center):
        nothing = jnp.zeros_like(center)
        return torus(center, nothing, nothing, nothing)

    def vertical_layers(adj):
        return [jnp.where(low, adj[FALLING[k], 8], adj[RISING[k], 1]) for k in range(6)]

    def take_vertical(adj, ref, start):
        for k in range(6):
            layer = ref[start + k]
            adj[RISING[k], 9] = layer
            adj[FALLING[k], 0] = layer

    def pack_x(adj, sign):
        source = 0 if sign == 1 else 7
        packed = None
        for k, i in enumerate(ALONG_X[sign]):
            values = roll(adj[i, 1 + VELOCITY[i][0] : 9 + VELOCITY[i][0]], k - source, 1)
            packed = values if packed is None else jnp.where(row3 == k, values, packed)
        return packed

    def pack_y(adj, sign):
        source = 0 if sign == 1 else 127
        packed = None
        for k, i in enumerate(ALONG_Y[sign]):
            values = roll(adj[i, 1 + VELOCITY[i][0] : 9 + VELOCITY[i][0]], k - source, 2)
            packed = values if packed is None else jnp.where(lane3 == k, values, packed)
        return packed

    def edge_row(sign):
        return 0 if sign == 1 else 7

    def phase_gradients(which, face, diag, start):
        center = phase[which]
        prev_x, next_x = face[SLOT[(1, 0)], :10], face[SLOT[(-1, 0)], :10]
        prev_y, next_y = face[SLOT[(0, 1)], :10], face[SLOT[(0, -1)], :10]
        row10 = lax.broadcasted_iota(jnp.int32, (10, 8, 128), 1)
        lane10 = lax.broadcasted_iota(jnp.int32, (10, 8, 128), 2)
        rows = layers(jnp.where(row10 < 4, next_x, prev_x), 1, 1)
        lanes = layers(jnp.where(lane10 < 64, next_y, prev_y), 1, 1)

        def corner(way):
            return diag[SLOT[way], start]

        lane_z = lax.broadcasted_iota(jnp.int32, (8, 128), 1)
        ahead = jnp.where(lane_z < 64, corner((-1, -1)), corner((-1, 1)))
        behind = jnp.where(lane_z < 64, corner((1, -1)), corner((1, 1)))
        both = jnp.where(
            row3 < 4,
            jnp.broadcast_to(ahead[:, None, :], (8, 8, 128)),
            jnp.broadcast_to(behind[:, None, :], (8, 8, 128)),
        )
        ext = torus(center, rows, lanes, layers(both, 2, 2))
        slope[which] = WELL * (3.0 * ext * ext - 3.0 * ext + 0.5)
        mid = ext[1:11]
        x_up, x_down = roll(mid, -1, 1), roll(mid, 1, 1)
        y_up, y_down = roll(mid, -1, 2), roll(mid, 1, 2)
        lap = ext[:10] + ext[2:] + x_up + x_down + y_up + y_down - 6.0 * mid
        pot = WELL * mid * (mid - 1.0) * (mid - 0.5) - STIFFNESS * lap
        pot = jnp.concatenate(
            [jnp.where(low, 0.0, pot[:1]), pot[1:9], jnp.where(low, pot[9:], 0.0)], 0
        )
        grads[which, 0] = 0.5 * (center[3:11] - center[1:9])
        grads[which, 1] = 0.5 * (x_up - x_down)[1:9, :8, :128]
        grads[which, 2] = 0.5 * (y_up - y_down)[1:9, :8, :128]
        grads[which, 3] = 0.5 * (pot[2:, :8, :128] - pot[:8, :8, :128])
        inner = pot[1:9]
        grads[which, 4] = 0.5 * (roll(inner, -1, 1) - roll(inner, 1, 1))[:, :8, :128]
        grads[which, 5] = 0.5 * (roll(inner, -1, 2) - roll(inner, 1, 2))[:, :8, :128]

    def collide_adjoint(which, pop, adj, face, start, diag, tile, result, shift, with_phi):
        def layer(z, carry):
            def bounce(i, own, bounced):
                if VELOCITY[i][0] == 1:
                    return jnp.where(jnp.logical_and(z == 7, jnp.logical_not(low)), bounced, own)
                if VELOCITY[i][0] == -1:
                    return jnp.where(jnp.logical_and(z == 0, low), bounced, own)
                return own

            def arrived(i):
                cz, cx, cy = VELOCITY[i]
                own = adj[i, z + (1 + cz)]
                erow = 7 if cx == 1 else 0
                elane = 127 if cy == 1 else 0
                moved = own
                if cx:
                    k = ALONG_X[cx].index(i)
                    got = roll(face[SLOT[(-cx, 0)], start + z], erow - k, 0)
                    moved = jnp.where(row == erow, got, roll(own, -cx, 0))
                if cy:
                    k = ALONG_Y[cy].index(i)
                    got = roll(face[SLOT[(0, -cy)], start + z], elane - k, 1)
                    if cx:
                        corner = diag[SLOT[(-cx, -cy)], tile, pl.ds(z, 1), :]
                        corner = roll(jnp.broadcast_to(corner, (8, 128)), -cy, 1)
                        got = jnp.where(row == erow, corner, roll(got, -cx, 0))
                    moved = jnp.where(lane == elane, got, roll(moved, -cy, 1))
                return bounce(i, moved, adj[OPPOSITE[i], z + 1])

            def arrived_phi(i):
                cz, cx, cy = VELOCITY[i]
                own = phi[z + (1 + cz)]
                if cx:
                    erow = 7 if cx == 1 else 0
                    got = jnp.broadcast_to(x3r[SLOT[(-cx, 0)], pl.ds(z, 1), :], (8, 128))
                    own = jnp.where(row == erow, got, roll(own, -cx, 0))
                if cy:
                    elane = 127 if cy == 1 else 0
                    got = roll(y3r[SLOT[(0, -cy)] - 2, z], -cy, 1)
                    own = jnp.where(lane == elane, got, roll(own, -cy, 1))
                return bounce(i, own, phi[z + 1])

            a = [arrived(i) for i in range(26)]
            if with_phi:
                a = a[:19] + [a[i] + arrived_phi(i) for i in range(19, 26)]
            f = [pop[i, z].astype(jnp.float32) for i in range(19)]

            def total(values):
                values = list(values)
                while len(values) > 1:
                    values = [
                        values[j] + values[j + 1] if j + 1 < len(values) else values[j]
                        for j in range(0, len(values), 2)
                    ]
                return values[0]

            def signed(values, weight):
                plus = [values[i] for i in range(len(values)) if weight(i) == 1]
                minus = [values[i] for i in range(len(values)) if weight(i) == -1]
                return total(plus) - total(minus)

            def part(d):
                return lambda i: VELOCITY[i][d]

            def pair(d, e):
                return lambda i: VELOCITY[i][d] * VELOCITY[i][e]

            frac = phase[which, z + 2]
            pressure = total(f)
            momentum = [signed(f, part(d)) for d in range(3)]
            wa = [a[0] * (1.0 / 3.0)]
            wa += [a[i] * (1.0 / 18.0) for i in range(1, 7)]
            wa += [a[i] * (1.0 / 36.0) for i in range(7, 19)]
            a0 = total(wa)
            a1 = [signed(wa, part(d)) for d in range(3)]
            a2 = {}
            for d in range(3):
                a2[d, d] = total([wa[i] for i in range(19) if VELOCITY[i][d]])
                for e in range(d):
                    a2[d, e] = a2[e, d] = signed(wa, pair(d, e))
            af = total([a[i] * f[i] for i in range(19)])
            g = a[19:]
            b0 = 0.25 * g[0] + 0.125 * total(g[1:])
            b1 = [0.125 * (g[1 + 2 * d] - g[2 + 2 * d]) for d in range(3)]

            def dot(u, v):
                return u[0] * v[0] + u[1] * v[1] + u[2] * v[2]

            density = 0.2 + 0.8 * frac
            rate = 1.1 + 0.5 * frac
            half = 1.0 - 0.5 * rate
            pg = [grads[which, d, z] for d in range(3)]
            mg = [grads[which, 3 + d, z] for d in range(3)]
            force = [-frac * m for m in mg]
            inverse = 1.0 / density
            u = [(momentum[d] + 0.5 * force[d]) * inverse for d in range(3)]
            a2u = [dot([a2[d, e] for e in range(3)], u) for d in range(3)]
            a2f = [dot([a2[d, e] for e in range(3)], force) for d in range(3)]
            speed = dot(u, u)
            quad = 3.0 * dot(u, a1) + 4.5 * dot(u, a2u) - 1.5 * speed * a0
            slant = [3.0 * a1[d] - 3.0 * a0 * u[d] + 9.0 * a2u[d] for d in range(3)]
            rate_density = rate * density
            phase_pull = (4.0 * PHASE_RATE) * frac
            ubar = [
                rate_density * slant[d]
                + half * (9.0 * a2f[d] - 3.0 * a0 * force[d])
                + phase_pull * b1[d]
                for d in range(3)
            ]
            jbar = [ubar[d] * inverse for d in range(3)]
            fbar = [half * slant[d] + 0.5 * jbar[d] for d in range(3)]
            density_bar = rate * quad - dot(jbar, u)
            rate_bar = pressure * a0 + density * quad - af - 0.5 * dot(force, slant)
            imag = lax.rsqrt(dot(pg, pg) + 0.0625)
            normal = [p * imag for p in pg]
            nb1 = dot(normal, b1)
            frac_bar = (
                0.5 * rate_bar
                + 0.8 * density_bar
                - dot(mg, fbar)
                + PHASE_RATE * (b0 + 4.0 * dot(u, b1))
                + (PHASE_RATE * 4.0 * SHARPEN) * (1.0 - 2.0 * frac) * nb1
            )
            pull = (PHASE_RATE * 4.0 * SHARPEN) * frac * (1.0 - frac) * imag
            for d in range(3):
                sens[d, z] = pull * (b1[d] - normal[d] * nb1)
                sens[3 + d, z] = -frac * fbar[d]
            phibar[z] = frac_bar
            pbar = rate * a0
            keep = 1.0 - rate
            for i in range(19):
                value = keep * a[i] + pbar
                for d in range(3):
                    if VELOCITY[i][d] == 1:
                        value = value + jbar[d]
                    elif VELOCITY[i][d] == -1:
                        value = value - jbar[d]
                result[i, z + shift] = value
            for k in range(7):
                result[19 + k, z + shift] = (1.0 - PHASE_RATE) * g[k]
            return carry

        lax.fori_loop(0, 8, layer, 0)

    def phase_share(which):
        def spread(first):
            vz = embed(sens[first])
            vx = embed(sens[first + 1])
            vy = embed(sens[first + 2])
            flat = roll(vx, 1, 1) - roll(vx, -1, 1) + roll(vy, 1, 2) - roll(vy, -1, 2)
            return 0.5 * (layers(flat, 1, 1) + layers(vz, 2, 0) - layers(vz, 0, 2))

        mu = spread(3)
        mu = jnp.concatenate(
            [jnp.where(low, 0.0, mu[:1]), mu[1:9], jnp.where(low, mu[9:], 0.0)], 0
        )
        flat = roll(mu, 1, 1) + roll(mu, -1, 1) + roll(mu, 1, 2) + roll(mu, -1, 2) - 6.0 * mu
        lap = layers(flat, 1, 1) + layers(mu, 2, 0) + layers(mu, 0, 2)
        rest = spread(0) + layers(embed(phibar[...]), 1, 1)
        return slope[which] * layers(mu, 1, 1) - STIFFNESS * lap + layers(rest, 1, 1)

    def send_share(share, zs, zr):
        edge = jnp.where(low, share[10:], share[:2])
        zs[...] = edge
        return send(zs, zr, partner)

    def share_sides(share, zcopy, zr, ds, dr, es, er):
        zcopy.wait_recv()
        extra = zr[...]
        lower = share[2:4] + jnp.where(low, 0.0, extra)
        upper = share[8:10] + jnp.where(low, extra, 0.0)
        share = jnp.concatenate([lower, share[4:8], upper], 0)
        ds[0] = share[:, 8:, :128]
        ds[1] = share[:, :8, 128:]
        es[0] = share[:, 15, 128:]
        es[1] = share[:, 8, 128:]
        group = []
        for way in SIDES:
            source = ds.at[0] if way[0] else ds.at[1]
            group.append(send(source, dr.at[SLOT[way]], device(way)))
        for way in CORNERS:
            group.append(send(es.at[0 if way[0] < 0 else 1], er.at[SLOT[way]], device(way)))
        return share[:, :8, :128], group

    def collect_share(center, group, dr, er):
        arrive(group)
        total = center
        total = total + jnp.where(row3 < 2, dr[SLOT[(1, 0)]], 0.0)
        total = total + jnp.where(row3 >= 6, dr[SLOT[(-1, 0)]], 0.0)
        total = total + jnp.where(lane3 < 2, dr[SLOT[(0, 1)]], 0.0)
        total = total + jnp.where(lane3 >= 126, dr[SLOT[(0, -1)]], 0.0)
        for way in CORNERS:
            at_row = row3 == (0 if way[0] == 1 else 7)
            at_lane = lane3 == (0 if way[1] == 1 else 127)
            wide = jnp.broadcast_to(er[SLOT[way]][:, None, :], (8, 8, 128))
            total = total + jnp.where(jnp.logical_and(at_row, at_lane), wide, 0.0)
        return total

    for which, pop in ((0, pop0), (1, pop1)):
        terms = [pop[i].astype(jnp.float32) for i in range(19, 26)]
        value = terms[0]
        for term in terms[1:]:
            value = value + term
        phase[which, 2:10] = value
    for which in range(2):
        z1s[2 * which : 2 * which + 2] = jnp.where(low, phase[which, 8:10], phase[which, 2:4])
    for k in range(6):
        z1s[4 + k] = jnp.where(low, cot[FALLING[k], 7], cot[RISING[k], 0])
    pl.semaphore_wait(barrier, 9)
    vertical = send(z1s, z1r, partner)
    for i in range(26):
        adj_a[i, 1:9] = cot[i]
    vertical.wait_recv()
    for which in range(2):
        got = z1r[2 * which : 2 * which + 2]
        phase[which, :2] = jnp.where(low, 0.0, got)
        phase[which, 10:] = jnp.where(low, got, 0.0)
    take_vertical(adj_a, z1r, 4)

    first = []
    for way in CORNERS:
        slot = SLOT[way]
        i = DIAGONAL[(-way[0], -way[1])]
        r = edge_row(-way[0])
        diag1s[slot, 0] = phase[1, 2:10, r, :]
        diag1s[slot, 1] = phase[0, 2:10, r, :]
        diag1s[slot, 2] = adj_a[i, 1:9, r, :]
        first.append(send(diag1s.at[slot], diag1r.at[slot], device(way)))
    for way in SIDES:
        slot = SLOT[way]
        face1s[slot, :10] = phase[1, 1:11]
        face1s[slot, 10:] = pack_x(adj_a, -way[0]) if way[0] else pack_y(adj_a, -way[1])
        first.append(send(face1s.at[slot], face1r.at[slot], device(way)))
    later = []
    for way in SIDES:
        slot = SLOT[way]
        later.append(send(phase.at[0, pl.ds(1, 10)], face0r.at[slot], device(way)))
    arrive(first)
    phase_gradients(1, face1r, diag1r, 0)
    collide_adjoint(1, pop1, adj_a, face1r, 10, diag1r, 2, adj_b, 1, False)

    for k, layer in enumerate(vertical_layers(adj_b)):
        z2s[k] = layer
    vertical = send(z2s, z2r, partner)
    share = phase_share(1)
    zcopy = send_share(share, zd2s, zd2r)
    vertical.wait_recv()
    take_vertical(adj_b, z2r, 0)
    second = []
    for way in CORNERS:
        slot = SLOT[way]
        diag2s[slot, 0] = adj_b[DIAGONAL[(-way[0], -way[1])], 1:9, edge_row(-way[0]), :]
        second.append(send(diag2s.at[slot], diag2r.at[slot], device(way)))
    for way in SIDES:
        slot = SLOT[way]
        face2s[slot] = pack_x(adj_b, -way[0]) if way[0] else pack_y(adj_b, -way[1])
        second.append(send(face2s.at[slot], face2r.at[slot], device(way)))
    center, group = share_sides(share, zcopy, zd2r, d2s, d2r, e2s, e2r)
    arrive(later)
    phase_gradients(0, face0r, diag1r, 1)
    phi[1:9] = collect_share(center, group, d2r, e2r)
    z3s[...] = jnp.where(low, phi[8], phi[1])
    third = [send(z3s, z3r, partner)]
    for way in SIDES:
        slot = SLOT[way]
        if way[0]:
            x3s[slot] = phi[1:9, edge_row(-way[0]), :]
            third.append(send(x3s.at[slot], x3r.at[slot], device(way)))
        else:
            third.append(send(phi.at[pl.ds(1, 8)], y3r.at[slot - 2], device(way)))
    arrive(second)
    arrive(third)
    phi[0] = z3r[...]
    phi[9] = z3r[...]
    collide_adjoint(0, pop0, adj_b, face2r, 0, diag2r, 0, out, 0, True)

    share = phase_share(0)
    zcopy = send_share(share, zd4s, zd4r)
    center, group = share_sides(share, zcopy, zd4r, d4s, d4r, e4s, e4r)
    total = collect_share(center, group, d4r, e4r)
    for k in range(7):
        out[19 + k] = out[19 + k] + total
    for copy in copies:
        copy.wait_send()


def local(populations0, populations1, cotangent):
    def vmem(*shape):
        return pltpu.VMEM(shape, jnp.float32)

    tile = (8, 128)
    scratch = [
        vmem(26, 10, *tile),
        vmem(26, 10, *tile),
        vmem(2, 12, *tile),
        vmem(2, 6, 8, *tile),
        vmem(6, 8, *tile),
        vmem(8, *tile),
        vmem(2, 12, 16, 256),
        vmem(10, *tile),
        vmem(10, *tile),
        vmem(10, *tile),
        vmem(4, 18, *tile),
        vmem(4, 18, *tile),
        vmem(4, 3, *tile),
        vmem(4, 3, *tile),
        vmem(4, 10, *tile),
        vmem(1, *tile),
        vmem(1, *tile),
        vmem(6, *tile),
        vmem(6, *tile),
        vmem(2, 16, 256),
        vmem(2, 16, 256),
        vmem(4, 8, *tile),
        vmem(4, 8, *tile),
        vmem(4, 1, *tile),
        vmem(4, 1, *tile),
        vmem(2, 8, *tile),
        vmem(4, 8, *tile),
        vmem(2, *tile),
        vmem(4, *tile),
        vmem(*tile),
        vmem(*tile),
        vmem(2, 8, *tile),
        vmem(2, *tile),
        vmem(2, *tile),
        vmem(2, 16, 256),
        vmem(2, 16, 256),
        vmem(2, 8, *tile),
        vmem(4, 8, *tile),
        vmem(2, *tile),
        vmem(4, *tile),
        pltpu.SemaphoreType.DMA((48,)),
        pltpu.SemaphoreType.DMA((48,)),
    ]
    return pl.pallas_call(
        kernel,
        out_shape=jax.ShapeDtypeStruct(cotangent.shape, jnp.float32),
        in_specs=[pl.BlockSpec(memory_space=pltpu.VMEM)] * 3,
        out_specs=pl.BlockSpec(memory_space=pltpu.VMEM),
        scratch_shapes=scratch,
        compiler_params=pltpu.CompilerParams(
            collective_id=0, has_side_effects=True, vmem_limit_bytes=40 * 1024 * 1024
        ),
    )(populations0, populations1, cotangent)


def solution(mesh):
    spec = P(None, "gz", "gx", "gy")
    return jax.shard_map(
        local, mesh=mesh, in_specs=(spec, spec, spec), out_specs=spec, check_vma=False
    )
```

```python
import jax
import jax.numpy as jnp
import numpy as np
from jax import lax
from jax.experimental import pallas as pl
from jax.experimental.pallas import tpu as pltpu
from jax.sharding import PartitionSpec as P

VELOCITY = [
    (0, 0, 0),
    (1, 0, 0),
    (-1, 0, 0),
    (0, 1, 0),
    (0, -1, 0),
    (0, 0, 1),
    (0, 0, -1),
    (1, 1, 0),
    (-1, -1, 0),
    (1, -1, 0),
    (-1, 1, 0),
    (1, 0, 1),
    (-1, 0, -1),
    (1, 0, -1),
    (-1, 0, 1),
    (0, 1, 1),
    (0, -1, -1),
    (0, 1, -1),
    (0, -1, 1),
]
OPPOSITE = [0, 2, 1, 4, 3, 6, 5, 8, 7, 10, 9, 12, 11, 14, 13, 16, 15, 18, 17]
VELOCITY = VELOCITY + VELOCITY[:7]
OPPOSITE = OPPOSITE + [19 + mirror for mirror in OPPOSITE[:7]]
WELL = 1.2
STIFFNESS = 0.6
SHARPEN = 0.3
PHASE_RATE = 1.4
MESH = pl.DeviceIdType.MESH

RISING = [i for i in range(26) if VELOCITY[i][0] == 1]
FALLING = [i for i in range(26) if VELOCITY[i][0] == -1]
ALONG_X = {sign: [i for i in range(26) if VELOCITY[i][1] == sign] for sign in (1, -1)}
ALONG_Y = {sign: [i for i in range(26) if VELOCITY[i][2] == sign] for sign in (1, -1)}
DIAGONAL = {VELOCITY[i][1:]: i for i in range(15, 19)}
SIDES = [(-1, 0), (1, 0), (0, -1), (0, 1)]
CORNERS = [(-1, -1), (-1, 1), (1, -1), (1, 1)]
SLOT = {way: i for i, way in enumerate(SIDES)}
SLOT.update({way: i for i, way in enumerate(CORNERS)})


def kernel(
    pop0_hbm, pop1_hbm, cot_hbm, out,
    pop0, pop1, adj_a, adj_b, phase, grads, sens, phibar, slope, phi, flow, moments, arrive_f,
    z1s, z1r, x1s, x1r, y1s, y1r, c1s, c1r,
    z2s, z2r, x2s, x2r, y2s, y2r, c2s, c2r,
    zd2s, zd2r, xd2s, xd2r, yd2s, yd2r, cd2s, cd2r,
    z3s, z3r, x3s, x3r, y3r,
    zd4s, zd4r, xd4s, xd4r, yd4s, yd4r, cd4s, cd4r,
    send_sem, recv_sem, load_sem,
):
    gx, gy, gz = lax.axis_index("gx"), lax.axis_index("gy"), lax.axis_index("gz")
    nx, ny = lax.axis_size("gx"), lax.axis_size("gy")
    low = gz == 0
    partner = (gx, gy, 1 - gz)
    pops = (pop0, pop1)

    def load(src, dst, index):
        copy = pltpu.make_async_copy(src, dst, load_sem.at[index])
        copy.start()
        return copy

    load_phase = [
        load(pop1_hbm.at[pl.ds(19, 7)], pop1.at[pl.ds(19, 7)], 0),
        load(pop0_hbm.at[pl.ds(19, 7)], pop0.at[pl.ds(19, 7)], 1),
    ]
    load_cot = [
        load(cot_hbm.at[pl.ds(0, 13)], adj_a.at[pl.ds(0, 13), pl.ds(1, 8)], 2),
        load(cot_hbm.at[pl.ds(13, 13)], adj_a.at[pl.ds(13, 13), pl.ds(1, 8)], 3),
    ]
    load_flow = [
        load(pop0_hbm.at[pl.ds(0, 19)], pop0.at[pl.ds(0, 19)], 4),
        load(pop1_hbm.at[pl.ds(0, 19)], pop1.at[pl.ds(0, 19)], 5),
    ]

    def device(way):
        return (lax.rem(gx + way[0] + nx, nx), lax.rem(gy + way[1] + ny, ny), gz)

    barrier = pltpu.get_barrier_semaphore()
    for target in [partner] + [device(way) for way in SIDES + CORNERS]:
        pl.semaphore_signal(barrier, inc=1, device_id=target, device_id_type=MESH)

    copies = []

    def send(src, dst, target):
        index = len(copies)
        copy = pltpu.make_async_remote_copy(
            src_ref=src,
            dst_ref=dst,
            send_sem=send_sem.at[index],
            recv_sem=recv_sem.at[index],
            device_id=target,
            device_id_type=MESH,
        )
        copy.start()
        copies.append(copy)
        return copy

    def arrive(group):
        for copy in group:
            copy.wait_recv()

    row = lax.broadcasted_iota(jnp.int32, (8, 128), 0)
    lane = lax.broadcasted_iota(jnp.int32, (8, 128), 1)

    def rows_of(count):
        return lax.broadcasted_iota(jnp.int32, (count, 8, 128), 1)

    def lanes_of(count):
        return lax.broadcasted_iota(jnp.int32, (count, 8, 128), 2)

    row3, lane3 = rows_of(8), lanes_of(8)

    def roll(values, shift, axis):
        shift = shift % values.shape[axis]
        return values if shift == 0 else pltpu.roll(values, shift, axis)

    def layers(values, before, after):
        shape = values.shape[1:]
        parts = [jnp.zeros((before, *shape), jnp.float32)] if before else []
        parts.append(values)
        if after:
            parts.append(jnp.zeros((after, *shape), jnp.float32))
        return jnp.concatenate(parts, 0)

    def wide(rows):
        return jnp.broadcast_to(rows[:, None, :], (rows.shape[0], 8, 128))

    def shift(inner, outer, step, axis):
        some = inner if inner is not None else outer
        size = some.shape[axis]
        edge = 0 if step == 1 else size - 1
        at_edge = lax.broadcasted_iota(jnp.int32, some.shape, axis) == edge
        a = 0.0 if inner is None else roll(inner, step, axis)
        b = 0.0 if outer is None else roll(outer, step, axis)
        return jnp.where(at_edge, b, a), jnp.where(at_edge, a, b)

    def difference(inner, outer, axis):
        up, down = shift(inner, outer, -1, axis), shift(inner, outer, 1, axis)
        return up[0] - down[0], up[1] - down[1]

    def both_sides(inner, outer, axis):
        up, down = shift(inner, outer, -1, axis), shift(inner, outer, 1, axis)
        return up[0] + down[0], up[1] + down[1]

    def vertical_layers(adj, ref, start):
        for k in range(6):
            ref[start + k] = jnp.where(low, adj[FALLING[k], 8], adj[RISING[k], 1])

    def take_vertical(adj, ref, start):
        for k in range(6):
            layer = ref[start + k]
            adj[RISING[k], 9] = layer
            adj[FALLING[k], 0] = layer

    def edge_row(sign):
        return 0 if sign == 1 else 7

    def rows_x(adj, sign, ref, slot):
        for k, i in enumerate(ALONG_X[sign]):
            cz = VELOCITY[i][0]
            ref[slot, k] = adj[i, 1 + cz : 9 + cz, edge_row(sign), :]

    def pack_y(adj, sign, packed):
        source = 0 if sign == 1 else 127
        for k, i in enumerate(ALONG_Y[sign]):
            cz = VELOCITY[i][0]
            values = roll(adj[i, 1 + cz : 9 + cz], k - source, 2)
            packed = values if packed is None else jnp.where(lane3 == k, values, packed)
        return packed

    def well(value):
        return WELL * value * (value - 1.0) * (value - 0.5)

    def well_slope(value):
        return WELL * (3.0 * value * value - 3.0 * value + 0.5)

    def phase_gradients(which, tile, place):
        full = phase[which]
        ahead, behind = SLOT[(-1, 0)], SLOT[(1, 0)]

        def side(slot):
            near = wide(x1r[slot, tile])
            far = wide(x1r[slot, tile + 1])
            first = x1r[slot, 10, place : place + 1, :]
            last = x1r[slot, 10, place + 1 : place + 2, :]
            first = jnp.broadcast_to(first, (8, 128))[None]
            last = jnp.broadcast_to(last, (8, 128))[None]
            return first, near, far, last

        first_n, near_n, far_n, last_n = side(ahead)
        first_p, near_p, far_p, last_p = side(behind)
        x_mid = jnp.where(
            row3 < 4,
            jnp.where(row3 == 0, near_n, far_n),
            jnp.where(row3 == 7, near_p, far_p),
        )
        upper_half = row[None] < 4
        x_tile = jnp.concatenate(
            [jnp.where(upper_half, first_n, first_p), x_mid, jnp.where(upper_half, last_n, last_p)], 0
        )
        start = 6 + 2 * (1 - which)
        y_tile = jnp.where(
            lanes_of(10) < 64,
            roll(y1r[SLOT[(0, -1)] - 2], -start, 2),
            roll(y1r[SLOT[(0, 1)] - 2], 126 - start, 2),
        )
        t = 1 - which
        before_y, after_y = lane < 64, lane >= 64
        corner_n = jnp.where(before_y, c1r[SLOT[(-1, -1)], t], c1r[SLOT[(-1, 1)], t])
        corner_p = jnp.where(before_y, c1r[SLOT[(1, -1)], t], c1r[SLOT[(1, 1)], t])
        b_tile = jnp.where(row3 < 4, wide(corner_n), wide(corner_p))
        mid, y_mid = full[1:11], y_tile[1:9]
        slope[which, 0] = well_slope(mid)
        slope[which, 1] = well_slope(x_tile)
        slope[which, 2] = well_slope(y_tile)

        x_up, x_down = shift(mid, x_tile, -1, 1), shift(mid, x_tile, 1, 1)
        y_up, y_down = shift(mid, y_tile, -1, 2), shift(mid, y_tile, 1, 2)
        grads[which, 0] = 0.5 * (full[3:11] - full[1:9])
        grads[which, 1] = 0.5 * (x_up[0] - x_down[0])[1:9]
        grads[which, 2] = 0.5 * (y_up[0] - y_down[0])[1:9]
        lap = x_up[0] + x_down[0] + y_up[0] + y_down[0] + full[:10] + full[2:] - 6.0 * mid
        pot = well(mid) - STIFFNESS * lap
        pot = jnp.concatenate(
            [jnp.where(low, 0.0, pot[:1]), pot[1:9], jnp.where(low, pot[9:], 0.0)], 0
        )
        lap = (x_up[1] + x_down[1])[1:9] + both_sides(x_mid, b_tile, 2)[0]
        lap = lap + x_tile[:8] + x_tile[2:] - 6.0 * x_mid
        pot_x = well(x_mid) - STIFFNESS * lap
        lap = (y_up[1] + y_down[1])[1:9] + both_sides(y_mid, b_tile, 1)[0]
        lap = lap + y_tile[:8] + y_tile[2:] - 6.0 * y_mid
        pot_y = well(y_mid) - STIFFNESS * lap
        grads[which, 3] = 0.5 * (pot[2:] - pot[:8])
        grads[which, 4] = 0.5 * difference(pot[1:9], pot_x, 1)[0]
        grads[which, 5] = 0.5 * difference(pot[1:9], pot_y, 2)[0]

    def total(values):
        values = list(values)
        while len(values) > 1:
            values = [
                values[j] + values[j + 1] if j + 1 < len(values) else values[j]
                for j in range(0, len(values), 2)
            ]
        return values[0]

    def signed(values, weight):
        plus = [values[i] for i in range(len(values)) if weight(i) == 1]
        minus = [values[i] for i in range(len(values)) if weight(i) == -1]
        return total(plus) - total(minus)

    def part(d):
        return lambda i: VELOCITY[i][d]

    def pair(d, e):
        return lambda i: VELOCITY[i][d] * VELOCITY[i][e]

    def dot(u, v):
        return u[0] * v[0] + u[1] * v[1] + u[2] * v[2]

    def flow_moments(which):
        def layer(z, carry):
            f = [pops[which][i, z].astype(jnp.float32) for i in range(19)]
            flow[which, 0, z] = total(f)
            for d in range(3):
                flow[which, 1 + d, z] = signed(f, part(d))
            return carry

        lax.fori_loop(0, 8, layer, 0)

    def bounce(z, i, own, bounced):
        if VELOCITY[i][0] == 1:
            return jnp.where(jnp.logical_and(z == 7, jnp.logical_not(low)), bounced, own)
        if VELOCITY[i][0] == -1:
            return jnp.where(jnp.logical_and(z == 0, low), bounced, own)
        return own

    def arrived(z, i, adj, xr, yr, ystart, cr, tile):
        cz, cx, cy = VELOCITY[i]
        own = adj[i, z + (1 + cz)]
        erow = 7 if cx == 1 else 0
        elane = 127 if cy == 1 else 0
        moved = own
        if cx:
            k = ALONG_X[cx].index(i)
            got = jnp.broadcast_to(xr[SLOT[(-cx, 0)], k, pl.ds(z, 1), :], (8, 128))
            moved = jnp.where(row == erow, got, roll(own, -cx, 0))
        if cy:
            k = ALONG_Y[cy].index(i)
            got = roll(yr[SLOT[(0, -cy)] - 2, ystart + z], elane - k, 1)
            if cx:
                corner = cr[SLOT[(-cx, -cy)], tile, pl.ds(z, 1), :]
                corner = roll(jnp.broadcast_to(corner, (8, 128)), -cy, 1)
                got = jnp.where(row == erow, corner, roll(got, -cx, 0))
            moved = jnp.where(lane == elane, got, roll(moved, -cy, 1))
        return bounce(z, i, moved, adj[OPPOSITE[i], z + 1])

    PAIRS = [(0, 0), (1, 1), (2, 2), (1, 0), (2, 0), (2, 1)]

    def gather_flow(which, *sources):
        def layer(z, carry):
            a = [arrived(z, i, *sources) for i in range(19)]
            for i in range(19):
                arrive_f[i, z] = a[i]
            wa = [a[0] * (1.0 / 3.0)]
            wa += [a[i] * (1.0 / 18.0) for i in range(1, 7)]
            wa += [a[i] * (1.0 / 36.0) for i in range(7, 19)]
            moments[0, z] = total(wa)
            for d in range(3):
                moments[1 + d, z] = signed(wa, part(d))
            for n, (d, e) in enumerate(PAIRS):
                if d == e:
                    moments[4 + n, z] = total([wa[i] for i in range(19) if VELOCITY[i][d]])
                else:
                    moments[4 + n, z] = signed(wa, pair(d, e))
            moments[10, z] = total([a[i] * pops[which][i, z].astype(jnp.float32) for i in range(19)])
            return carry

        lax.fori_loop(0, 8, layer, 0)

    def collide_adjoint(which, sources, result, offset, with_phi):
        def layer(z, carry):
            def arrived_phi(i):
                cz, cx, cy = VELOCITY[i]
                own = phi[z + (1 + cz)]
                if cx:
                    erow = 7 if cx == 1 else 0
                    got = jnp.broadcast_to(x3r[SLOT[(-cx, 0)], pl.ds(z, 1), :], (8, 128))
                    own = jnp.where(row == erow, got, roll(own, -cx, 0))
                if cy:
                    elane = 127 if cy == 1 else 0
                    got = roll(y3r[SLOT[(0, -cy)] - 2, z], -cy, 1)
                    own = jnp.where(lane == elane, got, roll(own, -cy, 1))
                return bounce(z, i, own, phi[z + 1])

            g = [arrived(z, i, *sources) for i in range(19, 26)]
            if with_phi:
                g = [g[k] + arrived_phi(19 + k) for k in range(7)]
            frac = phase[which, z + 2]
            pressure = flow[which, 0, z]
            momentum = [flow[which, 1 + d, z] for d in range(3)]
            a0 = moments[0, z]
            a1 = [moments[1 + d, z] for d in range(3)]
            a2 = {}
            for n, (d, e) in enumerate(PAIRS):
                a2[d, e] = a2[e, d] = moments[4 + n, z]
            af = moments[10, z]
            b0 = 0.25 * g[0] + 0.125 * total(g[1:])
            b1 = [0.125 * (g[1 + 2 * d] - g[2 + 2 * d]) for d in range(3)]
            density = 0.2 + 0.8 * frac
            rate = 1.1 + 0.5 * frac
            half = 1.0 - 0.5 * rate
            pg = [grads[which, d, z] for d in range(3)]
            mg = [grads[which, 3 + d, z] for d in range(3)]
            force = [-frac * m for m in mg]
            inverse = 1.0 / density
            u = [(momentum[d] + 0.5 * force[d]) * inverse for d in range(3)]
            a2u = [dot([a2[d, e] for e in range(3)], u) for d in range(3)]
            a2f = [dot([a2[d, e] for e in range(3)], force) for d in range(3)]
            speed = dot(u, u)
            quad = 3.0 * dot(u, a1) + 4.5 * dot(u, a2u) - 1.5 * speed * a0
            slant = [3.0 * a1[d] - 3.0 * a0 * u[d] + 9.0 * a2u[d] for d in range(3)]
            rate_density = rate * density
            phase_pull = (4.0 * PHASE_RATE) * frac
            ubar = [
                rate_density * slant[d]
                + half * (9.0 * a2f[d] - 3.0 * a0 * force[d])
                + phase_pull * b1[d]
                for d in range(3)
            ]
            jbar = [ubar[d] * inverse for d in range(3)]
            fbar = [half * slant[d] + 0.5 * jbar[d] for d in range(3)]
            density_bar = rate * quad - dot(jbar, u)
            rate_bar = pressure * a0 + density * quad - af - 0.5 * dot(force, slant)
            imag = lax.rsqrt(dot(pg, pg) + 0.0625)
            normal = [p * imag for p in pg]
            nb1 = dot(normal, b1)
            frac_bar = (
                0.5 * rate_bar
                + 0.8 * density_bar
                - dot(mg, fbar)
                + PHASE_RATE * (b0 + 4.0 * dot(u, b1))
                + (PHASE_RATE * 4.0 * SHARPEN) * (1.0 - 2.0 * frac) * nb1
            )
            pull = (PHASE_RATE * 4.0 * SHARPEN) * frac * (1.0 - frac) * imag
            for d in range(3):
                sens[d, z] = pull * (b1[d] - normal[d] * nb1)
                sens[3 + d, z] = -frac * fbar[d]
            phibar[z] = frac_bar
            pbar = rate * a0
            keep = 1.0 - rate
            for i in range(19):
                value = keep * arrive_f[i, z] + pbar
                for d in range(3):
                    if VELOCITY[i][d] == 1:
                        value = value + jbar[d]
                    elif VELOCITY[i][d] == -1:
                        value = value - jbar[d]
                result[i, z + offset] = value
            for k in range(7):
                result[19 + k, z + offset] = (1.0 - PHASE_RATE) * g[k]
            return carry

        lax.fori_loop(0, 8, layer, 0)

    def phase_share(which):
        def spread(first):
            vz = sens[first]
            in_x, out_x = difference(sens[first + 1], None, 1)
            in_y, out_y = difference(sens[first + 2], None, 2)
            inner = layers(-0.5 * (in_x + in_y), 1, 1)
            inner = inner + 0.5 * (layers(vz, 2, 0) - layers(vz, 0, 2))
            return inner, layers(-0.5 * out_x, 1, 1), layers(-0.5 * out_y, 1, 1)

        mu, mu_x, mu_y = spread(3)
        mu = jnp.concatenate(
            [jnp.where(low, 0.0, mu[:1]), mu[1:9], jnp.where(low, mu[9:], 0.0)], 0
        )
        own, own_x, own_y = spread(0)
        in_x, out_x = both_sides(mu, mu_x, 1)
        in_y, out_y = both_sides(mu, mu_y, 2)
        over_x, corner_x = both_sides(mu_x[1:9], None, 2)
        over_y, corner_y = both_sides(mu_y[1:9], None, 1)
        inner = slope[which, 0] * mu - STIFFNESS * (in_x + in_y - 6.0 * mu) + own
        inner = inner + layers(phibar[...], 1, 1)
        inner = layers(inner, 1, 1) - STIFFNESS * (layers(mu, 2, 0) + layers(mu, 0, 2))

        def beside(scale, values, out_share, over, extra):
            vertical = layers(values[1:], 0, 1) + layers(values[:9], 1, 0)
            lap = out_share + layers(over, 1, 1) + vertical - 6.0 * values
            return scale * values - STIFFNESS * lap + extra

        side_x = beside(slope[which, 1], mu_x, out_x, over_x, own_x)
        side_y = beside(slope[which, 2], mu_y, out_y, over_y, own_y)
        return inner, side_x, side_y, -STIFFNESS * (corner_x + corner_y)

    def send_share(share, zs, zr):
        inner, side_x, side_y, _ = share
        zs[:2] = jnp.where(low, inner[10:], inner[:2])
        zs[2:3] = jnp.where(low, side_x[9:], side_x[:1])
        zs[3:4] = jnp.where(low, side_y[9:], side_y[:1])
        return send(zs, zr, partner)

    def share_sides(share, zcopy, zr, xs, xr, ys, yr, cs, cr):
        inner, side_x, side_y, corner = share
        zcopy.wait_recv()

        def merge(values, extra, count):
            lower = values[:count] + jnp.where(low, 0.0, extra)
            upper = values[8 - count :] + jnp.where(low, extra, 0.0)
            return jnp.concatenate([lower, values[count : 8 - count], upper], 0)

        group = []
        ys[...] = merge(side_y[1:9], zr[3:4], 1)
        for way in SIDES[2:]:
            slot = SLOT[way] - 2
            group.append(send(ys, yr.at[slot], device(way)))
        side_x = merge(side_x[1:9], zr[2:3], 1)
        xs[0, 0], xs[0, 1] = side_x[:, 7, :], side_x[:, 6, :]
        xs[1, 0], xs[1, 1] = side_x[:, 0, :], side_x[:, 1, :]
        cs[0], cs[1] = corner[:, 7, :], corner[:, 0, :]
        for way in CORNERS:
            group.append(send(cs.at[0 if way[0] < 0 else 1], cr.at[SLOT[way]], device(way)))
        for way in SIDES[:2]:
            slot = SLOT[way]
            group.append(send(xs.at[slot], xr.at[slot], device(way)))
        return merge(inner[2:10], zr[:2], 2), group

    def collect_share(center, group, xr, yr, cr):
        arrive(group)
        prev, after = SLOT[(1, 0)], SLOT[(-1, 0)]
        near = jnp.where(row3 < 4, wide(xr[prev, 0]), wide(xr[after, 0]))
        far = jnp.where(row3 < 4, wide(xr[prev, 1]), wide(xr[after, 1]))
        end = jnp.logical_or(row3 == 0, row3 == 7)
        next_end = jnp.logical_or(row3 == 1, row3 == 6)
        result = center + jnp.where(end, near, jnp.where(next_end, far, 0.0))
        from_y = jnp.where(lane3 < 64, yr[SLOT[(0, 1)] - 2], yr[SLOT[(0, -1)] - 2])
        result = result + jnp.where(jnp.logical_or(lane3 < 2, lane3 >= 126), from_y, 0.0)
        before = lane < 64
        ends = jnp.logical_or(lane == 0, lane == 127)
        prev_c = jnp.where(ends, jnp.where(before, cr[SLOT[(1, 1)]], cr[SLOT[(1, -1)]]), 0.0)
        next_c = jnp.where(ends, jnp.where(before, cr[SLOT[(-1, 1)]], cr[SLOT[(-1, -1)]]), 0.0)
        corners = jnp.where(row3 == 0, wide(prev_c), wide(next_c))
        return result + jnp.where(end, corners, 0.0)

    for copy in load_phase:
        copy.wait()
    for which in range(2):
        phase[which, 2:10] = total([pops[which][i].astype(jnp.float32) for i in range(19, 26)])
        z1s[2 * which : 2 * which + 2] = jnp.where(low, phase[which, 8:10], phase[which, 2:4])
    for copy in load_cot:
        copy.wait()
    vertical_layers(adj_a, z1s, 4)
    pl.semaphore_wait(barrier, 9)
    vertical = send(z1s, z1r, partner)
    for copy in load_flow:
        copy.wait()
    flow_moments(1)
    vertical.wait_recv()
    for which in range(2):
        got = z1r[2 * which : 2 * which + 2]
        phase[which, :2] = jnp.where(low, 0.0, got)
        phase[which, 10:] = jnp.where(low, got, 0.0)
    take_vertical(adj_a, z1r, 4)

    first = []
    for way in SIDES[2:]:
        slot = SLOT[way] - 2
        source = 0 if way[1] < 0 else 126
        packed = jnp.where(
            lanes_of(10) < 8,
            roll(phase[1, 1:11], 6 - source, 2),
            roll(phase[0, 1:11], 8 - source, 2),
        )
        y1s[slot, 0] = packed[0]
        y1s[slot, 9] = packed[9]
        middle = packed[1:9]
        entries = pack_y(adj_a, -way[1], None)
        y1s[slot, 1:9] = jnp.where(lane3 < 6, entries, middle)
        first.append(send(y1s.at[slot], y1r.at[slot], device(way)))
    for way in CORNERS:
        slot = SLOT[way]
        r = edge_row(-way[0])
        c1s[slot, 0] = phase[1, 2:10, r, :]
        c1s[slot, 1] = phase[0, 2:10, r, :]
        c1s[slot, 2] = adj_a[DIAGONAL[(-way[0], -way[1])], 1:9, r, :]
        first.append(send(c1s.at[slot], c1r.at[slot], device(way)))
    for way in SIDES[:2]:
        slot = SLOT[way]
        r = edge_row(-way[0])
        rows_x(adj_a, -way[0], x1s, slot)
        for n, which in enumerate((1, 0)):
            x1s[slot, 6 + 2 * n] = phase[which, 2:10, r, :]
            x1s[slot, 7 + 2 * n] = phase[which, 2:10, r + (1 if r == 0 else -1), :]
            x1s[slot, 10, 2 * n : 2 * n + 1, :] = phase[which, 1, r : r + 1, :]
            x1s[slot, 10, 2 * n + 1 : 2 * n + 2, :] = phase[which, 10, r : r + 1, :]
        x1s[slot, 10, 4:, :] = jnp.zeros((4, 128), jnp.float32)
        first.append(send(x1s.at[slot], x1r.at[slot], device(way)))
    flow_moments(0)
    arrive(first)
    sources = (adj_a, x1r, y1r, 1, c1r, 2)
    phase_gradients(1, 6, 0)
    gather_flow(1, *sources)
    collide_adjoint(1, sources, adj_b, 1, False)

    vertical_layers(adj_b, z2s, 0)
    vertical = send(z2s, z2r, partner)
    share = phase_share(1)
    zcopy = send_share(share, zd2s, zd2r)
    phase_gradients(0, 8, 2)
    center, group = share_sides(share, zcopy, zd2r, xd2s, xd2r, yd2s, yd2r, cd2s, cd2r)
    vertical.wait_recv()
    take_vertical(adj_b, z2r, 0)
    second = []
    for way in SIDES[2:]:
        slot = SLOT[way] - 2
        y2s[slot] = pack_y(adj_b, -way[1], None)
        second.append(send(y2s.at[slot], y2r.at[slot], device(way)))
    for way in CORNERS:
        slot = SLOT[way]
        c2s[slot, 0] = adj_b[DIAGONAL[(-way[0], -way[1])], 1:9, edge_row(-way[0]), :]
        second.append(send(c2s.at[slot], c2r.at[slot], device(way)))
    for way in SIDES[:2]:
        slot = SLOT[way]
        rows_x(adj_b, -way[0], x2s, slot)
        second.append(send(x2s.at[slot], x2r.at[slot], device(way)))
    phi[1:9] = collect_share(center, group, xd2r, yd2r, cd2r)
    third = []
    for way in SIDES:
        slot = SLOT[way]
        if way[0]:
            x3s[slot] = phi[1:9, edge_row(-way[0]), :]
            third.append(send(x3s.at[slot], x3r.at[slot], device(way)))
        else:
            third.append(send(phi.at[pl.ds(1, 8)], y3r.at[slot - 2], device(way)))
    z3s[...] = jnp.where(low, phi[8], phi[1])
    third.append(send(z3s, z3r, partner))
    arrive(second)
    sources = (adj_b, x2r, y2r, 0, c2r, 0)
    gather_flow(0, *sources)
    arrive(third)
    phi[0] = z3r[...]
    phi[9] = z3r[...]
    collide_adjoint(0, sources, out, 0, True)

    share = phase_share(0)
    zcopy = send_share(share, zd4s, zd4r)
    center, group = share_sides(share, zcopy, zd4r, xd4s, xd4r, yd4s, yd4r, cd4s, cd4r)
    last = collect_share(center, group, xd4r, yd4r, cd4r)
    for k in range(7):
        out[19 + k] = out[19 + k] + last
    for copy in copies:
        copy.wait_send()


def local(populations0, populations1, cotangent):
    def vmem(*shape):
        return pltpu.VMEM(shape + (8, 128), jnp.float32)

    share = [
        vmem(4), vmem(4), vmem(2, 2), vmem(2, 2),
        vmem(8), vmem(2, 8), vmem(2), vmem(4),
    ]
    scratch = [
        pltpu.VMEM(populations0.shape, populations0.dtype),
        pltpu.VMEM(populations1.shape, populations1.dtype),
        vmem(26, 10), vmem(26, 10), vmem(2, 12), vmem(2, 6, 8), vmem(6, 8), vmem(8),
        vmem(2, 3, 10), vmem(10), vmem(2, 4, 8), vmem(11, 8), vmem(19, 8),
        vmem(10), vmem(10), vmem(2, 11), vmem(2, 11), vmem(2, 10), vmem(2, 10), vmem(4, 3), vmem(4, 3),
        vmem(6), vmem(6), vmem(2, 6), vmem(2, 6), vmem(2, 8), vmem(2, 8), vmem(4, 1), vmem(4, 1),
        *share,
        vmem(), vmem(), vmem(2), vmem(2), vmem(2, 8),
        *share,
        pltpu.SemaphoreType.DMA((48,)),
        pltpu.SemaphoreType.DMA((48,)),
        pltpu.SemaphoreType.DMA((6,)),
    ]
    return pl.pallas_call(
        kernel,
        out_shape=jax.ShapeDtypeStruct(cotangent.shape, jnp.float32),
        in_specs=[pl.BlockSpec(memory_space=pltpu.HBM)] * 3,
        out_specs=pl.BlockSpec(memory_space=pltpu.VMEM),
        scratch_shapes=scratch,
        compiler_params=pltpu.CompilerParams(
            collective_id=0, has_side_effects=True, vmem_limit_bytes=40 * 1024 * 1024
        ),
    )(populations0, populations1, cotangent)


def solution(mesh):
    spec = P(None, "gz", "gx", "gy")
    return jax.shard_map(
        local, mesh=mesh, in_specs=(spec, spec, spec), out_specs=spec, check_vma=False
    )
```

```python
import jax
import jax.numpy as jnp
import numpy as np
from jax import lax
from jax.experimental import pallas as pl
from jax.experimental.pallas import tpu as pltpu
from jax.sharding import PartitionSpec as P

VELOCITY = [
    (0, 0, 0),
    (1, 0, 0),
    (-1, 0, 0),
    (0, 1, 0),
    (0, -1, 0),
    (0, 0, 1),
    (0, 0, -1),
    (1, 1, 0),
    (-1, -1, 0),
    (1, -1, 0),
    (-1, 1, 0),
    (1, 0, 1),
    (-1, 0, -1),
    (1, 0, -1),
    (-1, 0, 1),
    (0, 1, 1),
    (0, -1, -1),
    (0, 1, -1),
    (0, -1, 1),
]
OPPOSITE = [0, 2, 1, 4, 3, 6, 5, 8, 7, 10, 9, 12, 11, 14, 13, 16, 15, 18, 17]
VELOCITY = VELOCITY + VELOCITY[:7]
OPPOSITE = OPPOSITE + [19 + mirror for mirror in OPPOSITE[:7]]
WELL = 1.2
STIFFNESS = 0.6
SHARPEN = 0.3
PHASE_RATE = 1.4
MESH = pl.DeviceIdType.MESH

RISING = [i for i in range(26) if VELOCITY[i][0] == 1]
FALLING = [i for i in range(26) if VELOCITY[i][0] == -1]
ALONG_X = {sign: [i for i in range(26) if VELOCITY[i][1] == sign] for sign in (1, -1)}
ALONG_Y = {sign: [i for i in range(26) if VELOCITY[i][2] == sign] for sign in (1, -1)}
DIAGONAL = {VELOCITY[i][1:]: i for i in range(15, 19)}
SIDES = [(-1, 0), (1, 0), (0, -1), (0, 1)]
CORNERS = [(-1, -1), (-1, 1), (1, -1), (1, 1)]
SLOT = {way: i for i, way in enumerate(SIDES)}
SLOT.update({way: i for i, way in enumerate(CORNERS)})


def kernel(
    pop0_hbm, pop1_hbm, cot_hbm, out_hbm,
    out, pop0, pop1, adj_a, adj_b, phase, grads, sens, phibar, slope, phi, flow, moments, arrive_f,
    z1s, z1r, x1s, x1r, y1s, y1r, c1s, c1r,
    z2s, z2r, x2s, x2r, y2s, y2r, c2s, c2r,
    zd2s, zd2r, xd2s, xd2r, yd2s, yd2r, cd2s, cd2r,
    z3s, z3r, x3s, x3r, y3r,
    zd4s, zd4r, xd4s, xd4r, yd4s, yd4r, cd4s, cd4r,
    send_sem, recv_sem, load_sem,
):
    gx, gy, gz = lax.axis_index("gx"), lax.axis_index("gy"), lax.axis_index("gz")
    nx, ny = lax.axis_size("gx"), lax.axis_size("gy")
    low = gz == 0
    partner = (gx, gy, 1 - gz)
    pops = (pop0, pop1)

    def load(src, dst, index):
        copy = pltpu.make_async_copy(src, dst, load_sem.at[index])
        copy.start()
        return copy

    load_phase = [
        load(pop1_hbm.at[pl.ds(19, 7)], pop1.at[pl.ds(19, 7)], 0),
        load(pop0_hbm.at[pl.ds(19, 7)], pop0.at[pl.ds(19, 7)], 1),
    ]
    load_cot = [
        load(cot_hbm.at[pl.ds(0, 13)], adj_a.at[pl.ds(0, 13), pl.ds(1, 8)], 2),
        load(cot_hbm.at[pl.ds(13, 13)], adj_a.at[pl.ds(13, 13), pl.ds(1, 8)], 3),
    ]
    load_flow = [
        load(pop0_hbm.at[pl.ds(0, 19)], pop0.at[pl.ds(0, 19)], 4),
        load(pop1_hbm.at[pl.ds(0, 19)], pop1.at[pl.ds(0, 19)], 5),
    ]

    def device(way):
        return (lax.rem(gx + way[0] + nx, nx), lax.rem(gy + way[1] + ny, ny), gz)

    barrier = pltpu.get_barrier_semaphore()
    for target in [partner] + [device(way) for way in SIDES + CORNERS]:
        pl.semaphore_signal(barrier, inc=1, device_id=target, device_id_type=MESH)

    copies = []

    def send(src, dst, target):
        index = len(copies)
        copy = pltpu.make_async_remote_copy(
            src_ref=src,
            dst_ref=dst,
            send_sem=send_sem.at[index],
            recv_sem=recv_sem.at[index],
            device_id=target,
            device_id_type=MESH,
        )
        copy.start()
        copies.append(copy)
        return copy

    def arrive(group):
        for copy in group:
            copy.wait_recv()

    row = lax.broadcasted_iota(jnp.int32, (8, 128), 0)
    lane = lax.broadcasted_iota(jnp.int32, (8, 128), 1)

    def rows_of(count):
        return lax.broadcasted_iota(jnp.int32, (count, 8, 128), 1)

    def lanes_of(count):
        return lax.broadcasted_iota(jnp.int32, (count, 8, 128), 2)

    row3, lane3 = rows_of(8), lanes_of(8)

    def roll(values, shift, axis):
        shift = shift % values.shape[axis]
        return values if shift == 0 else pltpu.roll(values, shift, axis)

    def layers(values, before, after):
        shape = values.shape[1:]
        parts = [jnp.zeros((before, *shape), jnp.float32)] if before else []
        parts.append(values)
        if after:
            parts.append(jnp.zeros((after, *shape), jnp.float32))
        return jnp.concatenate(parts, 0)

    def wide(rows):
        return jnp.broadcast_to(rows[:, None, :], (rows.shape[0], 8, 128))

    def shift(inner, outer, step, axis):
        some = inner if inner is not None else outer
        size = some.shape[axis]
        edge = 0 if step == 1 else size - 1
        at_edge = lax.broadcasted_iota(jnp.int32, some.shape, axis) == edge
        a = 0.0 if inner is None else roll(inner, step, axis)
        b = 0.0 if outer is None else roll(outer, step, axis)
        return jnp.where(at_edge, b, a), jnp.where(at_edge, a, b)

    def difference(inner, outer, axis):
        up, down = shift(inner, outer, -1, axis), shift(inner, outer, 1, axis)
        return up[0] - down[0], up[1] - down[1]

    def both_sides(inner, outer, axis):
        up, down = shift(inner, outer, -1, axis), shift(inner, outer, 1, axis)
        return up[0] + down[0], up[1] + down[1]

    def vertical_layers(adj, ref, start):
        for k in range(6):
            ref[start + k] = jnp.where(low, adj[FALLING[k], 8], adj[RISING[k], 1])

    def take_vertical(adj, ref, start):
        for k in range(6):
            layer = ref[start + k]
            adj[RISING[k], 9] = layer
            adj[FALLING[k], 0] = layer

    def edge_row(sign):
        return 0 if sign == 1 else 7

    def rows_x(adj, sign, ref, slot):
        for k, i in enumerate(ALONG_X[sign]):
            cz = VELOCITY[i][0]
            ref[slot, k] = adj[i, 1 + cz : 9 + cz, edge_row(sign), :]

    def pack_y(adj, sign, packed):
        source = 0 if sign == 1 else 127
        for k, i in enumerate(ALONG_Y[sign]):
            cz = VELOCITY[i][0]
            values = roll(adj[i, 1 + cz : 9 + cz], k - source, 2)
            packed = values if packed is None else jnp.where(lane3 == k, values, packed)
        return packed

    def well(value):
        return WELL * value * (value - 1.0) * (value - 0.5)

    def well_slope(value):
        return WELL * (3.0 * value * value - 3.0 * value + 0.5)

    def phase_gradients(which, tile, place):
        full = phase[which]
        ahead, behind = SLOT[(-1, 0)], SLOT[(1, 0)]

        def side(slot):
            near = wide(x1r[slot, tile])
            far = wide(x1r[slot, tile + 1])
            first = x1r[slot, 10, place : place + 1, :]
            last = x1r[slot, 10, place + 1 : place + 2, :]
            first = jnp.broadcast_to(first, (8, 128))[None]
            last = jnp.broadcast_to(last, (8, 128))[None]
            return first, near, far, last

        first_n, near_n, far_n, last_n = side(ahead)
        first_p, near_p, far_p, last_p = side(behind)
        x_mid = jnp.where(
            row3 < 4,
            jnp.where(row3 == 0, near_n, far_n),
            jnp.where(row3 == 7, near_p, far_p),
        )
        upper_half = row[None] < 4
        x_tile = jnp.concatenate(
            [jnp.where(upper_half, first_n, first_p), x_mid, jnp.where(upper_half, last_n, last_p)], 0
        )
        start = 6 + 2 * (1 - which)
        y_tile = jnp.where(
            lanes_of(10) < 64,
            roll(y1r[SLOT[(0, -1)] - 2], -start, 2),
            roll(y1r[SLOT[(0, 1)] - 2], 126 - start, 2),
        )
        t = 1 - which
        before_y, after_y = lane < 64, lane >= 64
        corner_n = jnp.where(before_y, c1r[SLOT[(-1, -1)], t], c1r[SLOT[(-1, 1)], t])
        corner_p = jnp.where(before_y, c1r[SLOT[(1, -1)], t], c1r[SLOT[(1, 1)], t])
        b_tile = jnp.where(row3 < 4, wide(corner_n), wide(corner_p))
        mid, y_mid = full[1:11], y_tile[1:9]
        slope[which, 0] = well_slope(mid)
        slope[which, 1] = well_slope(x_tile)
        slope[which, 2] = well_slope(y_tile)

        x_up, x_down = shift(mid, x_tile, -1, 1), shift(mid, x_tile, 1, 1)
        y_up, y_down = shift(mid, y_tile, -1, 2), shift(mid, y_tile, 1, 2)
        grads[which, 0] = 0.5 * (full[3:11] - full[1:9])
        grads[which, 1] = 0.5 * (x_up[0] - x_down[0])[1:9]
        grads[which, 2] = 0.5 * (y_up[0] - y_down[0])[1:9]
        lap = x_up[0] + x_down[0] + y_up[0] + y_down[0] + full[:10] + full[2:] - 6.0 * mid
        pot = well(mid) - STIFFNESS * lap
        pot = jnp.concatenate(
            [jnp.where(low, 0.0, pot[:1]), pot[1:9], jnp.where(low, pot[9:], 0.0)], 0
        )
        lap = (x_up[1] + x_down[1])[1:9] + both_sides(x_mid, b_tile, 2)[0]
        lap = lap + x_tile[:8] + x_tile[2:] - 6.0 * x_mid
        pot_x = well(x_mid) - STIFFNESS * lap
        lap = (y_up[1] + y_down[1])[1:9] + both_sides(y_mid, b_tile, 1)[0]
        lap = lap + y_tile[:8] + y_tile[2:] - 6.0 * y_mid
        pot_y = well(y_mid) - STIFFNESS * lap
        grads[which, 3] = 0.5 * (pot[2:] - pot[:8])
        grads[which, 4] = 0.5 * difference(pot[1:9], pot_x, 1)[0]
        grads[which, 5] = 0.5 * difference(pot[1:9], pot_y, 2)[0]

    def total(values):
        values = list(values)
        while len(values) > 1:
            values = [
                values[j] + values[j + 1] if j + 1 < len(values) else values[j]
                for j in range(0, len(values), 2)
            ]
        return values[0]

    def signed(values, weight):
        plus = [values[i] for i in range(len(values)) if weight(i) == 1]
        minus = [values[i] for i in range(len(values)) if weight(i) == -1]
        return total(plus) - total(minus)

    def part(d):
        return lambda i: VELOCITY[i][d]

    def pair(d, e):
        return lambda i: VELOCITY[i][d] * VELOCITY[i][e]

    def dot(u, v):
        return u[0] * v[0] + u[1] * v[1] + u[2] * v[2]

    def flow_moments(which):
        def layer(z, carry):
            f = [pops[which][i, z].astype(jnp.float32) for i in range(19)]
            flow[which, 0, z] = total(f)
            for d in range(3):
                flow[which, 1 + d, z] = signed(f, part(d))
            return carry

        lax.fori_loop(0, 8, layer, 0)

    def bounce(z, i, own, bounced):
        if VELOCITY[i][0] == 1:
            return jnp.where(jnp.logical_and(z == 7, jnp.logical_not(low)), bounced, own)
        if VELOCITY[i][0] == -1:
            return jnp.where(jnp.logical_and(z == 0, low), bounced, own)
        return own

    def arrived(z, i, adj, xr, yr, ystart, cr, tile):
        cz, cx, cy = VELOCITY[i]
        own = adj[i, z + (1 + cz)]
        erow = 7 if cx == 1 else 0
        elane = 127 if cy == 1 else 0
        moved = own
        if cx:
            k = ALONG_X[cx].index(i)
            got = jnp.broadcast_to(xr[SLOT[(-cx, 0)], k, pl.ds(z, 1), :], (8, 128))
            moved = jnp.where(row == erow, got, roll(own, -cx, 0))
        if cy:
            k = ALONG_Y[cy].index(i)
            got = roll(yr[SLOT[(0, -cy)] - 2, ystart + z], elane - k, 1)
            if cx:
                corner = cr[SLOT[(-cx, -cy)], tile, pl.ds(z, 1), :]
                corner = roll(jnp.broadcast_to(corner, (8, 128)), -cy, 1)
                got = jnp.where(row == erow, corner, roll(got, -cx, 0))
            moved = jnp.where(lane == elane, got, roll(moved, -cy, 1))
        return bounce(z, i, moved, adj[OPPOSITE[i], z + 1])

    PAIRS = [(0, 0), (1, 1), (2, 2), (1, 0), (2, 0), (2, 1)]

    def gather_flow(which, *sources):
        def layer(z, carry):
            a = [arrived(z, i, *sources) for i in range(19)]
            for i in range(19):
                arrive_f[i, z] = a[i]
            wa = [a[0] * (1.0 / 3.0)]
            wa += [a[i] * (1.0 / 18.0) for i in range(1, 7)]
            wa += [a[i] * (1.0 / 36.0) for i in range(7, 19)]
            moments[0, z] = total(wa)
            for d in range(3):
                moments[1 + d, z] = signed(wa, part(d))
            for n, (d, e) in enumerate(PAIRS):
                if d == e:
                    moments[4 + n, z] = total([wa[i] for i in range(19) if VELOCITY[i][d]])
                else:
                    moments[4 + n, z] = signed(wa, pair(d, e))
            moments[10, z] = total([a[i] * pops[which][i, z].astype(jnp.float32) for i in range(19)])
            return carry

        lax.fori_loop(0, 8, layer, 0)

    def collide_adjoint(which, sources, result, offset, with_phi):
        def layer(z, carry):
            def arrived_phi(i):
                cz, cx, cy = VELOCITY[i]
                own = phi[z + (1 + cz)]
                if cx:
                    erow = 7 if cx == 1 else 0
                    got = jnp.broadcast_to(x3r[SLOT[(-cx, 0)], pl.ds(z, 1), :], (8, 128))
                    own = jnp.where(row == erow, got, roll(own, -cx, 0))
                if cy:
                    elane = 127 if cy == 1 else 0
                    got = roll(y3r[SLOT[(0, -cy)] - 2, z], -cy, 1)
                    own = jnp.where(lane == elane, got, roll(own, -cy, 1))
                return bounce(z, i, own, phi[z + 1])

            g = [arrived(z, i, *sources) for i in range(19, 26)]
            if with_phi:
                g = [g[k] + arrived_phi(19 + k) for k in range(7)]
            frac = phase[which, z + 2]
            pressure = flow[which, 0, z]
            momentum = [flow[which, 1 + d, z] for d in range(3)]
            a0 = moments[0, z]
            a1 = [moments[1 + d, z] for d in range(3)]
            a2 = {}
            for n, (d, e) in enumerate(PAIRS):
                a2[d, e] = a2[e, d] = moments[4 + n, z]
            af = moments[10, z]
            b0 = 0.25 * g[0] + 0.125 * total(g[1:])
            b1 = [0.125 * (g[1 + 2 * d] - g[2 + 2 * d]) for d in range(3)]
            density = 0.2 + 0.8 * frac
            rate = 1.1 + 0.5 * frac
            half = 1.0 - 0.5 * rate
            pg = [grads[which, d, z] for d in range(3)]
            mg = [grads[which, 3 + d, z] for d in range(3)]
            force = [-frac * m for m in mg]
            inverse = 1.0 / density
            u = [(momentum[d] + 0.5 * force[d]) * inverse for d in range(3)]
            a2u = [dot([a2[d, e] for e in range(3)], u) for d in range(3)]
            a2f = [dot([a2[d, e] for e in range(3)], force) for d in range(3)]
            speed = dot(u, u)
            quad = 3.0 * dot(u, a1) + 4.5 * dot(u, a2u) - 1.5 * speed * a0
            slant = [3.0 * a1[d] - 3.0 * a0 * u[d] + 9.0 * a2u[d] for d in range(3)]
            rate_density = rate * density
            phase_pull = (4.0 * PHASE_RATE) * frac
            ubar = [
                rate_density * slant[d]
                + half * (9.0 * a2f[d] - 3.0 * a0 * force[d])
                + phase_pull * b1[d]
                for d in range(3)
            ]
            jbar = [ubar[d] * inverse for d in range(3)]
            fbar = [half * slant[d] + 0.5 * jbar[d] for d in range(3)]
            density_bar = rate * quad - dot(jbar, u)
            rate_bar = pressure * a0 + density * quad - af - 0.5 * dot(force, slant)
            imag = lax.rsqrt(dot(pg, pg) + 0.0625)
            normal = [p * imag for p in pg]
            nb1 = dot(normal, b1)
            frac_bar = (
                0.5 * rate_bar
                + 0.8 * density_bar
                - dot(mg, fbar)
                + PHASE_RATE * (b0 + 4.0 * dot(u, b1))
                + (PHASE_RATE * 4.0 * SHARPEN) * (1.0 - 2.0 * frac) * nb1
            )
            pull = (PHASE_RATE * 4.0 * SHARPEN) * frac * (1.0 - frac) * imag
            for d in range(3):
                sens[d, z] = pull * (b1[d] - normal[d] * nb1)
                sens[3 + d, z] = -frac * fbar[d]
            phibar[z] = frac_bar
            pbar = rate * a0
            keep = 1.0 - rate
            for i in range(19):
                value = keep * arrive_f[i, z] + pbar
                for d in range(3):
                    if VELOCITY[i][d] == 1:
                        value = value + jbar[d]
                    elif VELOCITY[i][d] == -1:
                        value = value - jbar[d]
                result[i, z + offset] = value
            for k in range(7):
                result[19 + k, z + offset] = (1.0 - PHASE_RATE) * g[k]
            return carry

        lax.fori_loop(0, 8, layer, 0)

    def phase_share(which):
        def spread(first):
            vz = sens[first]
            in_x, out_x = difference(sens[first + 1], None, 1)
            in_y, out_y = difference(sens[first + 2], None, 2)
            inner = layers(-0.5 * (in_x + in_y), 1, 1)
            inner = inner + 0.5 * (layers(vz, 2, 0) - layers(vz, 0, 2))
            return inner, layers(-0.5 * out_x, 1, 1), layers(-0.5 * out_y, 1, 1)

        mu, mu_x, mu_y = spread(3)
        mu = jnp.concatenate(
            [jnp.where(low, 0.0, mu[:1]), mu[1:9], jnp.where(low, mu[9:], 0.0)], 0
        )
        own, own_x, own_y = spread(0)
        in_x, out_x = both_sides(mu, mu_x, 1)
        in_y, out_y = both_sides(mu, mu_y, 2)
        over_x, corner_x = both_sides(mu_x[1:9], None, 2)
        over_y, corner_y = both_sides(mu_y[1:9], None, 1)
        inner = slope[which, 0] * mu - STIFFNESS * (in_x + in_y - 6.0 * mu) + own
        inner = inner + layers(phibar[...], 1, 1)
        inner = layers(inner, 1, 1) - STIFFNESS * (layers(mu, 2, 0) + layers(mu, 0, 2))

        def beside(scale, values, out_share, over, extra):
            vertical = layers(values[1:], 0, 1) + layers(values[:9], 1, 0)
            lap = out_share + layers(over, 1, 1) + vertical - 6.0 * values
            return scale * values - STIFFNESS * lap + extra

        side_x = beside(slope[which, 1], mu_x, out_x, over_x, own_x)
        side_y = beside(slope[which, 2], mu_y, out_y, over_y, own_y)
        return inner, side_x, side_y, -STIFFNESS * (corner_x + corner_y)

    def send_share(share, zs, zr):
        inner, side_x, side_y, _ = share
        zs[:2] = jnp.where(low, inner[10:], inner[:2])
        zs[2:3] = jnp.where(low, side_x[9:], side_x[:1])
        zs[3:4] = jnp.where(low, side_y[9:], side_y[:1])
        return send(zs, zr, partner)

    def share_sides(share, zcopy, zr, xs, xr, ys, yr, cs, cr):
        inner, side_x, side_y, corner = share
        zcopy.wait_recv()

        def merge(values, extra, count):
            lower = values[:count] + jnp.where(low, 0.0, extra)
            upper = values[8 - count :] + jnp.where(low, extra, 0.0)
            return jnp.concatenate([lower, values[count : 8 - count], upper], 0)

        group = []
        ys[...] = merge(side_y[1:9], zr[3:4], 1)
        for way in SIDES[2:]:
            slot = SLOT[way] - 2
            group.append(send(ys, yr.at[slot], device(way)))
        side_x = merge(side_x[1:9], zr[2:3], 1)
        xs[0, 0], xs[0, 1] = side_x[:, 7, :], side_x[:, 6, :]
        xs[1, 0], xs[1, 1] = side_x[:, 0, :], side_x[:, 1, :]
        cs[0], cs[1] = corner[:, 7, :], corner[:, 0, :]
        for way in CORNERS:
            group.append(send(cs.at[0 if way[0] < 0 else 1], cr.at[SLOT[way]], device(way)))
        for way in SIDES[:2]:
            slot = SLOT[way]
            group.append(send(xs.at[slot], xr.at[slot], device(way)))
        return merge(inner[2:10], zr[:2], 2), group

    def collect_share(center, group, xr, yr, cr):
        arrive(group)
        prev, after = SLOT[(1, 0)], SLOT[(-1, 0)]
        near = jnp.where(row3 < 4, wide(xr[prev, 0]), wide(xr[after, 0]))
        far = jnp.where(row3 < 4, wide(xr[prev, 1]), wide(xr[after, 1]))
        end = jnp.logical_or(row3 == 0, row3 == 7)
        next_end = jnp.logical_or(row3 == 1, row3 == 6)
        result = center + jnp.where(end, near, jnp.where(next_end, far, 0.0))
        from_y = jnp.where(lane3 < 64, yr[SLOT[(0, 1)] - 2], yr[SLOT[(0, -1)] - 2])
        result = result + jnp.where(jnp.logical_or(lane3 < 2, lane3 >= 126), from_y, 0.0)
        before = lane < 64
        ends = jnp.logical_or(lane == 0, lane == 127)
        prev_c = jnp.where(ends, jnp.where(before, cr[SLOT[(1, 1)]], cr[SLOT[(1, -1)]]), 0.0)
        next_c = jnp.where(ends, jnp.where(before, cr[SLOT[(-1, 1)]], cr[SLOT[(-1, -1)]]), 0.0)
        corners = jnp.where(row3 == 0, wide(prev_c), wide(next_c))
        return result + jnp.where(end, corners, 0.0)

    for copy in load_phase:
        copy.wait()
    for which in range(2):
        phase[which, 2:10] = total([pops[which][i].astype(jnp.float32) for i in range(19, 26)])
        z1s[2 * which : 2 * which + 2] = jnp.where(low, phase[which, 8:10], phase[which, 2:4])
    for copy in load_cot:
        copy.wait()
    vertical_layers(adj_a, z1s, 4)
    pl.semaphore_wait(barrier, 9)
    vertical = send(z1s, z1r, partner)
    for copy in load_flow:
        copy.wait()
    flow_moments(1)
    vertical.wait_recv()
    for which in range(2):
        got = z1r[2 * which : 2 * which + 2]
        phase[which, :2] = jnp.where(low, 0.0, got)
        phase[which, 10:] = jnp.where(low, got, 0.0)
    take_vertical(adj_a, z1r, 4)

    first = []
    for way in SIDES[2:]:
        slot = SLOT[way] - 2
        source = 0 if way[1] < 0 else 126
        packed = jnp.where(
            lanes_of(10) < 8,
            roll(phase[1, 1:11], 6 - source, 2),
            roll(phase[0, 1:11], 8 - source, 2),
        )
        y1s[slot, 0] = packed[0]
        y1s[slot, 9] = packed[9]
        middle = packed[1:9]
        entries = pack_y(adj_a, -way[1], None)
        y1s[slot, 1:9] = jnp.where(lane3 < 6, entries, middle)
        first.append(send(y1s.at[slot], y1r.at[slot], device(way)))
    for way in CORNERS:
        slot = SLOT[way]
        r = edge_row(-way[0])
        c1s[slot, 0] = phase[1, 2:10, r, :]
        c1s[slot, 1] = phase[0, 2:10, r, :]
        c1s[slot, 2] = adj_a[DIAGONAL[(-way[0], -way[1])], 1:9, r, :]
        first.append(send(c1s.at[slot], c1r.at[slot], device(way)))
    for way in SIDES[:2]:
        slot = SLOT[way]
        r = edge_row(-way[0])
        rows_x(adj_a, -way[0], x1s, slot)
        for n, which in enumerate((1, 0)):
            x1s[slot, 6 + 2 * n] = phase[which, 2:10, r, :]
            x1s[slot, 7 + 2 * n] = phase[which, 2:10, r + (1 if r == 0 else -1), :]
            x1s[slot, 10, 2 * n : 2 * n + 1, :] = phase[which, 1, r : r + 1, :]
            x1s[slot, 10, 2 * n + 1 : 2 * n + 2, :] = phase[which, 10, r : r + 1, :]
        x1s[slot, 10, 4:, :] = jnp.zeros((4, 128), jnp.float32)
        first.append(send(x1s.at[slot], x1r.at[slot], device(way)))
    flow_moments(0)
    arrive(first)
    sources = (adj_a, x1r, y1r, 1, c1r, 2)
    phase_gradients(1, 6, 0)
    gather_flow(1, *sources)
    collide_adjoint(1, sources, adj_b, 1, False)

    vertical_layers(adj_b, z2s, 0)
    vertical = send(z2s, z2r, partner)
    share = phase_share(1)
    zcopy = send_share(share, zd2s, zd2r)
    phase_gradients(0, 8, 2)
    center, group = share_sides(share, zcopy, zd2r, xd2s, xd2r, yd2s, yd2r, cd2s, cd2r)
    vertical.wait_recv()
    take_vertical(adj_b, z2r, 0)
    second = []
    for way in SIDES[2:]:
        slot = SLOT[way] - 2
        y2s[slot] = pack_y(adj_b, -way[1], None)
        second.append(send(y2s.at[slot], y2r.at[slot], device(way)))
    for way in CORNERS:
        slot = SLOT[way]
        c2s[slot, 0] = adj_b[DIAGONAL[(-way[0], -way[1])], 1:9, edge_row(-way[0]), :]
        second.append(send(c2s.at[slot], c2r.at[slot], device(way)))
    for way in SIDES[:2]:
        slot = SLOT[way]
        rows_x(adj_b, -way[0], x2s, slot)
        second.append(send(x2s.at[slot], x2r.at[slot], device(way)))
    phi[1:9] = collect_share(center, group, xd2r, yd2r, cd2r)
    third = []
    for way in SIDES:
        slot = SLOT[way]
        if way[0]:
            x3s[slot] = phi[1:9, edge_row(-way[0]), :]
            third.append(send(x3s.at[slot], x3r.at[slot], device(way)))
        else:
            third.append(send(phi.at[pl.ds(1, 8)], y3r.at[slot - 2], device(way)))
    z3s[...] = jnp.where(low, phi[8], phi[1])
    third.append(send(z3s, z3r, partner))
    arrive(second)
    sources = (adj_b, x2r, y2r, 0, c2r, 0)
    gather_flow(0, *sources)
    arrive(third)
    phi[0] = z3r[...]
    phi[9] = z3r[...]
    collide_adjoint(0, sources, out, 0, True)

    stores = [
        load(out.at[pl.ds(0, 10)], out_hbm.at[pl.ds(0, 10)], 6),
        load(out.at[pl.ds(10, 9)], out_hbm.at[pl.ds(10, 9)], 7),
    ]
    share = phase_share(0)
    zcopy = send_share(share, zd4s, zd4r)
    center, group = share_sides(share, zcopy, zd4r, xd4s, xd4r, yd4s, yd4r, cd4s, cd4r)
    last = collect_share(center, group, xd4r, yd4r, cd4r)
    for k in range(7):
        out[19 + k] = out[19 + k] + last
    stores.append(load(out.at[pl.ds(19, 7)], out_hbm.at[pl.ds(19, 7)], 8))
    for copy in stores:
        copy.wait()
    for copy in copies:
        copy.wait_send()


def local(populations0, populations1, cotangent):
    def vmem(*shape):
        return pltpu.VMEM(shape + (8, 128), jnp.float32)

    share = [
        vmem(4), vmem(4), vmem(2, 2), vmem(2, 2),
        vmem(8), vmem(2, 8), vmem(2), vmem(4),
    ]
    scratch = [
        vmem(26, 8),
        pltpu.VMEM(populations0.shape, populations0.dtype),
        pltpu.VMEM(populations1.shape, populations1.dtype),
        vmem(26, 10), vmem(26, 10), vmem(2, 12), vmem(2, 6, 8), vmem(6, 8), vmem(8),
        vmem(2, 3, 10), vmem(10), vmem(2, 4, 8), vmem(11, 8), vmem(19, 8),
        vmem(10), vmem(10), vmem(2, 11), vmem(2, 11), vmem(2, 10), vmem(2, 10), vmem(4, 3), vmem(4, 3),
        vmem(6), vmem(6), vmem(2, 6), vmem(2, 6), vmem(2, 8), vmem(2, 8), vmem(4, 1), vmem(4, 1),
        *share,
        vmem(), vmem(), vmem(2), vmem(2), vmem(2, 8),
        *share,
        pltpu.SemaphoreType.DMA((48,)),
        pltpu.SemaphoreType.DMA((48,)),
        pltpu.SemaphoreType.DMA((9,)),
    ]
    return pl.pallas_call(
        kernel,
        out_shape=jax.ShapeDtypeStruct(cotangent.shape, jnp.float32),
        in_specs=[pl.BlockSpec(memory_space=pltpu.HBM)] * 3,
        out_specs=pl.BlockSpec(memory_space=pltpu.HBM),
        scratch_shapes=scratch,
        compiler_params=pltpu.CompilerParams(
            collective_id=0, has_side_effects=True, vmem_limit_bytes=60 * 1024 * 1024
        ),
    )(populations0, populations1, cotangent)


def solution(mesh):
    spec = P(None, "gz", "gx", "gy")
    return jax.shard_map(
        local, mesh=mesh, in_specs=(spec, spec, spec), out_specs=spec, check_vma=False
    )
```

```python
import jax
import jax.numpy as jnp
import numpy as np
from jax import lax
from jax.experimental import pallas as pl
from jax.experimental.pallas import tpu as pltpu
from jax.sharding import PartitionSpec as P

VELOCITY = [
    (0, 0, 0),
    (1, 0, 0),
    (-1, 0, 0),
    (0, 1, 0),
    (0, -1, 0),
    (0, 0, 1),
    (0, 0, -1),
    (1, 1, 0),
    (-1, -1, 0),
    (1, -1, 0),
    (-1, 1, 0),
    (1, 0, 1),
    (-1, 0, -1),
    (1, 0, -1),
    (-1, 0, 1),
    (0, 1, 1),
    (0, -1, -1),
    (0, 1, -1),
    (0, -1, 1),
]
OPPOSITE = [0, 2, 1, 4, 3, 6, 5, 8, 7, 10, 9, 12, 11, 14, 13, 16, 15, 18, 17]
VELOCITY = VELOCITY + VELOCITY[:7]
OPPOSITE = OPPOSITE + [19 + mirror for mirror in OPPOSITE[:7]]
WELL = 1.2
STIFFNESS = 0.6
SHARPEN = 0.3
PHASE_RATE = 1.4
MESH = pl.DeviceIdType.MESH

RISING = [i for i in range(26) if VELOCITY[i][0] == 1]
FALLING = [i for i in range(26) if VELOCITY[i][0] == -1]
ALONG_X = {sign: [i for i in range(26) if VELOCITY[i][1] == sign] for sign in (1, -1)}
ALONG_Y = {sign: [i for i in range(26) if VELOCITY[i][2] == sign] for sign in (1, -1)}
DIAGONAL = {VELOCITY[i][1:]: i for i in range(15, 19)}
SIDES = [(-1, 0), (1, 0), (0, -1), (0, 1)]
CORNERS = [(-1, -1), (-1, 1), (1, -1), (1, 1)]
SLOT = {way: i for i, way in enumerate(SIDES)}
SLOT.update({way: i for i, way in enumerate(CORNERS)})


def kernel(
    pop0_hbm, pop1_hbm, cot_hbm, out_hbm,
    out, pop0, pop1, adj_a, adj_b, phase, grads, sens, phibar, slope, phi, flow, moments, arrive_f,
    z1s, z1r, x1s, x1r, y1s, y1r, c1s, c1r,
    z2s, z2r, x2s, x2r, y2s, y2r, c2s, c2r,
    zd2s, zd2r, xd2s, xd2r, yd2s, yd2r, cd2s, cd2r,
    z3s, z3r, x3s, x3r, y3r,
    zd4s, zd4r, xd4s, xd4r, yd4s, yd4r, cd4s, cd4r,
    send_sem, recv_sem, load_sem,
):
    gx, gy, gz = lax.axis_index("gx"), lax.axis_index("gy"), lax.axis_index("gz")
    nx, ny = lax.axis_size("gx"), lax.axis_size("gy")
    low = gz == 0
    partner = (gx, gy, 1 - gz)
    pops = (pop0, pop1)

    def load(src, dst, index):
        copy = pltpu.make_async_copy(src, dst, load_sem.at[index])
        copy.start()
        return copy

    load_phase = [
        load(pop1_hbm.at[pl.ds(19, 7)], pop1.at[pl.ds(19, 7)], 0),
        load(pop0_hbm.at[pl.ds(19, 7)], pop0.at[pl.ds(19, 7)], 1),
    ]
    load_cot = [
        load(cot_hbm.at[pl.ds(0, 13)], adj_a.at[pl.ds(0, 13), pl.ds(1, 8)], 2),
        load(cot_hbm.at[pl.ds(13, 13)], adj_a.at[pl.ds(13, 13), pl.ds(1, 8)], 3),
    ]
    load_flow = [
        load(pop0_hbm.at[pl.ds(0, 19)], pop0.at[pl.ds(0, 19)], 4),
        load(pop1_hbm.at[pl.ds(0, 19)], pop1.at[pl.ds(0, 19)], 5),
    ]

    def device(way):
        return (lax.rem(gx + way[0] + nx, nx), lax.rem(gy + way[1] + ny, ny), gz)

    barrier = pltpu.get_barrier_semaphore()
    for target in [partner] + [device(way) for way in SIDES + CORNERS]:
        pl.semaphore_signal(barrier, inc=1, device_id=target, device_id_type=MESH)

    copies = []

    def send(src, dst, target):
        index = len(copies)
        copy = pltpu.make_async_remote_copy(
            src_ref=src,
            dst_ref=dst,
            send_sem=send_sem.at[index],
            recv_sem=recv_sem.at[index],
            device_id=target,
            device_id_type=MESH,
        )
        copy.start()
        copies.append(copy)
        return copy

    def arrive(group):
        for copy in group:
            copy.wait_recv()

    row = lax.broadcasted_iota(jnp.int32, (8, 128), 0)
    lane = lax.broadcasted_iota(jnp.int32, (8, 128), 1)

    def rows_of(count):
        return lax.broadcasted_iota(jnp.int32, (count, 8, 128), 1)

    def lanes_of(count):
        return lax.broadcasted_iota(jnp.int32, (count, 8, 128), 2)

    row3, lane3 = rows_of(8), lanes_of(8)

    def roll(values, shift, axis):
        shift = shift % values.shape[axis]
        return values if shift == 0 else pltpu.roll(values, shift, axis)

    def layers(values, before, after):
        shape = values.shape[1:]
        parts = [jnp.zeros((before, *shape), jnp.float32)] if before else []
        parts.append(values)
        if after:
            parts.append(jnp.zeros((after, *shape), jnp.float32))
        return jnp.concatenate(parts, 0)

    def wide(rows):
        return jnp.broadcast_to(rows[:, None, :], (rows.shape[0], 8, 128))

    def shift(inner, outer, step, axis):
        some = inner if inner is not None else outer
        size = some.shape[axis]
        edge = 0 if step == 1 else size - 1
        at_edge = lax.broadcasted_iota(jnp.int32, some.shape, axis) == edge
        a = 0.0 if inner is None else roll(inner, step, axis)
        b = 0.0 if outer is None else roll(outer, step, axis)
        return jnp.where(at_edge, b, a), jnp.where(at_edge, a, b)

    def difference(inner, outer, axis):
        up, down = shift(inner, outer, -1, axis), shift(inner, outer, 1, axis)
        return up[0] - down[0], up[1] - down[1]

    def both_sides(inner, outer, axis):
        up, down = shift(inner, outer, -1, axis), shift(inner, outer, 1, axis)
        return up[0] + down[0], up[1] + down[1]

    def vertical_layers(adj, ref, start):
        for k in range(6):
            ref[start + k] = jnp.where(low, adj[FALLING[k], 8], adj[RISING[k], 1])

    def take_vertical(adj, ref, start):
        for k in range(6):
            layer = ref[start + k]
            adj[RISING[k], 9] = layer
            adj[FALLING[k], 0] = layer

    def edge_row(sign):
        return 0 if sign == 1 else 7

    def rows_x(adj, sign, ref, slot):
        for k, i in enumerate(ALONG_X[sign]):
            cz = VELOCITY[i][0]
            ref[slot, k] = adj[i, 1 + cz : 9 + cz, edge_row(sign), :]

    def pack_y(adj, sign, packed):
        source = 0 if sign == 1 else 127
        for k, i in enumerate(ALONG_Y[sign]):
            cz = VELOCITY[i][0]
            values = roll(adj[i, 1 + cz : 9 + cz], k - source, 2)
            packed = values if packed is None else jnp.where(lane3 == k, values, packed)
        return packed

    def well(value):
        return WELL * value * (value - 1.0) * (value - 0.5)

    def well_slope(value):
        return WELL * (3.0 * value * value - 3.0 * value + 0.5)

    def phase_gradients(which, tile, place):
        full = phase[which]
        ahead, behind = SLOT[(-1, 0)], SLOT[(1, 0)]

        def side(slot):
            near = wide(x1r[slot, tile])
            far = wide(x1r[slot, tile + 1])
            first = x1r[slot, 10, place : place + 1, :]
            last = x1r[slot, 10, place + 1 : place + 2, :]
            first = jnp.broadcast_to(first, (8, 128))[None]
            last = jnp.broadcast_to(last, (8, 128))[None]
            return first, near, far, last

        first_n, near_n, far_n, last_n = side(ahead)
        first_p, near_p, far_p, last_p = side(behind)
        x_mid = jnp.where(
            row3 < 4,
            jnp.where(row3 == 0, near_n, far_n),
            jnp.where(row3 == 7, near_p, far_p),
        )
        upper_half = row[None] < 4
        x_tile = jnp.concatenate(
            [jnp.where(upper_half, first_n, first_p), x_mid, jnp.where(upper_half, last_n, last_p)], 0
        )
        start = 6 + 2 * (1 - which)
        y_tile = jnp.where(
            lanes_of(10) < 64,
            roll(y1r[SLOT[(0, -1)] - 2], -start, 2),
            roll(y1r[SLOT[(0, 1)] - 2], 126 - start, 2),
        )
        t = 1 - which
        before_y, after_y = lane < 64, lane >= 64
        corner_n = jnp.where(before_y, c1r[SLOT[(-1, -1)], t], c1r[SLOT[(-1, 1)], t])
        corner_p = jnp.where(before_y, c1r[SLOT[(1, -1)], t], c1r[SLOT[(1, 1)], t])
        b_tile = jnp.where(row3 < 4, wide(corner_n), wide(corner_p))
        mid, y_mid = full[1:11], y_tile[1:9]
        slope[which, 0] = well_slope(mid)
        slope[which, 1] = well_slope(x_tile)
        slope[which, 2] = well_slope(y_tile)

        x_up, x_down = shift(mid, x_tile, -1, 1), shift(mid, x_tile, 1, 1)
        y_up, y_down = shift(mid, y_tile, -1, 2), shift(mid, y_tile, 1, 2)
        grads[which, 0] = 0.5 * (full[3:11] - full[1:9])
        grads[which, 1] = 0.5 * (x_up[0] - x_down[0])[1:9]
        grads[which, 2] = 0.5 * (y_up[0] - y_down[0])[1:9]
        lap = x_up[0] + x_down[0] + y_up[0] + y_down[0] + full[:10] + full[2:] - 6.0 * mid
        pot = well(mid) - STIFFNESS * lap
        pot = jnp.concatenate(
            [jnp.where(low, 0.0, pot[:1]), pot[1:9], jnp.where(low, pot[9:], 0.0)], 0
        )
        lap = (x_up[1] + x_down[1])[1:9] + both_sides(x_mid, b_tile, 2)[0]
        lap = lap + x_tile[:8] + x_tile[2:] - 6.0 * x_mid
        pot_x = well(x_mid) - STIFFNESS * lap
        lap = (y_up[1] + y_down[1])[1:9] + both_sides(y_mid, b_tile, 1)[0]
        lap = lap + y_tile[:8] + y_tile[2:] - 6.0 * y_mid
        pot_y = well(y_mid) - STIFFNESS * lap
        grads[which, 3] = 0.5 * (pot[2:] - pot[:8])
        grads[which, 4] = 0.5 * difference(pot[1:9], pot_x, 1)[0]
        grads[which, 5] = 0.5 * difference(pot[1:9], pot_y, 2)[0]

    def total(values):
        values = list(values)
        while len(values) > 1:
            values = [
                values[j] + values[j + 1] if j + 1 < len(values) else values[j]
                for j in range(0, len(values), 2)
            ]
        return values[0]

    def signed(values, weight):
        plus = [values[i] for i in range(len(values)) if weight(i) == 1]
        minus = [values[i] for i in range(len(values)) if weight(i) == -1]
        return total(plus) - total(minus)

    def part(d):
        return lambda i: VELOCITY[i][d]

    def pair(d, e):
        return lambda i: VELOCITY[i][d] * VELOCITY[i][e]

    def dot(u, v):
        return u[0] * v[0] + u[1] * v[1] + u[2] * v[2]

    def flow_moments(which):
        def layer(z, carry):
            f = [pops[which][i, z].astype(jnp.float32) for i in range(19)]
            flow[which, 0, z] = total(f)
            for d in range(3):
                flow[which, 1 + d, z] = signed(f, part(d))
            return carry

        lax.fori_loop(0, 8, layer, 0)

    def bounce(z, i, own, bounced):
        if VELOCITY[i][0] == 1:
            return jnp.where(jnp.logical_and(z == 7, jnp.logical_not(low)), bounced, own)
        if VELOCITY[i][0] == -1:
            return jnp.where(jnp.logical_and(z == 0, low), bounced, own)
        return own

    def arrived(z, i, adj, xr, yr, ystart, cr, tile):
        cz, cx, cy = VELOCITY[i]
        own = adj[i, z + (1 + cz)]
        erow = 7 if cx == 1 else 0
        elane = 127 if cy == 1 else 0
        moved = own
        if cx:
            k = ALONG_X[cx].index(i)
            got = jnp.broadcast_to(xr[SLOT[(-cx, 0)], k, pl.ds(z, 1), :], (8, 128))
            moved = jnp.where(row == erow, got, roll(own, -cx, 0))
        if cy:
            k = ALONG_Y[cy].index(i)
            got = roll(yr[SLOT[(0, -cy)] - 2, ystart + z], elane - k, 1)
            if cx:
                corner = cr[SLOT[(-cx, -cy)], tile, pl.ds(z, 1), :]
                corner = roll(jnp.broadcast_to(corner, (8, 128)), -cy, 1)
                got = jnp.where(row == erow, corner, roll(got, -cx, 0))
            moved = jnp.where(lane == elane, got, roll(moved, -cy, 1))
        return bounce(z, i, moved, adj[OPPOSITE[i], z + 1])

    PAIRS = [(0, 0), (1, 1), (2, 2), (1, 0), (2, 0), (2, 1)]

    def gather_flow(which, *sources):
        def layer(z, carry):
            a = [arrived(z, i, *sources) for i in range(19)]
            for i in range(19):
                arrive_f[i, z] = a[i]
            wa = [a[0] * (1.0 / 3.0)]
            wa += [a[i] * (1.0 / 18.0) for i in range(1, 7)]
            wa += [a[i] * (1.0 / 36.0) for i in range(7, 19)]
            moments[0, z] = total(wa)
            for d in range(3):
                moments[1 + d, z] = signed(wa, part(d))
            for n, (d, e) in enumerate(PAIRS):
                if d == e:
                    moments[4 + n, z] = total([wa[i] for i in range(19) if VELOCITY[i][d]])
                else:
                    moments[4 + n, z] = signed(wa, pair(d, e))
            moments[10, z] = total([a[i] * pops[which][i, z].astype(jnp.float32) for i in range(19)])
            return carry

        lax.fori_loop(0, 8, layer, 0)

    def collide_adjoint(which, sources, result, offset, with_phi):
        def layer(z, carry):
            def arrived_phi(i):
                cz, cx, cy = VELOCITY[i]
                own = phi[z + (1 + cz)]
                if cx:
                    erow = 7 if cx == 1 else 0
                    got = jnp.broadcast_to(x3r[SLOT[(-cx, 0)], pl.ds(z, 1), :], (8, 128))
                    own = jnp.where(row == erow, got, roll(own, -cx, 0))
                if cy:
                    elane = 127 if cy == 1 else 0
                    got = roll(y3r[SLOT[(0, -cy)] - 2, z], -cy, 1)
                    own = jnp.where(lane == elane, got, roll(own, -cy, 1))
                return bounce(z, i, own, phi[z + 1])

            g = [arrived(z, i, *sources) for i in range(19, 26)]
            if with_phi:
                g = [g[k] + arrived_phi(19 + k) for k in range(7)]
            frac = phase[which, z + 2]
            pressure = flow[which, 0, z]
            momentum = [flow[which, 1 + d, z] for d in range(3)]
            a0 = moments[0, z]
            a1 = [moments[1 + d, z] for d in range(3)]
            a2 = {}
            for n, (d, e) in enumerate(PAIRS):
                a2[d, e] = a2[e, d] = moments[4 + n, z]
            af = moments[10, z]
            b0 = 0.25 * g[0] + 0.125 * total(g[1:])
            b1 = [0.125 * (g[1 + 2 * d] - g[2 + 2 * d]) for d in range(3)]
            density = 0.2 + 0.8 * frac
            rate = 1.1 + 0.5 * frac
            half = 1.0 - 0.5 * rate
            pg = [grads[which, d, z] for d in range(3)]
            mg = [grads[which, 3 + d, z] for d in range(3)]
            force = [-frac * m for m in mg]
            inverse = 1.0 / density
            u = [(momentum[d] + 0.5 * force[d]) * inverse for d in range(3)]
            a2u = [dot([a2[d, e] for e in range(3)], u) for d in range(3)]
            a2f = [dot([a2[d, e] for e in range(3)], force) for d in range(3)]
            speed = dot(u, u)
            quad = 3.0 * dot(u, a1) + 4.5 * dot(u, a2u) - 1.5 * speed * a0
            slant = [3.0 * a1[d] - 3.0 * a0 * u[d] + 9.0 * a2u[d] for d in range(3)]
            rate_density = rate * density
            phase_pull = (4.0 * PHASE_RATE) * frac
            ubar = [
                rate_density * slant[d]
                + half * (9.0 * a2f[d] - 3.0 * a0 * force[d])
                + phase_pull * b1[d]
                for d in range(3)
            ]
            jbar = [ubar[d] * inverse for d in range(3)]
            fbar = [half * slant[d] + 0.5 * jbar[d] for d in range(3)]
            density_bar = rate * quad - dot(jbar, u)
            rate_bar = pressure * a0 + density * quad - af - 0.5 * dot(force, slant)
            imag = lax.rsqrt(dot(pg, pg) + 0.0625)
            normal = [p * imag for p in pg]
            nb1 = dot(normal, b1)
            frac_bar = (
                0.5 * rate_bar
                + 0.8 * density_bar
                - dot(mg, fbar)
                + PHASE_RATE * (b0 + 4.0 * dot(u, b1))
                + (PHASE_RATE * 4.0 * SHARPEN) * (1.0 - 2.0 * frac) * nb1
            )
            pull = (PHASE_RATE * 4.0 * SHARPEN) * frac * (1.0 - frac) * imag
            for d in range(3):
                sens[d, z] = pull * (b1[d] - normal[d] * nb1)
                sens[3 + d, z] = -frac * fbar[d]
            phibar[z] = frac_bar
            pbar = rate * a0
            keep = 1.0 - rate
            for i in range(19):
                value = keep * arrive_f[i, z] + pbar
                for d in range(3):
                    if VELOCITY[i][d] == 1:
                        value = value + jbar[d]
                    elif VELOCITY[i][d] == -1:
                        value = value - jbar[d]
                result[i, z + offset] = value
            for k in range(7):
                result[19 + k, z + offset] = (1.0 - PHASE_RATE) * g[k]
            return carry

        lax.fori_loop(0, 8, layer, 0)

    def phase_share(which):
        def spread(first):
            vz = sens[first]
            in_x, out_x = difference(sens[first + 1], None, 1)
            in_y, out_y = difference(sens[first + 2], None, 2)
            inner = layers(-0.5 * (in_x + in_y), 1, 1)
            inner = inner + 0.5 * (layers(vz, 2, 0) - layers(vz, 0, 2))
            return inner, layers(-0.5 * out_x, 1, 1), layers(-0.5 * out_y, 1, 1)

        mu, mu_x, mu_y = spread(3)
        mu = jnp.concatenate(
            [jnp.where(low, 0.0, mu[:1]), mu[1:9], jnp.where(low, mu[9:], 0.0)], 0
        )
        own, own_x, own_y = spread(0)
        in_x, out_x = both_sides(mu, mu_x, 1)
        in_y, out_y = both_sides(mu, mu_y, 2)
        over_x, corner_x = both_sides(mu_x[1:9], None, 2)
        over_y, corner_y = both_sides(mu_y[1:9], None, 1)
        inner = slope[which, 0] * mu - STIFFNESS * (in_x + in_y - 6.0 * mu) + own
        inner = inner + layers(phibar[...], 1, 1)
        inner = layers(inner, 1, 1) - STIFFNESS * (layers(mu, 2, 0) + layers(mu, 0, 2))

        def beside(scale, values, out_share, over, extra):
            vertical = layers(values[1:], 0, 1) + layers(values[:9], 1, 0)
            lap = out_share + layers(over, 1, 1) + vertical - 6.0 * values
            return scale * values - STIFFNESS * lap + extra

        side_x = beside(slope[which, 1], mu_x, out_x, over_x, own_x)
        side_y = beside(slope[which, 2], mu_y, out_y, over_y, own_y)
        return inner, side_x, side_y, -STIFFNESS * (corner_x + corner_y)

    def send_share(share, zs, zr):
        inner, side_x, side_y, _ = share
        zs[:2] = jnp.where(low, inner[10:], inner[:2])
        zs[2:3] = jnp.where(low, side_x[9:], side_x[:1])
        zs[3:4] = jnp.where(low, side_y[9:], side_y[:1])
        return send(zs, zr, partner)

    def share_sides(share, zcopy, zr, xs, xr, ys, yr, cs, cr):
        inner, side_x, side_y, corner = share
        zcopy.wait_recv()

        def merge(values, extra, count):
            lower = values[:count] + jnp.where(low, 0.0, extra)
            upper = values[8 - count :] + jnp.where(low, extra, 0.0)
            return jnp.concatenate([lower, values[count : 8 - count], upper], 0)

        group = []
        ys[...] = merge(side_y[1:9], zr[3:4], 1)
        for way in SIDES[2:]:
            slot = SLOT[way] - 2
            group.append(send(ys, yr.at[slot], device(way)))
        side_x = merge(side_x[1:9], zr[2:3], 1)
        xs[0, 0], xs[0, 1] = side_x[:, 7, :], side_x[:, 6, :]
        xs[1, 0], xs[1, 1] = side_x[:, 0, :], side_x[:, 1, :]
        cs[0], cs[1] = corner[:, 7, :], corner[:, 0, :]
        for way in CORNERS:
            group.append(send(cs.at[0 if way[0] < 0 else 1], cr.at[SLOT[way]], device(way)))
        for way in SIDES[:2]:
            slot = SLOT[way]
            group.append(send(xs.at[slot], xr.at[slot], device(way)))
        return merge(inner[2:10], zr[:2], 2), group

    def collect_share(center, group, xr, yr, cr):
        arrive(group)
        prev, after = SLOT[(1, 0)], SLOT[(-1, 0)]
        near = jnp.where(row3 < 4, wide(xr[prev, 0]), wide(xr[after, 0]))
        far = jnp.where(row3 < 4, wide(xr[prev, 1]), wide(xr[after, 1]))
        end = jnp.logical_or(row3 == 0, row3 == 7)
        next_end = jnp.logical_or(row3 == 1, row3 == 6)
        result = center + jnp.where(end, near, jnp.where(next_end, far, 0.0))
        from_y = jnp.where(lane3 < 64, yr[SLOT[(0, 1)] - 2], yr[SLOT[(0, -1)] - 2])
        result = result + jnp.where(jnp.logical_or(lane3 < 2, lane3 >= 126), from_y, 0.0)
        before = lane < 64
        ends = jnp.logical_or(lane == 0, lane == 127)
        prev_c = jnp.where(ends, jnp.where(before, cr[SLOT[(1, 1)]], cr[SLOT[(1, -1)]]), 0.0)
        next_c = jnp.where(ends, jnp.where(before, cr[SLOT[(-1, 1)]], cr[SLOT[(-1, -1)]]), 0.0)
        corners = jnp.where(row3 == 0, wide(prev_c), wide(next_c))
        return result + jnp.where(end, corners, 0.0)

    for copy in load_phase:
        copy.wait()
    for which in range(2):
        phase[which, 2:10] = total([pops[which][i].astype(jnp.float32) for i in range(19, 26)])
        z1s[2 * which : 2 * which + 2] = jnp.where(low, phase[which, 8:10], phase[which, 2:4])
    for copy in load_cot:
        copy.wait()
    vertical_layers(adj_a, z1s, 4)
    pl.semaphore_wait(barrier, 9)
    vertical = send(z1s, z1r, partner)
    for copy in load_flow:
        copy.wait()
    flow_moments(1)
    vertical.wait_recv()
    for which in range(2):
        got = z1r[2 * which : 2 * which + 2]
        phase[which, :2] = jnp.where(low, 0.0, got)
        phase[which, 10:] = jnp.where(low, got, 0.0)
    take_vertical(adj_a, z1r, 4)

    first = []
    for way in SIDES[2:]:
        slot = SLOT[way] - 2
        source = 0 if way[1] < 0 else 126
        packed = jnp.where(
            lanes_of(10) < 8,
            roll(phase[1, 1:11], 6 - source, 2),
            roll(phase[0, 1:11], 8 - source, 2),
        )
        y1s[slot, 0] = packed[0]
        y1s[slot, 9] = packed[9]
        middle = packed[1:9]
        entries = pack_y(adj_a, -way[1], None)
        y1s[slot, 1:9] = jnp.where(lane3 < 6, entries, middle)
        first.append(send(y1s.at[slot], y1r.at[slot], device(way)))
    for way in CORNERS:
        slot = SLOT[way]
        r = edge_row(-way[0])
        c1s[slot, 0] = phase[1, 2:10, r, :]
        c1s[slot, 1] = phase[0, 2:10, r, :]
        c1s[slot, 2] = adj_a[DIAGONAL[(-way[0], -way[1])], 1:9, r, :]
        first.append(send(c1s.at[slot], c1r.at[slot], device(way)))
    for way in SIDES[:2]:
        slot = SLOT[way]
        r = edge_row(-way[0])
        rows_x(adj_a, -way[0], x1s, slot)
        for n, which in enumerate((1, 0)):
            x1s[slot, 6 + 2 * n] = phase[which, 2:10, r, :]
            x1s[slot, 7 + 2 * n] = phase[which, 2:10, r + (1 if r == 0 else -1), :]
            x1s[slot, 10, 2 * n : 2 * n + 1, :] = phase[which, 1, r : r + 1, :]
            x1s[slot, 10, 2 * n + 1 : 2 * n + 2, :] = phase[which, 10, r : r + 1, :]
        x1s[slot, 10, 4:, :] = jnp.zeros((4, 128), jnp.float32)
        first.append(send(x1s.at[slot], x1r.at[slot], device(way)))
    flow_moments(0)
    arrive(first)
    sources = (adj_a, x1r, y1r, 1, c1r, 2)
    phase_gradients(1, 6, 0)
    gather_flow(1, *sources)
    collide_adjoint(1, sources, adj_b, 1, False)

    vertical_layers(adj_b, z2s, 0)
    vertical = send(z2s, z2r, partner)
    share = phase_share(1)
    zcopy = send_share(share, zd2s, zd2r)
    phase_gradients(0, 8, 2)
    center, group = share_sides(share, zcopy, zd2r, xd2s, xd2r, yd2s, yd2r, cd2s, cd2r)
    vertical.wait_recv()
    take_vertical(adj_b, z2r, 0)
    second = []
    for way in SIDES[2:]:
        slot = SLOT[way] - 2
        y2s[slot] = pack_y(adj_b, -way[1], None)
        second.append(send(y2s.at[slot], y2r.at[slot], device(way)))
    for way in CORNERS:
        slot = SLOT[way]
        c2s[slot, 0] = adj_b[DIAGONAL[(-way[0], -way[1])], 1:9, edge_row(-way[0]), :]
        second.append(send(c2s.at[slot], c2r.at[slot], device(way)))
    for way in SIDES[:2]:
        slot = SLOT[way]
        rows_x(adj_b, -way[0], x2s, slot)
        second.append(send(x2s.at[slot], x2r.at[slot], device(way)))
    phi[1:9] = collect_share(center, group, xd2r, yd2r, cd2r)
    third = []
    for way in SIDES:
        slot = SLOT[way]
        if way[0]:
            x3s[slot] = phi[1:9, edge_row(-way[0]), :]
            third.append(send(x3s.at[slot], x3r.at[slot], device(way)))
        else:
            third.append(send(phi.at[pl.ds(1, 8)], y3r.at[slot - 2], device(way)))
    z3s[...] = jnp.where(low, phi[8], phi[1])
    third.append(send(z3s, z3r, partner))
    arrive(second)
    sources = (adj_b, x2r, y2r, 0, c2r, 0)
    gather_flow(0, *sources)
    arrive(third)
    phi[0] = z3r[...]
    phi[9] = z3r[...]
    collide_adjoint(0, sources, out, 0, True)

    stores = [
        load(out.at[pl.ds(0, 10)], out_hbm.at[pl.ds(0, 10)], 6),
        load(out.at[pl.ds(10, 9)], out_hbm.at[pl.ds(10, 9)], 7),
    ]
    share = phase_share(0)
    zcopy = send_share(share, zd4s, zd4r)
    center, group = share_sides(share, zcopy, zd4r, xd4s, xd4r, yd4s, yd4r, cd4s, cd4r)
    last = collect_share(center, group, xd4r, yd4r, cd4r)
    for k in range(7):
        out[19 + k] = out[19 + k] + last
    stores.append(load(out.at[pl.ds(19, 7)], out_hbm.at[pl.ds(19, 7)], 8))
    for copy in stores:
        copy.wait()
    for copy in copies:
        copy.wait_send()


def local(populations0, populations1, cotangent):
    def vmem(*shape):
        return pltpu.VMEM(shape + (8, 128), jnp.float32)

    share = [
        vmem(4), vmem(4), vmem(2, 2), vmem(2, 2),
        vmem(8), vmem(2, 8), vmem(2), vmem(4),
    ]
    scratch = [
        vmem(26, 8),
        pltpu.VMEM(populations0.shape, populations0.dtype),
        pltpu.VMEM(populations1.shape, populations1.dtype),
        vmem(26, 10), vmem(26, 10), vmem(2, 12), vmem(2, 6, 8), vmem(6, 8), vmem(8),
        vmem(2, 3, 10), vmem(10), vmem(2, 4, 8), vmem(11, 8), vmem(19, 8),
        vmem(10), vmem(10), vmem(2, 11), vmem(2, 11), vmem(2, 10), vmem(2, 10), vmem(4, 3), vmem(4, 3),
        vmem(6), vmem(6), vmem(2, 6), vmem(2, 6), vmem(2, 8), vmem(2, 8), vmem(4, 1), vmem(4, 1),
        *share,
        vmem(), vmem(), vmem(2), vmem(2), vmem(2, 8),
        *share,
        pltpu.SemaphoreType.DMA((48,)),
        pltpu.SemaphoreType.DMA((48,)),
        pltpu.SemaphoreType.DMA((9,)),
    ]
    operands = [
        pltpu.with_memory_space_constraint(operand, pltpu.HBM)
        for operand in (populations0, populations1, cotangent)
    ]
    return pl.pallas_call(
        kernel,
        out_shape=jax.ShapeDtypeStruct(cotangent.shape, jnp.float32),
        in_specs=[pl.BlockSpec(memory_space=pltpu.HBM)] * 3,
        out_specs=pl.BlockSpec(memory_space=pl.ANY),
        scratch_shapes=scratch,
        compiler_params=pltpu.CompilerParams(
            collective_id=0, has_side_effects=True, vmem_limit_bytes=40 * 1024 * 1024
        ),
    )(*operands)


def solution(mesh):
    spec = P(None, "gz", "gx", "gy")
    return jax.shard_map(
        local, mesh=mesh, in_specs=(spec, spec, spec), out_specs=spec, check_vma=False
    )
```

```python
import jax
import jax.numpy as jnp
import numpy as np
from jax import lax
from jax.experimental import pallas as pl
from jax.experimental.pallas import tpu as pltpu
from jax.sharding import PartitionSpec as P

VELOCITY = [
    (0, 0, 0),
    (1, 0, 0),
    (-1, 0, 0),
    (0, 1, 0),
    (0, -1, 0),
    (0, 0, 1),
    (0, 0, -1),
    (1, 1, 0),
    (-1, -1, 0),
    (1, -1, 0),
    (-1, 1, 0),
    (1, 0, 1),
    (-1, 0, -1),
    (1, 0, -1),
    (-1, 0, 1),
    (0, 1, 1),
    (0, -1, -1),
    (0, 1, -1),
    (0, -1, 1),
]
OPPOSITE = [0, 2, 1, 4, 3, 6, 5, 8, 7, 10, 9, 12, 11, 14, 13, 16, 15, 18, 17]
VELOCITY = VELOCITY + VELOCITY[:7]
OPPOSITE = OPPOSITE + [19 + mirror for mirror in OPPOSITE[:7]]
WELL = 1.2
STIFFNESS = 0.6
SHARPEN = 0.3
PHASE_RATE = 1.4
MESH = pl.DeviceIdType.MESH

RISING = [i for i in range(26) if VELOCITY[i][0] == 1]
FALLING = [i for i in range(26) if VELOCITY[i][0] == -1]
ALONG_X = {sign: [i for i in range(26) if VELOCITY[i][1] == sign] for sign in (1, -1)}
ALONG_Y = {sign: [i for i in range(26) if VELOCITY[i][2] == sign] for sign in (1, -1)}
DIAGONAL = {VELOCITY[i][1:]: i for i in range(15, 19)}
SIDES = [(-1, 0), (1, 0), (0, -1), (0, 1)]
CORNERS = [(-1, -1), (-1, 1), (1, -1), (1, 1)]
SLOT = {way: i for i, way in enumerate(SIDES)}
SLOT.update({way: i for i, way in enumerate(CORNERS)})


def kernel(
    pop0_hbm, pop1_hbm, cot_hbm, out_hbm,
    out, pop0, pop1, adj_a, adj_b, phase, grads, sens, phibar, slope, phi, flow, moments, arrive_f,
    z1s, z1r, x1s, x1r, y1s, y1r, c1s, c1r,
    z2s, z2r, x2s, x2r, y2s, y2r, c2s, c2r,
    zx1s, zx1r, zy1s, zy1r,
    zd2s, zd2r, zs2s, zs2r, xd2s, xd2r, yd2s, yd2r, cd2s, cd2r,
    z3s, z3r, x3s, x3r, y3r,
    zd4s, zd4r, zs4s, zs4r, xd4s, xd4r, yd4s, yd4r, cd4s, cd4r,
    send_sem, recv_sem, load_sem,
):
    gx, gy, gz = lax.axis_index("gx"), lax.axis_index("gy"), lax.axis_index("gz")
    nx, ny = lax.axis_size("gx"), lax.axis_size("gy")
    low = gz == 0
    partner = (gx, gy, 1 - gz)
    pops = (pop0, pop1)

    def load(src, dst, index):
        copy = pltpu.make_async_copy(src, dst, load_sem.at[index])
        copy.start()
        return copy

    load_phase = [
        load(pop1_hbm.at[pl.ds(19, 7)], pop1.at[pl.ds(19, 7)], 0),
        load(pop0_hbm.at[pl.ds(19, 7)], pop0.at[pl.ds(19, 7)], 1),
    ]
    load_cot = [
        load(cot_hbm.at[pl.ds(0, 13)], adj_a.at[pl.ds(0, 13), pl.ds(1, 8)], 2),
        load(cot_hbm.at[pl.ds(13, 13)], adj_a.at[pl.ds(13, 13), pl.ds(1, 8)], 3),
    ]
    load_flow = [
        load(pop0_hbm.at[pl.ds(0, 19)], pop0.at[pl.ds(0, 19)], 4),
        load(pop1_hbm.at[pl.ds(0, 19)], pop1.at[pl.ds(0, 19)], 5),
    ]

    def device(way):
        return (lax.rem(gx + way[0] + nx, nx), lax.rem(gy + way[1] + ny, ny), gz)

    def across(way):
        return (*device(way)[:2], 1 - gz)

    barrier = pltpu.get_barrier_semaphore()
    others = [across(way) for way in SIDES]
    for target in [partner] + others + [device(way) for way in SIDES + CORNERS]:
        pl.semaphore_signal(barrier, inc=1, device_id=target, device_id_type=MESH)

    copies = []

    def send(src, dst, target):
        index = len(copies)
        copy = pltpu.make_async_remote_copy(
            src_ref=src,
            dst_ref=dst,
            send_sem=send_sem.at[index],
            recv_sem=recv_sem.at[index],
            device_id=target,
            device_id_type=MESH,
        )
        copy.start()
        copies.append(copy)
        return copy

    def arrive(group):
        for copy in group:
            copy.wait_recv()

    row = lax.broadcasted_iota(jnp.int32, (8, 128), 0)
    lane = lax.broadcasted_iota(jnp.int32, (8, 128), 1)

    def rows_of(count):
        return lax.broadcasted_iota(jnp.int32, (count, 8, 128), 1)

    def lanes_of(count):
        return lax.broadcasted_iota(jnp.int32, (count, 8, 128), 2)

    row3, lane3 = rows_of(8), lanes_of(8)

    def roll(values, shift, axis):
        shift = shift % values.shape[axis]
        return values if shift == 0 else pltpu.roll(values, shift, axis)

    def layers(values, before, after):
        shape = values.shape[1:]
        parts = [jnp.zeros((before, *shape), jnp.float32)] if before else []
        parts.append(values)
        if after:
            parts.append(jnp.zeros((after, *shape), jnp.float32))
        return jnp.concatenate(parts, 0)

    def wide(rows):
        return jnp.broadcast_to(rows[:, None, :], (rows.shape[0], 8, 128))

    def shift(inner, outer, step, axis):
        some = inner if inner is not None else outer
        size = some.shape[axis]
        edge = 0 if step == 1 else size - 1
        at_edge = lax.broadcasted_iota(jnp.int32, some.shape, axis) == edge
        a = 0.0 if inner is None else roll(inner, step, axis)
        b = 0.0 if outer is None else roll(outer, step, axis)
        return jnp.where(at_edge, b, a), jnp.where(at_edge, a, b)

    def difference(inner, outer, axis):
        up, down = shift(inner, outer, -1, axis), shift(inner, outer, 1, axis)
        return up[0] - down[0], up[1] - down[1]

    def both_sides(inner, outer, axis):
        up, down = shift(inner, outer, -1, axis), shift(inner, outer, 1, axis)
        return up[0] + down[0], up[1] + down[1]

    def vertical_layers(adj, ref, start):
        for k in range(6):
            ref[start + k] = jnp.where(low, adj[FALLING[k], 8], adj[RISING[k], 1])

    def take_vertical(adj, ref, start):
        for k in range(6):
            layer = ref[start + k]
            adj[RISING[k], 9] = layer
            adj[FALLING[k], 0] = layer

    def slanted(sign, d):
        rise = [i for i in RISING if VELOCITY[i][d] == sign][0]
        fall = [i for i in FALLING if VELOCITY[i][d] == sign][0]
        return rise, fall

    def edge_row(sign):
        return 0 if sign == 1 else 7

    def rows_x(adj, sign, ref, slot):
        for k, i in enumerate(ALONG_X[sign]):
            cz = VELOCITY[i][0]
            ref[slot, k] = adj[i, 1 + cz : 9 + cz, edge_row(sign), :]

    def pack_y(adj, sign, packed):
        source = 0 if sign == 1 else 127
        for k, i in enumerate(ALONG_Y[sign]):
            cz = VELOCITY[i][0]
            values = roll(adj[i, 1 + cz : 9 + cz], k - source, 2)
            packed = values if packed is None else jnp.where(lane3 == k, values, packed)
        return packed

    def well(value):
        return WELL * value * (value - 1.0) * (value - 0.5)

    def well_slope(value):
        return WELL * (3.0 * value * value - 3.0 * value + 0.5)

    def phase_gradients(which, tile, place):
        full = phase[which]
        ahead, behind = SLOT[(-1, 0)], SLOT[(1, 0)]

        def side(slot):
            near = wide(x1r[slot, tile])
            far = wide(x1r[slot, tile + 1])
            first = x1r[slot, 10, place : place + 1, :]
            last = x1r[slot, 10, place + 1 : place + 2, :]
            first = jnp.broadcast_to(first, (8, 128))[None]
            last = jnp.broadcast_to(last, (8, 128))[None]
            return first, near, far, last

        first_n, near_n, far_n, last_n = side(ahead)
        first_p, near_p, far_p, last_p = side(behind)
        x_mid = jnp.where(
            row3 < 4,
            jnp.where(row3 == 0, near_n, far_n),
            jnp.where(row3 == 7, near_p, far_p),
        )
        upper_half = row[None] < 4
        x_tile = jnp.concatenate(
            [jnp.where(upper_half, first_n, first_p), x_mid, jnp.where(upper_half, last_n, last_p)], 0
        )
        start = 6 + 2 * (1 - which)
        y_tile = jnp.where(
            lanes_of(10) < 64,
            roll(y1r[SLOT[(0, -1)] - 2], -start, 2),
            roll(y1r[SLOT[(0, 1)] - 2], 126 - start, 2),
        )
        t = 1 - which
        before_y, after_y = lane < 64, lane >= 64
        corner_n = jnp.where(before_y, c1r[SLOT[(-1, -1)], t], c1r[SLOT[(-1, 1)], t])
        corner_p = jnp.where(before_y, c1r[SLOT[(1, -1)], t], c1r[SLOT[(1, 1)], t])
        b_tile = jnp.where(row3 < 4, wide(corner_n), wide(corner_p))
        mid, y_mid = full[1:11], y_tile[1:9]
        slope[which, 0] = well_slope(mid)
        slope[which, 1] = well_slope(x_tile)
        slope[which, 2] = well_slope(y_tile)

        x_up, x_down = shift(mid, x_tile, -1, 1), shift(mid, x_tile, 1, 1)
        y_up, y_down = shift(mid, y_tile, -1, 2), shift(mid, y_tile, 1, 2)
        grads[which, 0] = 0.5 * (full[3:11] - full[1:9])
        grads[which, 1] = 0.5 * (x_up[0] - x_down[0])[1:9]
        grads[which, 2] = 0.5 * (y_up[0] - y_down[0])[1:9]
        lap = x_up[0] + x_down[0] + y_up[0] + y_down[0] + full[:10] + full[2:] - 6.0 * mid
        pot = well(mid) - STIFFNESS * lap
        pot = jnp.concatenate(
            [jnp.where(low, 0.0, pot[:1]), pot[1:9], jnp.where(low, pot[9:], 0.0)], 0
        )
        lap = (x_up[1] + x_down[1])[1:9] + both_sides(x_mid, b_tile, 2)[0]
        lap = lap + x_tile[:8] + x_tile[2:] - 6.0 * x_mid
        pot_x = well(x_mid) - STIFFNESS * lap
        lap = (y_up[1] + y_down[1])[1:9] + both_sides(y_mid, b_tile, 1)[0]
        lap = lap + y_tile[:8] + y_tile[2:] - 6.0 * y_mid
        pot_y = well(y_mid) - STIFFNESS * lap
        grads[which, 3] = 0.5 * (pot[2:] - pot[:8])
        grads[which, 4] = 0.5 * difference(pot[1:9], pot_x, 1)[0]
        grads[which, 5] = 0.5 * difference(pot[1:9], pot_y, 2)[0]

    def total(values):
        values = list(values)
        while len(values) > 1:
            values = [
                values[j] + values[j + 1] if j + 1 < len(values) else values[j]
                for j in range(0, len(values), 2)
            ]
        return values[0]

    def signed(values, weight):
        plus = [values[i] for i in range(len(values)) if weight(i) == 1]
        minus = [values[i] for i in range(len(values)) if weight(i) == -1]
        return total(plus) - total(minus)

    def part(d):
        return lambda i: VELOCITY[i][d]

    def pair(d, e):
        return lambda i: VELOCITY[i][d] * VELOCITY[i][e]

    def dot(u, v):
        return u[0] * v[0] + u[1] * v[1] + u[2] * v[2]

    def flow_moments(which):
        def layer(z, carry):
            f = [pops[which][i, z].astype(jnp.float32) for i in range(19)]
            flow[which, 0, z] = total(f)
            for d in range(3):
                flow[which, 1 + d, z] = signed(f, part(d))
            return carry

        lax.fori_loop(0, 8, layer, 0)

    def bounce(z, i, own, bounced):
        if VELOCITY[i][0] == 1:
            return jnp.where(jnp.logical_and(z == 7, jnp.logical_not(low)), bounced, own)
        if VELOCITY[i][0] == -1:
            return jnp.where(jnp.logical_and(z == 0, low), bounced, own)
        return own

    def arrived(z, i, adj, xr, yr, ystart, cr, tile):
        cz, cx, cy = VELOCITY[i]
        own = adj[i, z + (1 + cz)]
        erow = 7 if cx == 1 else 0
        elane = 127 if cy == 1 else 0
        moved = own
        if cx:
            k = ALONG_X[cx].index(i)
            got = jnp.broadcast_to(xr[SLOT[(-cx, 0)], k, pl.ds(z, 1), :], (8, 128))
            moved = jnp.where(row == erow, got, roll(own, -cx, 0))
        if cy:
            k = ALONG_Y[cy].index(i)
            got = roll(yr[SLOT[(0, -cy)] - 2, ystart + z], elane - k, 1)
            if cx:
                corner = cr[SLOT[(-cx, -cy)], tile, pl.ds(z, 1), :]
                corner = roll(jnp.broadcast_to(corner, (8, 128)), -cy, 1)
                got = jnp.where(row == erow, corner, roll(got, -cx, 0))
            moved = jnp.where(lane == elane, got, roll(moved, -cy, 1))
        return bounce(z, i, moved, adj[OPPOSITE[i], z + 1])

    PAIRS = [(0, 0), (1, 1), (2, 2), (1, 0), (2, 0), (2, 1)]

    def gather_flow(which, *sources):
        def layer(z, carry):
            a = [arrived(z, i, *sources) for i in range(19)]
            for i in range(19):
                arrive_f[i, z] = a[i]
            wa = [a[0] * (1.0 / 3.0)]
            wa += [a[i] * (1.0 / 18.0) for i in range(1, 7)]
            wa += [a[i] * (1.0 / 36.0) for i in range(7, 19)]
            moments[0, z] = total(wa)
            for d in range(3):
                moments[1 + d, z] = signed(wa, part(d))
            for n, (d, e) in enumerate(PAIRS):
                if d == e:
                    moments[4 + n, z] = total([wa[i] for i in range(19) if VELOCITY[i][d]])
                else:
                    moments[4 + n, z] = signed(wa, pair(d, e))
            moments[10, z] = total([a[i] * pops[which][i, z].astype(jnp.float32) for i in range(19)])
            return carry

        lax.fori_loop(0, 8, layer, 0)

    def collide_adjoint(which, sources, result, offset, with_phi):
        def layer(z, carry):
            def arrived_phi(i):
                cz, cx, cy = VELOCITY[i]
                own = phi[z + (1 + cz)]
                if cx:
                    erow = 7 if cx == 1 else 0
                    got = jnp.broadcast_to(x3r[SLOT[(-cx, 0)], pl.ds(z, 1), :], (8, 128))
                    own = jnp.where(row == erow, got, roll(own, -cx, 0))
                if cy:
                    elane = 127 if cy == 1 else 0
                    got = roll(y3r[SLOT[(0, -cy)] - 2, z], -cy, 1)
                    own = jnp.where(lane == elane, got, roll(own, -cy, 1))
                return bounce(z, i, own, phi[z + 1])

            g = [arrived(z, i, *sources) for i in range(19, 26)]
            if with_phi:
                g = [g[k] + arrived_phi(19 + k) for k in range(7)]
            frac = phase[which, z + 2]
            pressure = flow[which, 0, z]
            momentum = [flow[which, 1 + d, z] for d in range(3)]
            a0 = moments[0, z]
            a1 = [moments[1 + d, z] for d in range(3)]
            a2 = {}
            for n, (d, e) in enumerate(PAIRS):
                a2[d, e] = a2[e, d] = moments[4 + n, z]
            af = moments[10, z]
            b0 = 0.25 * g[0] + 0.125 * total(g[1:])
            b1 = [0.125 * (g[1 + 2 * d] - g[2 + 2 * d]) for d in range(3)]
            density = 0.2 + 0.8 * frac
            rate = 1.1 + 0.5 * frac
            half = 1.0 - 0.5 * rate
            pg = [grads[which, d, z] for d in range(3)]
            mg = [grads[which, 3 + d, z] for d in range(3)]
            force = [-frac * m for m in mg]
            inverse = 1.0 / density
            u = [(momentum[d] + 0.5 * force[d]) * inverse for d in range(3)]
            a2u = [dot([a2[d, e] for e in range(3)], u) for d in range(3)]
            a2f = [dot([a2[d, e] for e in range(3)], force) for d in range(3)]
            speed = dot(u, u)
            quad = 3.0 * dot(u, a1) + 4.5 * dot(u, a2u) - 1.5 * speed * a0
            slant = [3.0 * a1[d] - 3.0 * a0 * u[d] + 9.0 * a2u[d] for d in range(3)]
            rate_density = rate * density
            phase_pull = (4.0 * PHASE_RATE) * frac
            ubar = [
                rate_density * slant[d]
                + half * (9.0 * a2f[d] - 3.0 * a0 * force[d])
                + phase_pull * b1[d]
                for d in range(3)
            ]
            jbar = [ubar[d] * inverse for d in range(3)]
            fbar = [half * slant[d] + 0.5 * jbar[d] for d in range(3)]
            density_bar = rate * quad - dot(jbar, u)
            rate_bar = pressure * a0 + density * quad - af - 0.5 * dot(force, slant)
            imag = lax.rsqrt(dot(pg, pg) + 0.0625)
            normal = [p * imag for p in pg]
            nb1 = dot(normal, b1)
            frac_bar = (
                0.5 * rate_bar
                + 0.8 * density_bar
                - dot(mg, fbar)
                + PHASE_RATE * (b0 + 4.0 * dot(u, b1))
                + (PHASE_RATE * 4.0 * SHARPEN) * (1.0 - 2.0 * frac) * nb1
            )
            pull = (PHASE_RATE * 4.0 * SHARPEN) * frac * (1.0 - frac) * imag
            for d in range(3):
                sens[d, z] = pull * (b1[d] - normal[d] * nb1)
                sens[3 + d, z] = -frac * fbar[d]
            phibar[z] = frac_bar
            pbar = rate * a0
            keep = 1.0 - rate
            for i in range(19):
                value = keep * arrive_f[i, z] + pbar
                for d in range(3):
                    if VELOCITY[i][d] == 1:
                        value = value + jbar[d]
                    elif VELOCITY[i][d] == -1:
                        value = value - jbar[d]
                result[i, z + offset] = value
            for k in range(7):
                result[19 + k, z + offset] = (1.0 - PHASE_RATE) * g[k]
            return carry

        lax.fori_loop(0, 8, layer, 0)

    def phase_share(which):
        def spread(first):
            vz = sens[first]
            in_x, out_x = difference(sens[first + 1], None, 1)
            in_y, out_y = difference(sens[first + 2], None, 2)
            inner = layers(-0.5 * (in_x + in_y), 1, 1)
            inner = inner + 0.5 * (layers(vz, 2, 0) - layers(vz, 0, 2))
            return inner, layers(-0.5 * out_x, 1, 1), layers(-0.5 * out_y, 1, 1)

        mu, mu_x, mu_y = spread(3)
        mu = jnp.concatenate(
            [jnp.where(low, 0.0, mu[:1]), mu[1:9], jnp.where(low, mu[9:], 0.0)], 0
        )
        own, own_x, own_y = spread(0)
        in_x, out_x = both_sides(mu, mu_x, 1)
        in_y, out_y = both_sides(mu, mu_y, 2)
        over_x, corner_x = both_sides(mu_x[1:9], None, 2)
        over_y, corner_y = both_sides(mu_y[1:9], None, 1)
        inner = slope[which, 0] * mu - STIFFNESS * (in_x + in_y - 6.0 * mu) + own
        inner = inner + layers(phibar[...], 1, 1)
        inner = layers(inner, 1, 1) - STIFFNESS * (layers(mu, 2, 0) + layers(mu, 0, 2))

        def beside(scale, values, out_share, over, extra):
            vertical = layers(values[1:], 0, 1) + layers(values[:9], 1, 0)
            lap = out_share + layers(over, 1, 1) + vertical - 6.0 * values
            return scale * values - STIFFNESS * lap + extra

        side_x = beside(slope[which, 1], mu_x, out_x, over_x, own_x)
        side_y = beside(slope[which, 2], mu_y, out_y, over_y, own_y)
        return inner, side_x, side_y, -STIFFNESS * (corner_x + corner_y)

    def send_share(share, zs, zr, es, er, xs, xr, ys, yr, cs, cr):
        inner, side_x, side_y, corner = share
        group = []
        ys[...] = side_y[1:9]
        for way in SIDES[2:]:
            slot = SLOT[way] - 2
            group.append(send(ys, yr.at[slot], device(way)))
        xs[0, 0], xs[0, 1] = side_x[1:9, 7, :], side_x[1:9, 6, :]
        xs[1, 0], xs[1, 1] = side_x[1:9, 0, :], side_x[1:9, 1, :]
        cs[0], cs[1] = corner[:, 7, :], corner[:, 0, :]
        for way in CORNERS:
            group.append(send(cs.at[0 if way[0] < 0 else 1], cr.at[SLOT[way]], device(way)))
        for way in SIDES[:2]:
            slot = SLOT[way]
            group.append(send(xs.at[slot], xr.at[slot], device(way)))
        es[0] = jnp.where(low, side_x[9], side_x[0])
        es[1] = jnp.where(low, side_y[9], side_y[0])
        for way in SIDES:
            slot = SLOT[way]
            group.append(send(es.at[0 if way[0] else 1], er.at[slot], across(way)))
        zs[...] = jnp.where(low, inner[10:], inner[:2])
        group.append(send(zs, zr, partner))
        return inner[2:10], group

    def collect_share(center, group, zr, er, xr, yr, cr):
        arrive(group)
        prev_x, next_x, prev_y, next_y = (er[SLOT[way]] for way in ((1, 0), (-1, 0), (0, 1), (0, -1)))
        beyond = jnp.where(row == 0, prev_x, jnp.where(row == 7, next_x, 0.0))
        beyond = beyond + jnp.where(lane == 0, prev_y, jnp.where(lane == 127, next_y, 0.0))
        extra = zr[...]
        to_low = jnp.concatenate([extra[:1], extra[1:] + beyond[None]], 0)
        to_high = jnp.concatenate([extra[:1] + beyond[None], extra[1:]], 0)
        lower = center[:2] + jnp.where(low, 0.0, to_high)
        upper = center[6:] + jnp.where(low, to_low, 0.0)
        center = jnp.concatenate([lower, center[2:6], upper], 0)
        prev, after = SLOT[(1, 0)], SLOT[(-1, 0)]
        near = jnp.where(row3 < 4, wide(xr[prev, 0]), wide(xr[after, 0]))
        far = jnp.where(row3 < 4, wide(xr[prev, 1]), wide(xr[after, 1]))
        end = jnp.logical_or(row3 == 0, row3 == 7)
        next_end = jnp.logical_or(row3 == 1, row3 == 6)
        result = center + jnp.where(end, near, jnp.where(next_end, far, 0.0))
        from_y = jnp.where(lane3 < 64, yr[SLOT[(0, 1)] - 2], yr[SLOT[(0, -1)] - 2])
        result = result + jnp.where(jnp.logical_or(lane3 < 2, lane3 >= 126), from_y, 0.0)
        before = lane < 64
        ends = jnp.logical_or(lane == 0, lane == 127)
        prev_c = jnp.where(ends, jnp.where(before, cr[SLOT[(1, 1)]], cr[SLOT[(1, -1)]]), 0.0)
        next_c = jnp.where(ends, jnp.where(before, cr[SLOT[(-1, 1)]], cr[SLOT[(-1, -1)]]), 0.0)
        corners = jnp.where(row3 == 0, wide(prev_c), wide(next_c))
        return result + jnp.where(end, corners, 0.0)

    for copy in load_phase:
        copy.wait()
    for which in range(2):
        phase[which, 2:10] = total([pops[which][i].astype(jnp.float32) for i in range(19, 26)])
        z1s[2 * which : 2 * which + 2] = jnp.where(low, phase[which, 8:10], phase[which, 2:4])
    for copy in load_cot:
        copy.wait()
    vertical_layers(adj_a, z1s, 4)
    pl.semaphore_wait(barrier, 13)
    first = [send(z1s, z1r, partner)]

    def edge_layer(values):
        return jnp.where(low, values[7], values[0])

    for way in SIDES[2:]:
        slot = SLOT[way] - 2
        source = 0 if way[1] < 0 else 126
        middle = jnp.where(
            lane3 < 8,
            roll(phase[1, 2:10], 6 - source, 2),
            roll(phase[0, 2:10], 8 - source, 2),
        )
        entries = pack_y(adj_a, -way[1], None)
        y1s[slot] = jnp.where(lane3 < 6, entries, middle)
        first.append(send(y1s.at[slot], y1r.at[slot, pl.ds(1, 8)], device(way)))
        rise, fall = slanted(-way[1], 2)
        beyond = jnp.where(low, adj_a[fall, 8], adj_a[rise, 1])
        edge = edge_layer(middle)
        for i in (rise, fall):
            k = ALONG_Y[-way[1]].index(i)
            edge = jnp.where(lane == k, roll(beyond, k - (0 if way[1] < 0 else 127), 1), edge)
        zy1s[slot] = edge
        first.append(send(zy1s.at[slot], zy1r.at[slot], across(way)))
    for way in CORNERS:
        slot = SLOT[way]
        r = edge_row(-way[0])
        c1s[slot, 0] = phase[1, 2:10, r, :]
        c1s[slot, 1] = phase[0, 2:10, r, :]
        c1s[slot, 2] = adj_a[DIAGONAL[(-way[0], -way[1])], 1:9, r, :]
        first.append(send(c1s.at[slot], c1r.at[slot], device(way)))
    for way in SIDES[:2]:
        slot = SLOT[way]
        r = edge_row(-way[0])
        rows_x(adj_a, -way[0], x1s, slot)
        for n, which in enumerate((1, 0)):
            x1s[slot, 6 + 2 * n] = phase[which, 2:10, r, :]
            x1s[slot, 7 + 2 * n] = phase[which, 2:10, r + (1 if r == 0 else -1), :]
            zx1s[slot, n : n + 1, :] = jnp.where(
                low, phase[which, 9, r : r + 1, :], phase[which, 2, r : r + 1, :]
            )
        rise, fall = slanted(-way[0], 1)
        zx1s[slot, 2:3, :] = jnp.where(
            low, adj_a[fall, 8, r : r + 1, :], adj_a[rise, 1, r : r + 1, :]
        )
        zx1s[slot, 3:, :] = jnp.zeros((5, 128), jnp.float32)
        first.append(send(x1s.at[slot], x1r.at[slot, pl.ds(0, 10)], device(way)))
        first.append(send(zx1s.at[slot], zx1r.at[slot], across(way)))
    for copy in load_flow:
        copy.wait()
    flow_moments(1)
    flow_moments(0)
    arrive(first)
    for which in range(2):
        got = z1r[2 * which : 2 * which + 2]
        phase[which, :2] = jnp.where(low, 0.0, got)
        phase[which, 10:] = jnp.where(low, got, 0.0)
    take_vertical(adj_a, z1r, 4)
    for way in SIDES:
        sign = -way[0] - way[1]
        if way[0]:
            slot = SLOT[way]
            rise, fall = slanted(sign, 1)
            entry = zx1r[slot, 2:3, :]
            x1r[slot, ALONG_X[sign].index(rise), 7:8, :] = entry
            x1r[slot, ALONG_X[sign].index(fall), 0:1, :] = entry
            for n in range(2):
                line = zx1r[slot, n : n + 1, :]
                x1r[slot, 10, 2 * n : 2 * n + 1, :] = jnp.where(low, 0.0, line)
                x1r[slot, 10, 2 * n + 1 : 2 * n + 2, :] = jnp.where(low, line, 0.0)
        else:
            slot = SLOT[way] - 2
            rise, fall = slanted(sign, 2)
            tile = zy1r[slot]
            y1r[slot, 0] = jnp.where(low, 0.0, tile)
            y1r[slot, 9] = jnp.where(low, tile, 0.0)
            y1r[slot, 8] = jnp.where(lane == ALONG_Y[sign].index(rise), tile, y1r[slot, 8])
            y1r[slot, 1] = jnp.where(lane == ALONG_Y[sign].index(fall), tile, y1r[slot, 1])
    sources = (adj_a, x1r, y1r, 1, c1r, 2)
    phase_gradients(1, 6, 0)
    gather_flow(1, *sources)
    collide_adjoint(1, sources, adj_b, 1, False)

    vertical_layers(adj_b, z2s, 0)
    vertical = send(z2s, z2r, partner)
    share = phase_share(1)
    center, group = send_share(
        share, zd2s, zd2r, zs2s, zs2r, xd2s, xd2r, yd2s, yd2r, cd2s, cd2r
    )
    vertical.wait_recv()
    take_vertical(adj_b, z2r, 0)
    second = []
    for way in SIDES[2:]:
        slot = SLOT[way] - 2
        y2s[slot] = pack_y(adj_b, -way[1], None)
        second.append(send(y2s.at[slot], y2r.at[slot], device(way)))
    for way in CORNERS:
        slot = SLOT[way]
        c2s[slot, 0] = adj_b[DIAGONAL[(-way[0], -way[1])], 1:9, edge_row(-way[0]), :]
        second.append(send(c2s.at[slot], c2r.at[slot], device(way)))
    for way in SIDES[:2]:
        slot = SLOT[way]
        rows_x(adj_b, -way[0], x2s, slot)
        second.append(send(x2s.at[slot], x2r.at[slot], device(way)))
    phase_gradients(0, 8, 2)
    phi[1:9] = collect_share(center, group, zd2r, zs2r, xd2r, yd2r, cd2r)
    third = []
    for way in SIDES:
        slot = SLOT[way]
        if way[0]:
            x3s[slot] = phi[1:9, edge_row(-way[0]), :]
            third.append(send(x3s.at[slot], x3r.at[slot], device(way)))
        else:
            third.append(send(phi.at[pl.ds(1, 8)], y3r.at[slot - 2], device(way)))
    z3s[...] = jnp.where(low, phi[8], phi[1])
    third.append(send(z3s, z3r, partner))
    arrive(second)
    sources = (adj_b, x2r, y2r, 0, c2r, 0)
    gather_flow(0, *sources)
    arrive(third)
    phi[0] = z3r[...]
    phi[9] = z3r[...]
    collide_adjoint(0, sources, out, 0, True)

    stores = [
        load(out.at[pl.ds(0, 10)], out_hbm.at[pl.ds(0, 10)], 6),
        load(out.at[pl.ds(10, 9)], out_hbm.at[pl.ds(10, 9)], 7),
    ]
    share = phase_share(0)
    center, group = send_share(
        share, zd4s, zd4r, zs4s, zs4r, xd4s, xd4r, yd4s, yd4r, cd4s, cd4r
    )
    last = collect_share(center, group, zd4r, zs4r, xd4r, yd4r, cd4r)
    for k in range(7):
        out[19 + k] = out[19 + k] + last
    stores.append(load(out.at[pl.ds(19, 7)], out_hbm.at[pl.ds(19, 7)], 8))
    for copy in stores:
        copy.wait()
    for copy in copies:
        copy.wait_send()


def local(populations0, populations1, cotangent):
    def vmem(*shape):
        return pltpu.VMEM(shape + (8, 128), jnp.float32)

    share = [
        vmem(2), vmem(2), vmem(2), vmem(4), vmem(2, 2), vmem(2, 2),
        vmem(8), vmem(2, 8), vmem(2), vmem(4),
    ]
    scratch = [
        vmem(26, 8),
        pltpu.VMEM(populations0.shape, populations0.dtype),
        pltpu.VMEM(populations1.shape, populations1.dtype),
        vmem(26, 10), vmem(26, 10), vmem(2, 12), vmem(2, 6, 8), vmem(6, 8), vmem(8),
        vmem(2, 3, 10), vmem(10), vmem(2, 4, 8), vmem(11, 8), vmem(19, 8),
        vmem(10), vmem(10), vmem(2, 10), vmem(2, 11), vmem(2, 8), vmem(2, 10), vmem(4, 3), vmem(4, 3),
        vmem(6), vmem(6), vmem(2, 6), vmem(2, 6), vmem(2, 8), vmem(2, 8), vmem(4, 1), vmem(4, 1),
        vmem(2), vmem(2), vmem(2), vmem(2),
        *share,
        vmem(), vmem(), vmem(2), vmem(2), vmem(2, 8),
        *share,
        pltpu.SemaphoreType.DMA((64,)),
        pltpu.SemaphoreType.DMA((64,)),
        pltpu.SemaphoreType.DMA((9,)),
    ]
    operands = [
        pltpu.with_memory_space_constraint(operand, pltpu.HBM)
        for operand in (populations0, populations1, cotangent)
    ]
    return pl.pallas_call(
        kernel,
        out_shape=jax.ShapeDtypeStruct(cotangent.shape, jnp.float32),
        in_specs=[pl.BlockSpec(memory_space=pltpu.HBM)] * 3,
        out_specs=pl.BlockSpec(memory_space=pl.ANY),
        scratch_shapes=scratch,
        compiler_params=pltpu.CompilerParams(
            collective_id=0, has_side_effects=True, vmem_limit_bytes=40 * 1024 * 1024
        ),
    )(*operands)


def solution(mesh):
    spec = P(None, "gz", "gx", "gy")
    return jax.shard_map(
        local, mesh=mesh, in_specs=(spec, spec, spec), out_specs=spec, check_vma=False
    )
```

```python
import jax
import jax.numpy as jnp
import numpy as np
from jax import lax
from jax.experimental import pallas as pl
from jax.experimental.pallas import tpu as pltpu
from jax.sharding import PartitionSpec as P

VELOCITY = [
    (0, 0, 0),
    (1, 0, 0),
    (-1, 0, 0),
    (0, 1, 0),
    (0, -1, 0),
    (0, 0, 1),
    (0, 0, -1),
    (1, 1, 0),
    (-1, -1, 0),
    (1, -1, 0),
    (-1, 1, 0),
    (1, 0, 1),
    (-1, 0, -1),
    (1, 0, -1),
    (-1, 0, 1),
    (0, 1, 1),
    (0, -1, -1),
    (0, 1, -1),
    (0, -1, 1),
]
OPPOSITE = [0, 2, 1, 4, 3, 6, 5, 8, 7, 10, 9, 12, 11, 14, 13, 16, 15, 18, 17]
VELOCITY = VELOCITY + VELOCITY[:7]
OPPOSITE = OPPOSITE + [19 + mirror for mirror in OPPOSITE[:7]]
WELL = 1.2
STIFFNESS = 0.6
SHARPEN = 0.3
PHASE_RATE = 1.4
MESH = pl.DeviceIdType.MESH
TOGETHER = 4

RISING = [i for i in range(26) if VELOCITY[i][0] == 1]
FALLING = [i for i in range(26) if VELOCITY[i][0] == -1]
ALONG_X = {sign: [i for i in range(26) if VELOCITY[i][1] == sign] for sign in (1, -1)}
ALONG_Y = {sign: [i for i in range(26) if VELOCITY[i][2] == sign] for sign in (1, -1)}
DIAGONAL = {VELOCITY[i][1:]: i for i in range(15, 19)}
SIDES = [(-1, 0), (1, 0), (0, -1), (0, 1)]
CORNERS = [(-1, -1), (-1, 1), (1, -1), (1, 1)]
SLOT = {way: i for i, way in enumerate(SIDES)}
SLOT.update({way: i for i, way in enumerate(CORNERS)})


def kernel(
    pop0_hbm, pop1_hbm, cot_hbm, out_hbm,
    out, pop0, pop1, adj_a, adj_b, phase, grads, sens, phibar, slope, phi, flow, moments, arrive_f,
    z1s, z1r, x1s, x1r, y1s, y1r, c1s, c1r,
    z2s, z2r, x2s, x2r, y2s, y2r, c2s, c2r,
    zx1s, zx1r, zy1s, zy1r,
    zd2s, zd2r, zs2s, zs2r, xd2s, xd2r, yd2s, yd2r, cd2s, cd2r,
    z3s, z3r, x3s, x3r, y3r,
    zd4s, zd4r, zs4s, zs4r, xd4s, xd4r, yd4s, yd4r, cd4s, cd4r,
    send_sem, recv_sem, load_sem,
):
    gx, gy, gz = lax.axis_index("gx"), lax.axis_index("gy"), lax.axis_index("gz")
    nx, ny = lax.axis_size("gx"), lax.axis_size("gy")
    low = gz == 0
    partner = (gx, gy, 1 - gz)
    pops = (pop0, pop1)

    def load(src, dst, index):
        copy = pltpu.make_async_copy(src, dst, load_sem.at[index])
        copy.start()
        return copy

    load_phase = [
        load(pop1_hbm.at[pl.ds(19, 7)], pop1.at[pl.ds(19, 7)], 0),
        load(pop0_hbm.at[pl.ds(19, 7)], pop0.at[pl.ds(19, 7)], 1),
    ]
    load_cot = [
        load(cot_hbm.at[pl.ds(0, 13)], adj_a.at[pl.ds(0, 13), pl.ds(1, 8)], 2),
        load(cot_hbm.at[pl.ds(13, 13)], adj_a.at[pl.ds(13, 13), pl.ds(1, 8)], 3),
    ]
    load_flow = [
        load(pop0_hbm.at[pl.ds(0, 19)], pop0.at[pl.ds(0, 19)], 4),
        load(pop1_hbm.at[pl.ds(0, 19)], pop1.at[pl.ds(0, 19)], 5),
    ]

    def device(way):
        return (lax.rem(gx + way[0] + nx, nx), lax.rem(gy + way[1] + ny, ny), gz)

    def across(way):
        return (*device(way)[:2], 1 - gz)

    barrier = pltpu.get_barrier_semaphore()
    others = [across(way) for way in SIDES]
    for target in [partner] + others + [device(way) for way in SIDES + CORNERS]:
        pl.semaphore_signal(barrier, inc=1, device_id=target, device_id_type=MESH)

    copies = []

    def send(src, dst, target):
        index = len(copies)
        copy = pltpu.make_async_remote_copy(
            src_ref=src,
            dst_ref=dst,
            send_sem=send_sem.at[index],
            recv_sem=recv_sem.at[index],
            device_id=target,
            device_id_type=MESH,
        )
        copy.start()
        copies.append(copy)
        return copy

    def arrive(group):
        for copy in group:
            copy.wait_recv()

    row = lax.broadcasted_iota(jnp.int32, (8, 128), 0)
    lane = lax.broadcasted_iota(jnp.int32, (8, 128), 1)

    def rows_of(count):
        return lax.broadcasted_iota(jnp.int32, (count, 8, 128), 1)

    def lanes_of(count):
        return lax.broadcasted_iota(jnp.int32, (count, 8, 128), 2)

    row3, lane3 = rows_of(8), lanes_of(8)

    def roll(values, shift, axis):
        shift = shift % values.shape[axis]
        return values if shift == 0 else pltpu.roll(values, shift, axis)

    def layers(values, before, after):
        shape = values.shape[1:]
        parts = [jnp.zeros((before, *shape), jnp.float32)] if before else []
        parts.append(values)
        if after:
            parts.append(jnp.zeros((after, *shape), jnp.float32))
        return jnp.concatenate(parts, 0)

    def wide(rows):
        return jnp.broadcast_to(rows[:, None, :], (rows.shape[0], 8, 128))

    def shift(inner, outer, step, axis):
        some = inner if inner is not None else outer
        size = some.shape[axis]
        edge = 0 if step == 1 else size - 1
        at_edge = lax.broadcasted_iota(jnp.int32, some.shape, axis) == edge
        a = 0.0 if inner is None else roll(inner, step, axis)
        b = 0.0 if outer is None else roll(outer, step, axis)
        return jnp.where(at_edge, b, a), jnp.where(at_edge, a, b)

    def difference(inner, outer, axis):
        up, down = shift(inner, outer, -1, axis), shift(inner, outer, 1, axis)
        return up[0] - down[0], up[1] - down[1]

    def both_sides(inner, outer, axis):
        up, down = shift(inner, outer, -1, axis), shift(inner, outer, 1, axis)
        return up[0] + down[0], up[1] + down[1]

    def vertical_layers(adj, ref, start):
        for k in range(6):
            ref[start + k] = jnp.where(low, adj[FALLING[k], 8], adj[RISING[k], 1])

    def take_vertical(adj, ref, start):
        for k in range(6):
            layer = ref[start + k]
            adj[RISING[k], 9] = layer
            adj[FALLING[k], 0] = layer

    def slanted(sign, d):
        rise = [i for i in RISING if VELOCITY[i][d] == sign][0]
        fall = [i for i in FALLING if VELOCITY[i][d] == sign][0]
        return rise, fall

    def edge_row(sign):
        return 0 if sign == 1 else 7

    def rows_x(adj, sign, ref, slot):
        for k, i in enumerate(ALONG_X[sign]):
            cz = VELOCITY[i][0]
            ref[slot, k] = adj[i, 1 + cz : 9 + cz, edge_row(sign), :]

    def pack_y(adj, sign, packed):
        source = 0 if sign == 1 else 127
        for k, i in enumerate(ALONG_Y[sign]):
            cz = VELOCITY[i][0]
            values = roll(adj[i, 1 + cz : 9 + cz], k - source, 2)
            packed = values if packed is None else jnp.where(lane3 == k, values, packed)
        return packed

    def well(value):
        return WELL * value * (value - 1.0) * (value - 0.5)

    def well_slope(value):
        return WELL * (3.0 * value * value - 3.0 * value + 0.5)

    def phase_gradients(which, tile, place):
        full = phase[which]
        ahead, behind = SLOT[(-1, 0)], SLOT[(1, 0)]

        def side(slot):
            near = wide(x1r[slot, tile])
            far = wide(x1r[slot, tile + 1])
            first = x1r[slot, 10, place : place + 1, :]
            last = x1r[slot, 10, place + 1 : place + 2, :]
            first = jnp.broadcast_to(first, (8, 128))[None]
            last = jnp.broadcast_to(last, (8, 128))[None]
            return first, near, far, last

        first_n, near_n, far_n, last_n = side(ahead)
        first_p, near_p, far_p, last_p = side(behind)
        x_mid = jnp.where(
            row3 < 4,
            jnp.where(row3 == 0, near_n, far_n),
            jnp.where(row3 == 7, near_p, far_p),
        )
        upper_half = row[None] < 4
        x_tile = jnp.concatenate(
            [jnp.where(upper_half, first_n, first_p), x_mid, jnp.where(upper_half, last_n, last_p)], 0
        )
        start = 6 + 2 * (1 - which)
        y_tile = jnp.where(
            lanes_of(10) < 64,
            roll(y1r[SLOT[(0, -1)] - 2], -start, 2),
            roll(y1r[SLOT[(0, 1)] - 2], 126 - start, 2),
        )
        t = 1 - which
        before_y, after_y = lane < 64, lane >= 64
        corner_n = jnp.where(before_y, c1r[SLOT[(-1, -1)], t], c1r[SLOT[(-1, 1)], t])
        corner_p = jnp.where(before_y, c1r[SLOT[(1, -1)], t], c1r[SLOT[(1, 1)], t])
        b_tile = jnp.where(row3 < 4, wide(corner_n), wide(corner_p))
        mid, y_mid = full[1:11], y_tile[1:9]
        slope[which, 0] = well_slope(mid)
        slope[which, 1] = well_slope(x_tile)
        slope[which, 2] = well_slope(y_tile)

        x_up, x_down = shift(mid, x_tile, -1, 1), shift(mid, x_tile, 1, 1)
        y_up, y_down = shift(mid, y_tile, -1, 2), shift(mid, y_tile, 1, 2)
        grads[which, 0] = 0.5 * (full[3:11] - full[1:9])
        grads[which, 1] = 0.5 * (x_up[0] - x_down[0])[1:9]
        grads[which, 2] = 0.5 * (y_up[0] - y_down[0])[1:9]
        lap = x_up[0] + x_down[0] + y_up[0] + y_down[0] + full[:10] + full[2:] - 6.0 * mid
        pot = well(mid) - STIFFNESS * lap
        pot = jnp.concatenate(
            [jnp.where(low, 0.0, pot[:1]), pot[1:9], jnp.where(low, pot[9:], 0.0)], 0
        )
        lap = (x_up[1] + x_down[1])[1:9] + both_sides(x_mid, b_tile, 2)[0]
        lap = lap + x_tile[:8] + x_tile[2:] - 6.0 * x_mid
        pot_x = well(x_mid) - STIFFNESS * lap
        lap = (y_up[1] + y_down[1])[1:9] + both_sides(y_mid, b_tile, 1)[0]
        lap = lap + y_tile[:8] + y_tile[2:] - 6.0 * y_mid
        pot_y = well(y_mid) - STIFFNESS * lap
        grads[which, 3] = 0.5 * (pot[2:] - pot[:8])
        grads[which, 4] = 0.5 * difference(pot[1:9], pot_x, 1)[0]
        grads[which, 5] = 0.5 * difference(pot[1:9], pot_y, 2)[0]

    def total(values):
        values = list(values)
        while len(values) > 1:
            values = [
                values[j] + values[j + 1] if j + 1 < len(values) else values[j]
                for j in range(0, len(values), 2)
            ]
        return values[0]

    def signed(values, weight):
        plus = [values[i] for i in range(len(values)) if weight(i) == 1]
        minus = [values[i] for i in range(len(values)) if weight(i) == -1]
        return total(plus) - total(minus)

    def part(d):
        return lambda i: VELOCITY[i][d]

    def pair(d, e):
        return lambda i: VELOCITY[i][d] * VELOCITY[i][e]

    def dot(u, v):
        return u[0] * v[0] + u[1] * v[1] + u[2] * v[2]

    def each_layer(layer):
        def several(step, carry):
            for n in range(TOGETHER):
                layer(step * TOGETHER + n, carry)
            return carry

        lax.fori_loop(0, 8 // TOGETHER, several, 0)

    def flow_moments(which):
        def layer(z, carry):
            f = [pops[which][i, z].astype(jnp.float32) for i in range(19)]
            flow[which, 0, z] = total(f)
            for d in range(3):
                flow[which, 1 + d, z] = signed(f, part(d))
            return carry

        each_layer(layer)

    def bounce(z, i, own, bounced):
        if VELOCITY[i][0] == 1:
            return jnp.where(jnp.logical_and(z == 7, jnp.logical_not(low)), bounced, own)
        if VELOCITY[i][0] == -1:
            return jnp.where(jnp.logical_and(z == 0, low), bounced, own)
        return own

    def arrived(z, i, adj, xr, yr, ystart, cr, tile):
        cz, cx, cy = VELOCITY[i]
        own = adj[i, z + (1 + cz)]
        erow = 7 if cx == 1 else 0
        elane = 127 if cy == 1 else 0
        moved = own
        if cx:
            k = ALONG_X[cx].index(i)
            got = jnp.broadcast_to(xr[SLOT[(-cx, 0)], k, pl.ds(z, 1), :], (8, 128))
            moved = jnp.where(row == erow, got, roll(own, -cx, 0))
        if cy:
            k = ALONG_Y[cy].index(i)
            got = roll(yr[SLOT[(0, -cy)] - 2, ystart + z], elane - k, 1)
            if cx:
                corner = cr[SLOT[(-cx, -cy)], tile, pl.ds(z, 1), :]
                corner = roll(jnp.broadcast_to(corner, (8, 128)), -cy, 1)
                got = jnp.where(row == erow, corner, roll(got, -cx, 0))
            moved = jnp.where(lane == elane, got, roll(moved, -cy, 1))
        return bounce(z, i, moved, adj[OPPOSITE[i], z + 1])

    PAIRS = [(0, 0), (1, 1), (2, 2), (1, 0), (2, 0), (2, 1)]

    def gather_flow(which, *sources):
        def layer(z, carry):
            a = [arrived(z, i, *sources) for i in range(19)]
            for i in range(19):
                arrive_f[i, z] = a[i]
            wa = [a[0] * (1.0 / 3.0)]
            wa += [a[i] * (1.0 / 18.0) for i in range(1, 7)]
            wa += [a[i] * (1.0 / 36.0) for i in range(7, 19)]
            moments[0, z] = total(wa)
            for d in range(3):
                moments[1 + d, z] = signed(wa, part(d))
            for n, (d, e) in enumerate(PAIRS):
                if d == e:
                    moments[4 + n, z] = total([wa[i] for i in range(19) if VELOCITY[i][d]])
                else:
                    moments[4 + n, z] = signed(wa, pair(d, e))
            moments[10, z] = total([a[i] * pops[which][i, z].astype(jnp.float32) for i in range(19)])
            return carry

        each_layer(layer)

    def collide_adjoint(which, sources, result, offset, with_phi):
        def layer(z, carry):
            def arrived_phi(i):
                cz, cx, cy = VELOCITY[i]
                own = phi[z + (1 + cz)]
                if cx:
                    erow = 7 if cx == 1 else 0
                    got = jnp.broadcast_to(x3r[SLOT[(-cx, 0)], pl.ds(z, 1), :], (8, 128))
                    own = jnp.where(row == erow, got, roll(own, -cx, 0))
                if cy:
                    elane = 127 if cy == 1 else 0
                    got = roll(y3r[SLOT[(0, -cy)] - 2, z], -cy, 1)
                    own = jnp.where(lane == elane, got, roll(own, -cy, 1))
                return bounce(z, i, own, phi[z + 1])

            g = [arrived(z, i, *sources) for i in range(19, 26)]
            if with_phi:
                g = [g[k] + arrived_phi(19 + k) for k in range(7)]
            frac = phase[which, z + 2]
            pressure = flow[which, 0, z]
            momentum = [flow[which, 1 + d, z] for d in range(3)]
            a0 = moments[0, z]
            a1 = [moments[1 + d, z] for d in range(3)]
            a2 = {}
            for n, (d, e) in enumerate(PAIRS):
                a2[d, e] = a2[e, d] = moments[4 + n, z]
            af = moments[10, z]
            b0 = 0.25 * g[0] + 0.125 * total(g[1:])
            b1 = [0.125 * (g[1 + 2 * d] - g[2 + 2 * d]) for d in range(3)]
            density = 0.2 + 0.8 * frac
            rate = 1.1 + 0.5 * frac
            half = 1.0 - 0.5 * rate
            pg = [grads[which, d, z] for d in range(3)]
            mg = [grads[which, 3 + d, z] for d in range(3)]
            force = [-frac * m for m in mg]
            inverse = 1.0 / density
            u = [(momentum[d] + 0.5 * force[d]) * inverse for d in range(3)]
            a2u = [dot([a2[d, e] for e in range(3)], u) for d in range(3)]
            a2f = [dot([a2[d, e] for e in range(3)], force) for d in range(3)]
            speed = dot(u, u)
            quad = 3.0 * dot(u, a1) + 4.5 * dot(u, a2u) - 1.5 * speed * a0
            slant = [3.0 * a1[d] - 3.0 * a0 * u[d] + 9.0 * a2u[d] for d in range(3)]
            rate_density = rate * density
            phase_pull = (4.0 * PHASE_RATE) * frac
            ubar = [
                rate_density * slant[d]
                + half * (9.0 * a2f[d] - 3.0 * a0 * force[d])
                + phase_pull * b1[d]
                for d in range(3)
            ]
            jbar = [ubar[d] * inverse for d in range(3)]
            fbar = [half * slant[d] + 0.5 * jbar[d] for d in range(3)]
            density_bar = rate * quad - dot(jbar, u)
            rate_bar = pressure * a0 + density * quad - af - 0.5 * dot(force, slant)
            imag = lax.rsqrt(dot(pg, pg) + 0.0625)
            normal = [p * imag for p in pg]
            nb1 = dot(normal, b1)
            frac_bar = (
                0.5 * rate_bar
                + 0.8 * density_bar
                - dot(mg, fbar)
                + PHASE_RATE * (b0 + 4.0 * dot(u, b1))
                + (PHASE_RATE * 4.0 * SHARPEN) * (1.0 - 2.0 * frac) * nb1
            )
            pull = (PHASE_RATE * 4.0 * SHARPEN) * frac * (1.0 - frac) * imag
            for d in range(3):
                sens[d, z] = pull * (b1[d] - normal[d] * nb1)
                sens[3 + d, z] = -frac * fbar[d]
            phibar[z] = frac_bar
            pbar = rate * a0
            keep = 1.0 - rate
            for i in range(19):
                value = keep * arrive_f[i, z] + pbar
                for d in range(3):
                    if VELOCITY[i][d] == 1:
                        value = value + jbar[d]
                    elif VELOCITY[i][d] == -1:
                        value = value - jbar[d]
                result[i, z + offset] = value
            for k in range(7):
                result[19 + k, z + offset] = (1.0 - PHASE_RATE) * g[k]
            return carry

        each_layer(layer)

    def phase_share(which):
        def spread(first):
            vz = sens[first]
            in_x, out_x = difference(sens[first + 1], None, 1)
            in_y, out_y = difference(sens[first + 2], None, 2)
            inner = layers(-0.5 * (in_x + in_y), 1, 1)
            inner = inner + 0.5 * (layers(vz, 2, 0) - layers(vz, 0, 2))
            return inner, layers(-0.5 * out_x, 1, 1), layers(-0.5 * out_y, 1, 1)

        mu, mu_x, mu_y = spread(3)
        mu = jnp.concatenate(
            [jnp.where(low, 0.0, mu[:1]), mu[1:9], jnp.where(low, mu[9:], 0.0)], 0
        )
        own, own_x, own_y = spread(0)
        in_x, out_x = both_sides(mu, mu_x, 1)
        in_y, out_y = both_sides(mu, mu_y, 2)
        over_x, corner_x = both_sides(mu_x[1:9], None, 2)
        over_y, corner_y = both_sides(mu_y[1:9], None, 1)
        inner = slope[which, 0] * mu - STIFFNESS * (in_x + in_y - 6.0 * mu) + own
        inner = inner + layers(phibar[...], 1, 1)
        inner = layers(inner, 1, 1) - STIFFNESS * (layers(mu, 2, 0) + layers(mu, 0, 2))

        def beside(scale, values, out_share, over, extra):
            vertical = layers(values[1:], 0, 1) + layers(values[:9], 1, 0)
            lap = out_share + layers(over, 1, 1) + vertical - 6.0 * values
            return scale * values - STIFFNESS * lap + extra

        side_x = beside(slope[which, 1], mu_x, out_x, over_x, own_x)
        side_y = beside(slope[which, 2], mu_y, out_y, over_y, own_y)
        return inner, side_x, side_y, -STIFFNESS * (corner_x + corner_y)

    def send_share(share, zs, zr, es, er, xs, xr, ys, yr, cs, cr):
        inner, side_x, side_y, corner = share
        group = []
        ys[...] = side_y[1:9]
        for way in SIDES[2:]:
            slot = SLOT[way] - 2
            group.append(send(ys, yr.at[slot], device(way)))
        xs[0, 0], xs[0, 1] = side_x[1:9, 7, :], side_x[1:9, 6, :]
        xs[1, 0], xs[1, 1] = side_x[1:9, 0, :], side_x[1:9, 1, :]
        cs[0], cs[1] = corner[:, 7, :], corner[:, 0, :]
        for way in CORNERS:
            group.append(send(cs.at[0 if way[0] < 0 else 1], cr.at[SLOT[way]], device(way)))
        for way in SIDES[:2]:
            slot = SLOT[way]
            group.append(send(xs.at[slot], xr.at[slot], device(way)))
        es[0] = jnp.where(low, side_x[9], side_x[0])
        es[1] = jnp.where(low, side_y[9], side_y[0])
        for way in SIDES:
            slot = SLOT[way]
            group.append(send(es.at[0 if way[0] else 1], er.at[slot], across(way)))
        zs[...] = jnp.where(low, inner[10:], inner[:2])
        group.append(send(zs, zr, partner))
        return inner[2:10], group

    def collect_share(center, group, zr, er, xr, yr, cr):
        arrive(group)
        prev_x, next_x, prev_y, next_y = (er[SLOT[way]] for way in ((1, 0), (-1, 0), (0, 1), (0, -1)))
        beyond = jnp.where(row == 0, prev_x, jnp.where(row == 7, next_x, 0.0))
        beyond = beyond + jnp.where(lane == 0, prev_y, jnp.where(lane == 127, next_y, 0.0))
        extra = zr[...]
        to_low = jnp.concatenate([extra[:1], extra[1:] + beyond[None]], 0)
        to_high = jnp.concatenate([extra[:1] + beyond[None], extra[1:]], 0)
        lower = center[:2] + jnp.where(low, 0.0, to_high)
        upper = center[6:] + jnp.where(low, to_low, 0.0)
        center = jnp.concatenate([lower, center[2:6], upper], 0)
        prev, after = SLOT[(1, 0)], SLOT[(-1, 0)]
        near = jnp.where(row3 < 4, wide(xr[prev, 0]), wide(xr[after, 0]))
        far = jnp.where(row3 < 4, wide(xr[prev, 1]), wide(xr[after, 1]))
        end = jnp.logical_or(row3 == 0, row3 == 7)
        next_end = jnp.logical_or(row3 == 1, row3 == 6)
        result = center + jnp.where(end, near, jnp.where(next_end, far, 0.0))
        from_y = jnp.where(lane3 < 64, yr[SLOT[(0, 1)] - 2], yr[SLOT[(0, -1)] - 2])
        result = result + jnp.where(jnp.logical_or(lane3 < 2, lane3 >= 126), from_y, 0.0)
        before = lane < 64
        ends = jnp.logical_or(lane == 0, lane == 127)
        prev_c = jnp.where(ends, jnp.where(before, cr[SLOT[(1, 1)]], cr[SLOT[(1, -1)]]), 0.0)
        next_c = jnp.where(ends, jnp.where(before, cr[SLOT[(-1, 1)]], cr[SLOT[(-1, -1)]]), 0.0)
        corners = jnp.where(row3 == 0, wide(prev_c), wide(next_c))
        return result + jnp.where(end, corners, 0.0)

    for copy in load_phase:
        copy.wait()
    for which in range(2):
        phase[which, 2:10] = total([pops[which][i].astype(jnp.float32) for i in range(19, 26)])
        z1s[2 * which : 2 * which + 2] = jnp.where(low, phase[which, 8:10], phase[which, 2:4])
    for copy in load_cot:
        copy.wait()
    vertical_layers(adj_a, z1s, 4)
    pl.semaphore_wait(barrier, 13)
    first = [send(z1s, z1r, partner)]

    def edge_layer(values):
        return jnp.where(low, values[7], values[0])

    for way in SIDES[2:]:
        slot = SLOT[way] - 2
        source = 0 if way[1] < 0 else 126
        middle = jnp.where(
            lane3 < 8,
            roll(phase[1, 2:10], 6 - source, 2),
            roll(phase[0, 2:10], 8 - source, 2),
        )
        entries = pack_y(adj_a, -way[1], None)
        y1s[slot] = jnp.where(lane3 < 6, entries, middle)
        first.append(send(y1s.at[slot], y1r.at[slot, pl.ds(1, 8)], device(way)))
        rise, fall = slanted(-way[1], 2)
        beyond = jnp.where(low, adj_a[fall, 8], adj_a[rise, 1])
        edge = edge_layer(middle)
        for i in (rise, fall):
            k = ALONG_Y[-way[1]].index(i)
            edge = jnp.where(lane == k, roll(beyond, k - (0 if way[1] < 0 else 127), 1), edge)
        zy1s[slot] = edge
        first.append(send(zy1s.at[slot], zy1r.at[slot], across(way)))
    for way in CORNERS:
        slot = SLOT[way]
        r = edge_row(-way[0])
        c1s[slot, 0] = phase[1, 2:10, r, :]
        c1s[slot, 1] = phase[0, 2:10, r, :]
        c1s[slot, 2] = adj_a[DIAGONAL[(-way[0], -way[1])], 1:9, r, :]
        first.append(send(c1s.at[slot], c1r.at[slot], device(way)))
    for way in SIDES[:2]:
        slot = SLOT[way]
        r = edge_row(-way[0])
        rows_x(adj_a, -way[0], x1s, slot)
        for n, which in enumerate((1, 0)):
            x1s[slot, 6 + 2 * n] = phase[which, 2:10, r, :]
            x1s[slot, 7 + 2 * n] = phase[which, 2:10, r + (1 if r == 0 else -1), :]
            zx1s[slot, n : n + 1, :] = jnp.where(
                low, phase[which, 9, r : r + 1, :], phase[which, 2, r : r + 1, :]
            )
        rise, fall = slanted(-way[0], 1)
        zx1s[slot, 2:3, :] = jnp.where(
            low, adj_a[fall, 8, r : r + 1, :], adj_a[rise, 1, r : r + 1, :]
        )
        zx1s[slot, 3:, :] = jnp.zeros((5, 128), jnp.float32)
        first.append(send(x1s.at[slot], x1r.at[slot, pl.ds(0, 10)], device(way)))
        first.append(send(zx1s.at[slot], zx1r.at[slot], across(way)))
    for copy in load_flow:
        copy.wait()
    flow_moments(1)
    flow_moments(0)
    arrive(first)
    for which in range(2):
        got = z1r[2 * which : 2 * which + 2]
        phase[which, :2] = jnp.where(low, 0.0, got)
        phase[which, 10:] = jnp.where(low, got, 0.0)
    take_vertical(adj_a, z1r, 4)
    for way in SIDES:
        sign = -way[0] - way[1]
        if way[0]:
            slot = SLOT[way]
            rise, fall = slanted(sign, 1)
            entry = zx1r[slot, 2:3, :]
            x1r[slot, ALONG_X[sign].index(rise), 7:8, :] = entry
            x1r[slot, ALONG_X[sign].index(fall), 0:1, :] = entry
            for n in range(2):
                line = zx1r[slot, n : n + 1, :]
                x1r[slot, 10, 2 * n : 2 * n + 1, :] = jnp.where(low, 0.0, line)
                x1r[slot, 10, 2 * n + 1 : 2 * n + 2, :] = jnp.where(low, line, 0.0)
        else:
            slot = SLOT[way] - 2
            rise, fall = slanted(sign, 2)
            tile = zy1r[slot]
            y1r[slot, 0] = jnp.where(low, 0.0, tile)
            y1r[slot, 9] = jnp.where(low, tile, 0.0)
            y1r[slot, 8] = jnp.where(lane == ALONG_Y[sign].index(rise), tile, y1r[slot, 8])
            y1r[slot, 1] = jnp.where(lane == ALONG_Y[sign].index(fall), tile, y1r[slot, 1])
    sources = (adj_a, x1r, y1r, 1, c1r, 2)
    phase_gradients(1, 6, 0)
    gather_flow(1, *sources)
    collide_adjoint(1, sources, adj_b, 1, False)

    vertical_layers(adj_b, z2s, 0)
    vertical = send(z2s, z2r, partner)
    share = phase_share(1)
    center, group = send_share(
        share, zd2s, zd2r, zs2s, zs2r, xd2s, xd2r, yd2s, yd2r, cd2s, cd2r
    )
    vertical.wait_recv()
    take_vertical(adj_b, z2r, 0)
    second = []
    for way in SIDES[2:]:
        slot = SLOT[way] - 2
        y2s[slot] = pack_y(adj_b, -way[1], None)
        second.append(send(y2s.at[slot], y2r.at[slot], device(way)))
    for way in CORNERS:
        slot = SLOT[way]
        c2s[slot, 0] = adj_b[DIAGONAL[(-way[0], -way[1])], 1:9, edge_row(-way[0]), :]
        second.append(send(c2s.at[slot], c2r.at[slot], device(way)))
    for way in SIDES[:2]:
        slot = SLOT[way]
        rows_x(adj_b, -way[0], x2s, slot)
        second.append(send(x2s.at[slot], x2r.at[slot], device(way)))
    phase_gradients(0, 8, 2)
    phi[1:9] = collect_share(center, group, zd2r, zs2r, xd2r, yd2r, cd2r)
    third = []
    for way in SIDES:
        slot = SLOT[way]
        if way[0]:
            x3s[slot] = phi[1:9, edge_row(-way[0]), :]
            third.append(send(x3s.at[slot], x3r.at[slot], device(way)))
        else:
            third.append(send(phi.at[pl.ds(1, 8)], y3r.at[slot - 2], device(way)))
    z3s[...] = jnp.where(low, phi[8], phi[1])
    third.append(send(z3s, z3r, partner))
    arrive(second)
    sources = (adj_b, x2r, y2r, 0, c2r, 0)
    gather_flow(0, *sources)
    arrive(third)
    phi[0] = z3r[...]
    phi[9] = z3r[...]
    collide_adjoint(0, sources, out, 0, True)

    stores = [
        load(out.at[pl.ds(0, 10)], out_hbm.at[pl.ds(0, 10)], 6),
        load(out.at[pl.ds(10, 9)], out_hbm.at[pl.ds(10, 9)], 7),
    ]
    share = phase_share(0)
    center, group = send_share(
        share, zd4s, zd4r, zs4s, zs4r, xd4s, xd4r, yd4s, yd4r, cd4s, cd4r
    )
    last = collect_share(center, group, zd4r, zs4r, xd4r, yd4r, cd4r)
    for k in range(7):
        out[19 + k] = out[19 + k] + last
    stores.append(load(out.at[pl.ds(19, 7)], out_hbm.at[pl.ds(19, 7)], 8))
    for copy in stores:
        copy.wait()
    for copy in copies:
        copy.wait_send()


def local(populations0, populations1, cotangent):
    def vmem(*shape):
        return pltpu.VMEM(shape + (8, 128), jnp.float32)

    share = [
        vmem(2), vmem(2), vmem(2), vmem(4), vmem(2, 2), vmem(2, 2),
        vmem(8), vmem(2, 8), vmem(2), vmem(4),
    ]
    scratch = [
        vmem(26, 8),
        pltpu.VMEM(populations0.shape, populations0.dtype),
        pltpu.VMEM(populations1.shape, populations1.dtype),
        vmem(26, 10), vmem(26, 10), vmem(2, 12), vmem(2, 6, 8), vmem(6, 8), vmem(8),
        vmem(2, 3, 10), vmem(10), vmem(2, 4, 8), vmem(11, 8), vmem(19, 8),
        vmem(10), vmem(10), vmem(2, 10), vmem(2, 11), vmem(2, 8), vmem(2, 10), vmem(4, 3), vmem(4, 3),
        vmem(6), vmem(6), vmem(2, 6), vmem(2, 6), vmem(2, 8), vmem(2, 8), vmem(4, 1), vmem(4, 1),
        vmem(2), vmem(2), vmem(2), vmem(2),
        *share,
        vmem(), vmem(), vmem(2), vmem(2), vmem(2, 8),
        *share,
        pltpu.SemaphoreType.DMA((64,)),
        pltpu.SemaphoreType.DMA((64,)),
        pltpu.SemaphoreType.DMA((9,)),
    ]
    operands = [
        pltpu.with_memory_space_constraint(operand, pltpu.HBM)
        for operand in (populations0, populations1, cotangent)
    ]
    return pl.pallas_call(
        kernel,
        out_shape=jax.ShapeDtypeStruct(cotangent.shape, jnp.float32),
        in_specs=[pl.BlockSpec(memory_space=pltpu.HBM)] * 3,
        out_specs=pl.BlockSpec(memory_space=pl.ANY),
        scratch_shapes=scratch,
        compiler_params=pltpu.CompilerParams(
            collective_id=0, has_side_effects=True, vmem_limit_bytes=40 * 1024 * 1024
        ),
    )(*operands)


def solution(mesh):
    spec = P(None, "gz", "gx", "gy")
    return jax.shard_map(
        local, mesh=mesh, in_specs=(spec, spec, spec), out_specs=spec, check_vma=False
    )
```

```python
import jax
import jax.numpy as jnp
import numpy as np
from jax import lax
from jax.experimental import pallas as pl
from jax.experimental.pallas import tpu as pltpu
from jax.sharding import PartitionSpec as P

VELOCITY = [
    (0, 0, 0),
    (1, 0, 0),
    (-1, 0, 0),
    (0, 1, 0),
    (0, -1, 0),
    (0, 0, 1),
    (0, 0, -1),
    (1, 1, 0),
    (-1, -1, 0),
    (1, -1, 0),
    (-1, 1, 0),
    (1, 0, 1),
    (-1, 0, -1),
    (1, 0, -1),
    (-1, 0, 1),
    (0, 1, 1),
    (0, -1, -1),
    (0, 1, -1),
    (0, -1, 1),
]
OPPOSITE = [0, 2, 1, 4, 3, 6, 5, 8, 7, 10, 9, 12, 11, 14, 13, 16, 15, 18, 17]
VELOCITY = VELOCITY + VELOCITY[:7]
OPPOSITE = OPPOSITE + [19 + mirror for mirror in OPPOSITE[:7]]
WELL = 1.2
STIFFNESS = 0.6
SHARPEN = 0.3
PHASE_RATE = 1.4
MESH = pl.DeviceIdType.MESH
TOGETHER = 4

RISING = [i for i in range(26) if VELOCITY[i][0] == 1]
FALLING = [i for i in range(26) if VELOCITY[i][0] == -1]
ALONG_X = {sign: [i for i in range(26) if VELOCITY[i][1] == sign] for sign in (1, -1)}
ALONG_Y = {sign: [i for i in range(26) if VELOCITY[i][2] == sign] for sign in (1, -1)}
DIAGONAL = {VELOCITY[i][1:]: i for i in range(15, 19)}
SIDES = [(-1, 0), (1, 0), (0, -1), (0, 1)]
CORNERS = [(-1, -1), (-1, 1), (1, -1), (1, 1)]
SLOT = {way: i for i, way in enumerate(SIDES)}
SLOT.update({way: i for i, way in enumerate(CORNERS)})


def kernel(
    pop0_hbm, pop1_hbm, cot_hbm, out_hbm,
    out, pop0, pop1, adj_a, adj_b, phase, grads, sens, phibar, slope, phi, flow, moments, arrive_f, pulls,
    z1s, z1r, x1s, x1r, y1s, y1r, c1s, c1r,
    z2s, z2r, x2s, x2r, y2s, y2r, c2s, c2r,
    zx1s, zx1r, zy1s, zy1r,
    zd2s, zd2r, zs2s, zs2r, xd2s, xd2r, yd2s, yd2r, cd2s, cd2r,
    z3s, z3r, x3s, x3r, y3r,
    zd4s, zd4r, zs4s, zs4r, xd4s, xd4r, yd4s, yd4r, cd4s, cd4r,
    send_sem, recv_sem, load_sem,
):
    gx, gy, gz = lax.axis_index("gx"), lax.axis_index("gy"), lax.axis_index("gz")
    nx, ny = lax.axis_size("gx"), lax.axis_size("gy")
    low = gz == 0
    partner = (gx, gy, 1 - gz)
    pops = (pop0, pop1)

    def load(src, dst, index):
        copy = pltpu.make_async_copy(src, dst, load_sem.at[index])
        copy.start()
        return copy

    load_phase = [
        load(pop1_hbm.at[pl.ds(19, 7)], pop1.at[pl.ds(19, 7)], 0),
        load(pop0_hbm.at[pl.ds(19, 7)], pop0.at[pl.ds(19, 7)], 1),
    ]
    load_cot = [
        load(cot_hbm.at[pl.ds(0, 13)], adj_a.at[pl.ds(0, 13), pl.ds(1, 8)], 2),
        load(cot_hbm.at[pl.ds(13, 13)], adj_a.at[pl.ds(13, 13), pl.ds(1, 8)], 3),
    ]
    load_flow = [
        load(pop0_hbm.at[pl.ds(0, 19)], pop0.at[pl.ds(0, 19)], 4),
        load(pop1_hbm.at[pl.ds(0, 19)], pop1.at[pl.ds(0, 19)], 5),
    ]

    def device(way):
        return (lax.rem(gx + way[0] + nx, nx), lax.rem(gy + way[1] + ny, ny), gz)

    def across(way):
        return (*device(way)[:2], 1 - gz)

    barrier = pltpu.get_barrier_semaphore()
    others = [across(way) for way in SIDES]
    for target in [partner] + others + [device(way) for way in SIDES + CORNERS]:
        pl.semaphore_signal(barrier, inc=1, device_id=target, device_id_type=MESH)

    copies = []

    def send(src, dst, target):
        index = len(copies)
        copy = pltpu.make_async_remote_copy(
            src_ref=src,
            dst_ref=dst,
            send_sem=send_sem.at[index],
            recv_sem=recv_sem.at[index],
            device_id=target,
            device_id_type=MESH,
        )
        copy.start()
        copies.append(copy)
        return copy

    def arrive(group):
        for copy in group:
            copy.wait_recv()

    row = lax.broadcasted_iota(jnp.int32, (8, 128), 0)
    lane = lax.broadcasted_iota(jnp.int32, (8, 128), 1)

    def rows_of(count):
        return lax.broadcasted_iota(jnp.int32, (count, 8, 128), 1)

    def lanes_of(count):
        return lax.broadcasted_iota(jnp.int32, (count, 8, 128), 2)

    row3, lane3 = rows_of(8), lanes_of(8)

    def roll(values, shift, axis):
        shift = shift % values.shape[axis]
        return values if shift == 0 else pltpu.roll(values, shift, axis)

    def layers(values, before, after):
        shape = values.shape[1:]
        parts = [jnp.zeros((before, *shape), jnp.float32)] if before else []
        parts.append(values)
        if after:
            parts.append(jnp.zeros((after, *shape), jnp.float32))
        return jnp.concatenate(parts, 0)

    def wide(rows):
        return jnp.broadcast_to(rows[:, None, :], (rows.shape[0], 8, 128))

    def shift(inner, outer, step, axis):
        some = inner if inner is not None else outer
        size = some.shape[axis]
        edge = 0 if step == 1 else size - 1
        at_edge = lax.broadcasted_iota(jnp.int32, some.shape, axis) == edge
        a = 0.0 if inner is None else roll(inner, step, axis)
        b = 0.0 if outer is None else roll(outer, step, axis)
        return jnp.where(at_edge, b, a), jnp.where(at_edge, a, b)

    def difference(inner, outer, axis):
        up, down = shift(inner, outer, -1, axis), shift(inner, outer, 1, axis)
        return up[0] - down[0], up[1] - down[1]

    def both_sides(inner, outer, axis):
        up, down = shift(inner, outer, -1, axis), shift(inner, outer, 1, axis)
        return up[0] + down[0], up[1] + down[1]

    def vertical_layers(adj, ref, start):
        for k in range(6):
            ref[start + k] = jnp.where(low, adj[FALLING[k], 8], adj[RISING[k], 1])

    def take_vertical(adj, ref, start):
        for k in range(6):
            layer = ref[start + k]
            adj[RISING[k], 9] = layer
            adj[FALLING[k], 0] = layer

    def slanted(sign, d):
        rise = [i for i in RISING if VELOCITY[i][d] == sign][0]
        fall = [i for i in FALLING if VELOCITY[i][d] == sign][0]
        return rise, fall

    def edge_row(sign):
        return 0 if sign == 1 else 7

    def rows_x(adj, sign, ref, slot):
        for k, i in enumerate(ALONG_X[sign]):
            cz = VELOCITY[i][0]
            ref[slot, k] = adj[i, 1 + cz : 9 + cz, edge_row(sign), :]

    def pack_y(adj, sign, packed):
        source = 0 if sign == 1 else 127
        for k, i in enumerate(ALONG_Y[sign]):
            cz = VELOCITY[i][0]
            values = roll(adj[i, 1 + cz : 9 + cz], k - source, 2)
            packed = values if packed is None else jnp.where(lane3 == k, values, packed)
        return packed

    def well(value):
        return WELL * value * (value - 1.0) * (value - 0.5)

    def well_slope(value):
        return WELL * (3.0 * value * value - 3.0 * value + 0.5)

    def phase_gradients(which, tile, place):
        full = phase[which]
        ahead, behind = SLOT[(-1, 0)], SLOT[(1, 0)]

        def side(slot):
            near = wide(x1r[slot, tile])
            far = wide(x1r[slot, tile + 1])
            first = x1r[slot, 10, place : place + 1, :]
            last = x1r[slot, 10, place + 1 : place + 2, :]
            first = jnp.broadcast_to(first, (8, 128))[None]
            last = jnp.broadcast_to(last, (8, 128))[None]
            return first, near, far, last

        first_n, near_n, far_n, last_n = side(ahead)
        first_p, near_p, far_p, last_p = side(behind)
        x_mid = jnp.where(
            row3 < 4,
            jnp.where(row3 == 0, near_n, far_n),
            jnp.where(row3 == 7, near_p, far_p),
        )
        upper_half = row[None] < 4
        x_tile = jnp.concatenate(
            [jnp.where(upper_half, first_n, first_p), x_mid, jnp.where(upper_half, last_n, last_p)], 0
        )
        start = 6 + 2 * (1 - which)
        y_tile = jnp.where(
            lanes_of(10) < 64,
            roll(y1r[SLOT[(0, -1)] - 2], -start, 2),
            roll(y1r[SLOT[(0, 1)] - 2], 126 - start, 2),
        )
        t = 1 - which
        before_y, after_y = lane < 64, lane >= 64
        corner_n = jnp.where(before_y, c1r[SLOT[(-1, -1)], t], c1r[SLOT[(-1, 1)], t])
        corner_p = jnp.where(before_y, c1r[SLOT[(1, -1)], t], c1r[SLOT[(1, 1)], t])
        b_tile = jnp.where(row3 < 4, wide(corner_n), wide(corner_p))
        mid, y_mid = full[1:11], y_tile[1:9]
        slope[which, 0] = well_slope(mid)
        slope[which, 1] = well_slope(x_tile)
        slope[which, 2] = well_slope(y_tile)

        x_up, x_down = shift(mid, x_tile, -1, 1), shift(mid, x_tile, 1, 1)
        y_up, y_down = shift(mid, y_tile, -1, 2), shift(mid, y_tile, 1, 2)
        grads[which, 0] = 0.5 * (full[3:11] - full[1:9])
        grads[which, 1] = 0.5 * (x_up[0] - x_down[0])[1:9]
        grads[which, 2] = 0.5 * (y_up[0] - y_down[0])[1:9]
        lap = x_up[0] + x_down[0] + y_up[0] + y_down[0] + full[:10] + full[2:] - 6.0 * mid
        pot = well(mid) - STIFFNESS * lap
        pot = jnp.concatenate(
            [jnp.where(low, 0.0, pot[:1]), pot[1:9], jnp.where(low, pot[9:], 0.0)], 0
        )
        lap = (x_up[1] + x_down[1])[1:9] + both_sides(x_mid, b_tile, 2)[0]
        lap = lap + x_tile[:8] + x_tile[2:] - 6.0 * x_mid
        pot_x = well(x_mid) - STIFFNESS * lap
        lap = (y_up[1] + y_down[1])[1:9] + both_sides(y_mid, b_tile, 1)[0]
        lap = lap + y_tile[:8] + y_tile[2:] - 6.0 * y_mid
        pot_y = well(y_mid) - STIFFNESS * lap
        grads[which, 3] = 0.5 * (pot[2:] - pot[:8])
        grads[which, 4] = 0.5 * difference(pot[1:9], pot_x, 1)[0]
        grads[which, 5] = 0.5 * difference(pot[1:9], pot_y, 2)[0]

    def total(values):
        values = list(values)
        while len(values) > 1:
            values = [
                values[j] + values[j + 1] if j + 1 < len(values) else values[j]
                for j in range(0, len(values), 2)
            ]
        return values[0]

    def signed(values, weight):
        plus = [values[i] for i in range(len(values)) if weight(i) == 1]
        minus = [values[i] for i in range(len(values)) if weight(i) == -1]
        return total(plus) - total(minus)

    def part(d):
        return lambda i: VELOCITY[i][d]

    def pair(d, e):
        return lambda i: VELOCITY[i][d] * VELOCITY[i][e]

    def dot(u, v):
        return u[0] * v[0] + u[1] * v[1] + u[2] * v[2]

    def each_layer(layer):
        def several(step, carry):
            for n in range(TOGETHER):
                layer(step * TOGETHER + n, carry)
            return carry

        lax.fori_loop(0, 8 // TOGETHER, several, 0)

    def flow_moments(which):
        def layer(z, carry):
            f = [pops[which][i, z].astype(jnp.float32) for i in range(19)]
            flow[which, 0, z] = total(f)
            for d in range(3):
                flow[which, 1 + d, z] = signed(f, part(d))
            return carry

        each_layer(layer)

    def bounce(z, i, own, bounced):
        if VELOCITY[i][0] == 1:
            return jnp.where(jnp.logical_and(z == 7, jnp.logical_not(low)), bounced, own)
        if VELOCITY[i][0] == -1:
            return jnp.where(jnp.logical_and(z == 0, low), bounced, own)
        return own

    def arrived(z, i, adj, xr, yr, ystart, cr, tile):
        cz, cx, cy = VELOCITY[i]
        own = adj[i, z + (1 + cz)]
        erow = 7 if cx == 1 else 0
        elane = 127 if cy == 1 else 0
        moved = own
        if cx:
            k = ALONG_X[cx].index(i)
            got = jnp.broadcast_to(xr[SLOT[(-cx, 0)], k, pl.ds(z, 1), :], (8, 128))
            moved = jnp.where(row == erow, got, roll(own, -cx, 0))
        if cy:
            k = ALONG_Y[cy].index(i)
            got = roll(yr[SLOT[(0, -cy)] - 2, ystart + z], elane - k, 1)
            if cx:
                corner = cr[SLOT[(-cx, -cy)], tile, pl.ds(z, 1), :]
                corner = roll(jnp.broadcast_to(corner, (8, 128)), -cy, 1)
                got = jnp.where(row == erow, corner, roll(got, -cx, 0))
            moved = jnp.where(lane == elane, got, roll(moved, -cy, 1))
        return bounce(z, i, moved, adj[OPPOSITE[i], z + 1])

    PAIRS = [(0, 0), (1, 1), (2, 2), (1, 0), (2, 0), (2, 1)]

    def gather_flow(which, *sources):
        def layer(z, carry):
            a = [arrived(z, i, *sources) for i in range(19)]
            for i in range(19):
                arrive_f[i, z] = a[i]
            wa = [a[0] * (1.0 / 3.0)]
            wa += [a[i] * (1.0 / 18.0) for i in range(1, 7)]
            wa += [a[i] * (1.0 / 36.0) for i in range(7, 19)]
            moments[0, z] = total(wa)
            for d in range(3):
                moments[1 + d, z] = signed(wa, part(d))
            for n, (d, e) in enumerate(PAIRS):
                if d == e:
                    moments[4 + n, z] = total([wa[i] for i in range(19) if VELOCITY[i][d]])
                else:
                    moments[4 + n, z] = signed(wa, pair(d, e))
            moments[10, z] = total([a[i] * pops[which][i, z].astype(jnp.float32) for i in range(19)])
            return carry

        each_layer(layer)

    def collide_adjoint(which, sources, result, offset, with_phi):
        def layer(z, carry):
            def arrived_phi(i):
                cz, cx, cy = VELOCITY[i]
                own = phi[z + (1 + cz)]
                if cx:
                    erow = 7 if cx == 1 else 0
                    got = jnp.broadcast_to(x3r[SLOT[(-cx, 0)], pl.ds(z, 1), :], (8, 128))
                    own = jnp.where(row == erow, got, roll(own, -cx, 0))
                if cy:
                    elane = 127 if cy == 1 else 0
                    got = roll(y3r[SLOT[(0, -cy)] - 2, z], -cy, 1)
                    own = jnp.where(lane == elane, got, roll(own, -cy, 1))
                return bounce(z, i, own, phi[z + 1])

            g = [arrived(z, i, *sources) for i in range(19, 26)]
            if with_phi:
                g = [g[k] + arrived_phi(19 + k) for k in range(7)]
            frac = phase[which, z + 2]
            pressure = flow[which, 0, z]
            momentum = [flow[which, 1 + d, z] for d in range(3)]
            a0 = moments[0, z]
            a1 = [moments[1 + d, z] for d in range(3)]
            a2 = {}
            for n, (d, e) in enumerate(PAIRS):
                a2[d, e] = a2[e, d] = moments[4 + n, z]
            af = moments[10, z]
            b0 = 0.25 * g[0] + 0.125 * total(g[1:])
            b1 = [0.125 * (g[1 + 2 * d] - g[2 + 2 * d]) for d in range(3)]
            density = 0.2 + 0.8 * frac
            rate = 1.1 + 0.5 * frac
            half = 1.0 - 0.5 * rate
            pg = [grads[which, d, z] for d in range(3)]
            mg = [grads[which, 3 + d, z] for d in range(3)]
            force = [-frac * m for m in mg]
            inverse = 1.0 / density
            u = [(momentum[d] + 0.5 * force[d]) * inverse for d in range(3)]
            a2u = [dot([a2[d, e] for e in range(3)], u) for d in range(3)]
            a2f = [dot([a2[d, e] for e in range(3)], force) for d in range(3)]
            speed = dot(u, u)
            quad = 3.0 * dot(u, a1) + 4.5 * dot(u, a2u) - 1.5 * speed * a0
            slant = [3.0 * a1[d] - 3.0 * a0 * u[d] + 9.0 * a2u[d] for d in range(3)]
            rate_density = rate * density
            phase_pull = (4.0 * PHASE_RATE) * frac
            ubar = [
                rate_density * slant[d]
                + half * (9.0 * a2f[d] - 3.0 * a0 * force[d])
                + phase_pull * b1[d]
                for d in range(3)
            ]
            jbar = [ubar[d] * inverse for d in range(3)]
            fbar = [half * slant[d] + 0.5 * jbar[d] for d in range(3)]
            density_bar = rate * quad - dot(jbar, u)
            rate_bar = pressure * a0 + density * quad - af - 0.5 * dot(force, slant)
            imag = lax.rsqrt(dot(pg, pg) + 0.0625)
            normal = [p * imag for p in pg]
            nb1 = dot(normal, b1)
            frac_bar = (
                0.5 * rate_bar
                + 0.8 * density_bar
                - dot(mg, fbar)
                + PHASE_RATE * (b0 + 4.0 * dot(u, b1))
                + (PHASE_RATE * 4.0 * SHARPEN) * (1.0 - 2.0 * frac) * nb1
            )
            pull = (PHASE_RATE * 4.0 * SHARPEN) * frac * (1.0 - frac) * imag
            for d in range(3):
                sens[d, z] = pull * (b1[d] - normal[d] * nb1)
                sens[3 + d, z] = -frac * fbar[d]
            phibar[z] = frac_bar
            for d in range(3):
                pulls[d, z] = jbar[d]
            pulls[3, z] = rate * a0
            for k in range(7):
                result[19 + k, z + offset] = (1.0 - PHASE_RATE) * g[k]
            return carry

        each_layer(layer)

    def flow_result(which, result, offset):
        def layer(z, carry):
            keep = -0.1 - 0.5 * phase[which, z + 2]
            jbar = [pulls[d, z] for d in range(3)]
            pbar = pulls[3, z]
            for i in range(19):
                value = keep * arrive_f[i, z] + pbar
                for d in range(3):
                    if VELOCITY[i][d] == 1:
                        value = value + jbar[d]
                    elif VELOCITY[i][d] == -1:
                        value = value - jbar[d]
                result[i, z + offset] = value
            return carry

        each_layer(layer)

    def phase_share(which):
        def spread(first):
            vz = sens[first]
            in_x, out_x = difference(sens[first + 1], None, 1)
            in_y, out_y = difference(sens[first + 2], None, 2)
            inner = layers(-0.5 * (in_x + in_y), 1, 1)
            inner = inner + 0.5 * (layers(vz, 2, 0) - layers(vz, 0, 2))
            return inner, layers(-0.5 * out_x, 1, 1), layers(-0.5 * out_y, 1, 1)

        mu, mu_x, mu_y = spread(3)
        mu = jnp.concatenate(
            [jnp.where(low, 0.0, mu[:1]), mu[1:9], jnp.where(low, mu[9:], 0.0)], 0
        )
        own, own_x, own_y = spread(0)
        in_x, out_x = both_sides(mu, mu_x, 1)
        in_y, out_y = both_sides(mu, mu_y, 2)
        over_x, corner_x = both_sides(mu_x[1:9], None, 2)
        over_y, corner_y = both_sides(mu_y[1:9], None, 1)
        inner = slope[which, 0] * mu - STIFFNESS * (in_x + in_y - 6.0 * mu) + own
        inner = inner + layers(phibar[...], 1, 1)
        inner = layers(inner, 1, 1) - STIFFNESS * (layers(mu, 2, 0) + layers(mu, 0, 2))

        def beside(scale, values, out_share, over, extra):
            vertical = layers(values[1:], 0, 1) + layers(values[:9], 1, 0)
            lap = out_share + layers(over, 1, 1) + vertical - 6.0 * values
            return scale * values - STIFFNESS * lap + extra

        side_x = beside(slope[which, 1], mu_x, out_x, over_x, own_x)
        side_y = beside(slope[which, 2], mu_y, out_y, over_y, own_y)
        return inner, side_x, side_y, -STIFFNESS * (corner_x + corner_y)

    def send_share(share, zs, zr, es, er, xs, xr, ys, yr, cs, cr):
        inner, side_x, side_y, corner = share
        group = []
        ys[...] = side_y[1:9]
        for way in SIDES[2:]:
            slot = SLOT[way] - 2
            group.append(send(ys, yr.at[slot], device(way)))
        xs[0, 0], xs[0, 1] = side_x[1:9, 7, :], side_x[1:9, 6, :]
        xs[1, 0], xs[1, 1] = side_x[1:9, 0, :], side_x[1:9, 1, :]
        cs[0], cs[1] = corner[:, 7, :], corner[:, 0, :]
        for way in CORNERS:
            group.append(send(cs.at[0 if way[0] < 0 else 1], cr.at[SLOT[way]], device(way)))
        for way in SIDES[:2]:
            slot = SLOT[way]
            group.append(send(xs.at[slot], xr.at[slot], device(way)))
        es[0] = jnp.where(low, side_x[9], side_x[0])
        es[1] = jnp.where(low, side_y[9], side_y[0])
        for way in SIDES:
            slot = SLOT[way]
            group.append(send(es.at[0 if way[0] else 1], er.at[slot], across(way)))
        zs[...] = jnp.where(low, inner[10:], inner[:2])
        group.append(send(zs, zr, partner))
        return inner[2:10], group

    def collect_share(center, group, zr, er, xr, yr, cr):
        arrive(group)
        prev_x, next_x, prev_y, next_y = (er[SLOT[way]] for way in ((1, 0), (-1, 0), (0, 1), (0, -1)))
        beyond = jnp.where(row == 0, prev_x, jnp.where(row == 7, next_x, 0.0))
        beyond = beyond + jnp.where(lane == 0, prev_y, jnp.where(lane == 127, next_y, 0.0))
        extra = zr[...]
        to_low = jnp.concatenate([extra[:1], extra[1:] + beyond[None]], 0)
        to_high = jnp.concatenate([extra[:1] + beyond[None], extra[1:]], 0)
        lower = center[:2] + jnp.where(low, 0.0, to_high)
        upper = center[6:] + jnp.where(low, to_low, 0.0)
        center = jnp.concatenate([lower, center[2:6], upper], 0)
        prev, after = SLOT[(1, 0)], SLOT[(-1, 0)]
        near = jnp.where(row3 < 4, wide(xr[prev, 0]), wide(xr[after, 0]))
        far = jnp.where(row3 < 4, wide(xr[prev, 1]), wide(xr[after, 1]))
        end = jnp.logical_or(row3 == 0, row3 == 7)
        next_end = jnp.logical_or(row3 == 1, row3 == 6)
        result = center + jnp.where(end, near, jnp.where(next_end, far, 0.0))
        from_y = jnp.where(lane3 < 64, yr[SLOT[(0, 1)] - 2], yr[SLOT[(0, -1)] - 2])
        result = result + jnp.where(jnp.logical_or(lane3 < 2, lane3 >= 126), from_y, 0.0)
        before = lane < 64
        ends = jnp.logical_or(lane == 0, lane == 127)
        prev_c = jnp.where(ends, jnp.where(before, cr[SLOT[(1, 1)]], cr[SLOT[(1, -1)]]), 0.0)
        next_c = jnp.where(ends, jnp.where(before, cr[SLOT[(-1, 1)]], cr[SLOT[(-1, -1)]]), 0.0)
        corners = jnp.where(row3 == 0, wide(prev_c), wide(next_c))
        return result + jnp.where(end, corners, 0.0)

    for copy in load_phase:
        copy.wait()
    for which in range(2):
        phase[which, 2:10] = total([pops[which][i].astype(jnp.float32) for i in range(19, 26)])
        z1s[2 * which : 2 * which + 2] = jnp.where(low, phase[which, 8:10], phase[which, 2:4])
    for copy in load_cot:
        copy.wait()
    vertical_layers(adj_a, z1s, 4)
    pl.semaphore_wait(barrier, 13)
    first = [send(z1s, z1r, partner)]

    def edge_layer(values):
        return jnp.where(low, values[7], values[0])

    for way in SIDES[2:]:
        slot = SLOT[way] - 2
        source = 0 if way[1] < 0 else 126
        middle = jnp.where(
            lane3 < 8,
            roll(phase[1, 2:10], 6 - source, 2),
            roll(phase[0, 2:10], 8 - source, 2),
        )
        entries = pack_y(adj_a, -way[1], None)
        y1s[slot] = jnp.where(lane3 < 6, entries, middle)
        first.append(send(y1s.at[slot], y1r.at[slot, pl.ds(1, 8)], device(way)))
        rise, fall = slanted(-way[1], 2)
        beyond = jnp.where(low, adj_a[fall, 8], adj_a[rise, 1])
        edge = edge_layer(middle)
        for i in (rise, fall):
            k = ALONG_Y[-way[1]].index(i)
            edge = jnp.where(lane == k, roll(beyond, k - (0 if way[1] < 0 else 127), 1), edge)
        zy1s[slot] = edge
        first.append(send(zy1s.at[slot], zy1r.at[slot], across(way)))
    for way in CORNERS:
        slot = SLOT[way]
        r = edge_row(-way[0])
        c1s[slot, 0] = phase[1, 2:10, r, :]
        c1s[slot, 1] = phase[0, 2:10, r, :]
        c1s[slot, 2] = adj_a[DIAGONAL[(-way[0], -way[1])], 1:9, r, :]
        first.append(send(c1s.at[slot], c1r.at[slot], device(way)))
    for way in SIDES[:2]:
        slot = SLOT[way]
        r = edge_row(-way[0])
        rows_x(adj_a, -way[0], x1s, slot)
        for n, which in enumerate((1, 0)):
            x1s[slot, 6 + 2 * n] = phase[which, 2:10, r, :]
            x1s[slot, 7 + 2 * n] = phase[which, 2:10, r + (1 if r == 0 else -1), :]
            zx1s[slot, n : n + 1, :] = jnp.where(
                low, phase[which, 9, r : r + 1, :], phase[which, 2, r : r + 1, :]
            )
        rise, fall = slanted(-way[0], 1)
        zx1s[slot, 2:3, :] = jnp.where(
            low, adj_a[fall, 8, r : r + 1, :], adj_a[rise, 1, r : r + 1, :]
        )
        zx1s[slot, 3:, :] = jnp.zeros((5, 128), jnp.float32)
        first.append(send(x1s.at[slot], x1r.at[slot, pl.ds(0, 10)], device(way)))
        first.append(send(zx1s.at[slot], zx1r.at[slot], across(way)))
    for copy in load_flow:
        copy.wait()
    flow_moments(1)
    flow_moments(0)
    arrive(first)
    for which in range(2):
        got = z1r[2 * which : 2 * which + 2]
        phase[which, :2] = jnp.where(low, 0.0, got)
        phase[which, 10:] = jnp.where(low, got, 0.0)
    take_vertical(adj_a, z1r, 4)
    for way in SIDES:
        sign = -way[0] - way[1]
        if way[0]:
            slot = SLOT[way]
            rise, fall = slanted(sign, 1)
            entry = zx1r[slot, 2:3, :]
            x1r[slot, ALONG_X[sign].index(rise), 7:8, :] = entry
            x1r[slot, ALONG_X[sign].index(fall), 0:1, :] = entry
            for n in range(2):
                line = zx1r[slot, n : n + 1, :]
                x1r[slot, 10, 2 * n : 2 * n + 1, :] = jnp.where(low, 0.0, line)
                x1r[slot, 10, 2 * n + 1 : 2 * n + 2, :] = jnp.where(low, line, 0.0)
        else:
            slot = SLOT[way] - 2
            rise, fall = slanted(sign, 2)
            tile = zy1r[slot]
            y1r[slot, 0] = jnp.where(low, 0.0, tile)
            y1r[slot, 9] = jnp.where(low, tile, 0.0)
            y1r[slot, 8] = jnp.where(lane == ALONG_Y[sign].index(rise), tile, y1r[slot, 8])
            y1r[slot, 1] = jnp.where(lane == ALONG_Y[sign].index(fall), tile, y1r[slot, 1])
    sources = (adj_a, x1r, y1r, 1, c1r, 2)
    phase_gradients(1, 6, 0)
    gather_flow(1, *sources)
    collide_adjoint(1, sources, adj_b, 1, False)

    share = phase_share(1)
    center, group = send_share(
        share, zd2s, zd2r, zs2s, zs2r, xd2s, xd2r, yd2s, yd2r, cd2s, cd2r
    )
    flow_result(1, adj_b, 1)
    vertical_layers(adj_b, z2s, 0)
    vertical = send(z2s, z2r, partner)
    phase_gradients(0, 8, 2)
    vertical.wait_recv()
    take_vertical(adj_b, z2r, 0)
    second = []
    for way in SIDES[2:]:
        slot = SLOT[way] - 2
        y2s[slot] = pack_y(adj_b, -way[1], None)
        second.append(send(y2s.at[slot], y2r.at[slot], device(way)))
    for way in CORNERS:
        slot = SLOT[way]
        c2s[slot, 0] = adj_b[DIAGONAL[(-way[0], -way[1])], 1:9, edge_row(-way[0]), :]
        second.append(send(c2s.at[slot], c2r.at[slot], device(way)))
    for way in SIDES[:2]:
        slot = SLOT[way]
        rows_x(adj_b, -way[0], x2s, slot)
        second.append(send(x2s.at[slot], x2r.at[slot], device(way)))
    phi[1:9] = collect_share(center, group, zd2r, zs2r, xd2r, yd2r, cd2r)
    third = []
    for way in SIDES:
        slot = SLOT[way]
        if way[0]:
            x3s[slot] = phi[1:9, edge_row(-way[0]), :]
            third.append(send(x3s.at[slot], x3r.at[slot], device(way)))
        else:
            third.append(send(phi.at[pl.ds(1, 8)], y3r.at[slot - 2], device(way)))
    z3s[...] = jnp.where(low, phi[8], phi[1])
    third.append(send(z3s, z3r, partner))
    arrive(second)
    sources = (adj_b, x2r, y2r, 0, c2r, 0)
    gather_flow(0, *sources)
    arrive(third)
    phi[0] = z3r[...]
    phi[9] = z3r[...]
    collide_adjoint(0, sources, out, 0, True)

    share = phase_share(0)
    center, group = send_share(
        share, zd4s, zd4r, zs4s, zs4r, xd4s, xd4r, yd4s, yd4r, cd4s, cd4r
    )
    flow_result(0, out, 0)
    stores = [
        load(out.at[pl.ds(0, 10)], out_hbm.at[pl.ds(0, 10)], 6),
        load(out.at[pl.ds(10, 9)], out_hbm.at[pl.ds(10, 9)], 7),
    ]
    last = collect_share(center, group, zd4r, zs4r, xd4r, yd4r, cd4r)
    for k in range(7):
        out[19 + k] = out[19 + k] + last
    stores.append(load(out.at[pl.ds(19, 7)], out_hbm.at[pl.ds(19, 7)], 8))
    for copy in stores:
        copy.wait()
    for copy in copies:
        copy.wait_send()


def local(populations0, populations1, cotangent):
    def vmem(*shape):
        return pltpu.VMEM(shape + (8, 128), jnp.float32)

    share = [
        vmem(2), vmem(2), vmem(2), vmem(4), vmem(2, 2), vmem(2, 2),
        vmem(8), vmem(2, 8), vmem(2), vmem(4),
    ]
    scratch = [
        vmem(26, 8),
        pltpu.VMEM(populations0.shape, populations0.dtype),
        pltpu.VMEM(populations1.shape, populations1.dtype),
        vmem(26, 10), vmem(26, 10), vmem(2, 12), vmem(2, 6, 8), vmem(6, 8), vmem(8),
        vmem(2, 3, 10), vmem(10), vmem(2, 4, 8), vmem(11, 8), vmem(19, 8), vmem(4, 8),
        vmem(10), vmem(10), vmem(2, 10), vmem(2, 11), vmem(2, 8), vmem(2, 10), vmem(4, 3), vmem(4, 3),
        vmem(6), vmem(6), vmem(2, 6), vmem(2, 6), vmem(2, 8), vmem(2, 8), vmem(4, 1), vmem(4, 1),
        vmem(2), vmem(2), vmem(2), vmem(2),
        *share,
        vmem(), vmem(), vmem(2), vmem(2), vmem(2, 8),
        *share,
        pltpu.SemaphoreType.DMA((64,)),
        pltpu.SemaphoreType.DMA((64,)),
        pltpu.SemaphoreType.DMA((9,)),
    ]
    operands = [
        pltpu.with_memory_space_constraint(operand, pltpu.HBM)
        for operand in (populations0, populations1, cotangent)
    ]
    return pl.pallas_call(
        kernel,
        out_shape=jax.ShapeDtypeStruct(cotangent.shape, jnp.float32),
        in_specs=[pl.BlockSpec(memory_space=pltpu.HBM)] * 3,
        out_specs=pl.BlockSpec(memory_space=pl.ANY),
        scratch_shapes=scratch,
        compiler_params=pltpu.CompilerParams(
            collective_id=0, has_side_effects=True, vmem_limit_bytes=40 * 1024 * 1024
        ),
    )(*operands)


def solution(mesh):
    spec = P(None, "gz", "gx", "gy")
    return jax.shard_map(
        local, mesh=mesh, in_specs=(spec, spec, spec), out_specs=spec, check_vma=False
    )
```
